256 devices in a mesh: sample: 32 (over z, y), head: 8 (over x, core).
Axes of the slice: x: 4, y: 4, z: 8, core: 2. Of those that a mesh axis runs over, the one named last changes fastest.
Arguments:
- child_stream: bfloat16 [32768, 1024], P('sample'), may hold values from -6 to 6
- cache_keys: bfloat16 [32768, 8, 1024], P('sample', None, 'head'), may hold values from -102 to 102
- cache_values: bfloat16 [32768, 8, 1024], P('sample', None, 'head'), may hold values from -6 to 6
- child_counts: int32 [32768], P('sample'), may hold values from 0 to 4, as said below
- child_slots: int32 [32768, 4], P('sample'), may hold values from -1 to 32767, as said below
- w_qkv: bfloat16 [3, 1024, 1024], P(None, None, 'head'), may hold values from -0.1875 to 0.1875
- w_out: bfloat16 [1024, 1024], P('head'), may hold values from -0.1875 to 0.1875
- w_up: bfloat16 [1024, 4096], P(None, 'head'), may hold values from -0.1875 to 0.1875
- w_down: bfloat16 [4096, 1024], P('head'), may hold values from -0.09375 to 0.09375
Outputs:
- layer_out: bfloat16 [32768, 1024], P('sample', 'head')
- new_kv: bfloat16 [32768, 2, 1024], P('sample', None, 'head')
The draws below stay inside these ranges and needn't reach their ends.
Inputs may be any that keep to these rules, and one draw needn't show every extreme that they name: `child_counts`: the counts of the 1024 parents of one index of sample sum to 1024. `child_slots`: entry k of parent r names the slot of its k-th child for k < child_counts[r] and is -1 otherwise; every slot is named exactly once; slot j belongs to index j // 1024 of sample; the children that the parents of one index send to the slots of one index number 48 or 16, each for half of the indices in every row and every column of such pairs.
All inputs are finite; a program needn't handle non-finite values.
Results may differ from the reference program's by a relative error of at most 0.02.
Values may be sent and summed in bfloat16 or wider, within the bound.
No kernel may reach another device: no remote copies, remote signals or barrier semaphores. Data moves between devices by JAX's collectives and lax.ppermute only.
A program may use at most 128 MiB of HBM per device.

```python
import jax
import jax.numpy as jnp
from jax import lax

D = 1024
H = 16
HD = 64
FF = 4096
P_SIZE = 8
R_DEV = 1024
ROWS = 32768
N_SAMPLE = 32
N_HEAD = 8


def child_plan(key):
    peer_count = N_SAMPLE
    row_count = R_DEV
    high = 3 * row_count // (2 * peer_count)
    lower = row_count // (2 * peer_count)
    subkeys = jax.random.split(key, 6)
    levels = jnp.where(jax.random.permutation(subkeys[0], peer_count) < peer_count // 2, high, lower).astype(jnp.int32)
    across = jax.random.permutation(subkeys[1], peer_count)
    downward = jax.random.permutation(subkeys[2], peer_count)
    quota = levels[(across[:, None] + downward[None, :]) % peer_count]
    before = jnp.cumsum(quota, axis=0) - quota
    offset = jax.random.randint(subkeys[3], (), 0, 3)
    orders = jax.vmap(lambda subkey: jax.random.permutation(subkey, row_count))(jax.random.split(subkeys[4], peer_count))

    def one_source(source):
        source_key = jax.random.fold_in(subkeys[5], source)
        first_key, second_key = jax.random.split(source_key)
        kind = (source + offset) % 3
        ranks = jnp.arange(row_count, dtype=jnp.int32)
        pattern = jnp.where(kind == 0, 1, jnp.where(kind == 1, jnp.where(ranks < row_count // 2, 2, 0), jnp.where(ranks < row_count // 4, 4, 0))).astype(jnp.int32)
        counts = pattern[jax.random.permutation(first_key, row_count)]
        is_live = (jnp.arange(4, dtype=jnp.int32)[None, :] < counts[:, None]).reshape(-1)
        order = jnp.cumsum(is_live.astype(jnp.int32)) - 1
        bounds = jnp.cumsum(quota[source])
        sequence = jnp.sum((ranks[:, None] >= bounds[None, :]).astype(jnp.int32), axis=1)
        owners = sequence[jax.random.permutation(second_key, row_count)]
        onehot = (owners[:, None] == jnp.arange(peer_count, dtype=jnp.int32)[None, :]).astype(jnp.int32)
        ranking = jnp.sum(jnp.cumsum(onehot, axis=0) * onehot, axis=1) - 1
        position = before[source, owners] + ranking
        final = owners * row_count + orders[owners, position]
        slots = jnp.where(is_live, final[jnp.clip(order, 0, row_count - 1)], -1).reshape(row_count, 4)
        return (counts, slots.astype(jnp.int32))
    counts, slots = jax.vmap(one_source)(jnp.arange(peer_count, dtype=jnp.int32))
    return (counts.reshape(-1), slots.reshape(-1, 4))


def draw_child_counts(key, part):
    counts, slots = child_plan(key)
    return counts


def draw_child_slots(key, part):
    counts, slots = child_plan(key)
    return slots


def draw_cache_keys(key, part):
    key = jax.random.fold_in(key, 5)
    row_total = R_DEV * N_SAMPLE
    shape = (row_total, P_SIZE, H * HD)
    subkeys = jax.random.split(key, 1)
    result = jnp.clip(jax.random.normal(subkeys[0], shape, jnp.float32), -6.0, 6.0)
    return result.astype(jnp.bfloat16)


def block_levels(stream_key, extent, cuts, least, high):
    def one(dim, parts):
        heights = jax.random.uniform(jax.random.fold_in(jax.random.fold_in(stream_key, 6), dim), (parts,), jnp.float32, least / len(cuts), high / len(cuts))
        return jnp.repeat(jnp.exp(heights), extent[dim] // parts).reshape((-1,) + (1,) * (len(extent) - dim - 1))

    gain = one(*cuts[0])
    for cut in cuts[1:]:
        gain = gain * one(*cut)
    return gain


def normal_values(own_key, extent, scale, bound, cuts=(), kind=jnp.bfloat16):
    array = scale * jax.random.normal(own_key, extent, jnp.float32)
    if cuts:
        array = array * block_levels(own_key, extent, cuts, -0.22, 0.18)
    return jnp.clip(array, -bound, bound).astype(kind)


def setup_inputs(seed: int = 0) -> dict:
    keys = jax.random.split(jax.random.key(seed), 10)
    child_stream = normal_values(keys[0], (ROWS, D), 1.0, 6.0, ((0, 32),))
    cache_keys = draw_cache_keys(jax.random.fold_in(keys[9], 71), 0)
    cache_values = normal_values(keys[2], (ROWS, P_SIZE, H * HD), 1.0, 6.0, ((0, 32), (2, 8)))
    child_counts = draw_child_counts(jax.random.fold_in(keys[9], 71), 0)
    child_slots = draw_child_slots(jax.random.fold_in(keys[9], 71), 0)
    w_qkv = normal_values(keys[5], (3, D, H * HD), D ** -0.5, 0.1875, ((2, 8),))
    w_out = normal_values(keys[6], (H * HD, D), (H * HD) ** -0.5, 0.1875, ((0, 8),))
    w_up = normal_values(keys[7], (D, FF), D ** -0.5, 0.1875, ((1, 8),))
    w_down = normal_values(keys[8], (FF, D), FF ** -0.5, 0.09375, ((0, 8),))
    return {"child_stream": child_stream, "cache_keys": cache_keys, "cache_values": cache_values, "child_counts": child_counts, "child_slots": child_slots, "w_qkv": w_qkv, "w_out": w_out, "w_up": w_up, "w_down": w_down}


def rms_rows(stream):
    return stream * lax.rsqrt(lax.optimization_barrier(jnp.mean(stream * stream, axis=-1, keepdims=True)) + 1e-05)

def attend_rows(queries, own_keys, own_values, key_rows, value_rows, head_size):
    item_count = queries.shape[0]
    head_count = queries.shape[1] // head_size
    token_positions = key_rows.shape[1]
    score_scale = 1.0 / head_size ** 0.5
    per_head_queries = queries.reshape(item_count, head_count, head_size).astype(jnp.float32)
    per_head_keys = key_rows.reshape(item_count, token_positions, head_count, head_size).astype(jnp.float32)
    per_head_values = value_rows.reshape(item_count, token_positions, head_count, head_size).astype(jnp.float32)
    current_keys = own_keys.reshape(item_count, head_count, head_size).astype(jnp.float32)
    current_values = own_values.reshape(item_count, head_count, head_size).astype(jnp.float32)
    stored_prefix_entries = jnp.einsum('okg,otkg->okt', per_head_queries, per_head_keys) * score_scale
    self_entry = jnp.einsum('ezl,ezl->ez', per_head_queries, current_keys) * score_scale
    scores = jnp.concatenate([stored_prefix_entries, self_entry[:, :, None]], axis=-1)
    highest = lax.optimization_barrier(jnp.max(scores, axis=-1, keepdims=True))
    expo = jnp.exp(scores - highest)
    attention_weight = (expo / lax.optimization_barrier(jnp.sum(expo, axis=-1, keepdims=True))).astype(jnp.bfloat16).astype(jnp.float32)
    attention_blend = jnp.einsum('fet,ftes->fes', attention_weight[:, :, :token_positions], per_head_values)
    attention_blend = attention_blend + attention_weight[:, :, token_positions][:, :, None] * current_values
    return attention_blend.reshape(item_count, head_count * head_size).astype(jnp.bfloat16)

def grouped_product(left, right, groups):
    row_count = left.shape[0]
    inner = left.shape[1] // groups
    terms = jnp.einsum('rgc,gcd->rgd', left.reshape(row_count, groups, inner).astype(jnp.float32), right.reshape(groups, inner, right.shape[1]).astype(jnp.float32))
    return lax.optimization_barrier(jnp.sum(terms.astype(jnp.bfloat16).astype(jnp.float32), axis=1))

def reference(child_stream, cache_keys, cache_values, child_counts, child_slots, w_qkv, w_out, w_up, w_down):
    row_total = child_stream.shape[0]
    block_count = row_total // R_DEV
    is_live = jnp.arange(4, dtype=jnp.int32)[None, :] < child_counts[:, None]
    target = jnp.where(is_live, child_slots, row_total).reshape(-1).astype(jnp.int32)
    parents = jnp.repeat(jnp.arange(row_total, dtype=jnp.int32), 4)
    parent_of = jnp.zeros((row_total,), jnp.int32).at[target].set(parents, mode='drop')

    def one_block(start):
        stream = lax.dynamic_slice_in_dim(child_stream, start, R_DEV, 0).astype(jnp.float32)
        owners = lax.dynamic_slice_in_dim(parent_of, start, R_DEV, 0)
        normed = rms_rows(stream).astype(jnp.bfloat16)
        queries = jnp.dot(normed, w_qkv[0], preferred_element_type=jnp.float32).astype(jnp.bfloat16)
        own_keys = jnp.dot(normed, w_qkv[1], preferred_element_type=jnp.float32).astype(jnp.bfloat16)
        own_values = jnp.dot(normed, w_qkv[2], preferred_element_type=jnp.float32).astype(jnp.bfloat16)
        attended = attend_rows(queries, own_keys, own_values, cache_keys[owners], cache_values[owners], HD)
        attn_out = grouped_product(attended, w_out, N_HEAD)
        hidden = (stream + attn_out).astype(jnp.bfloat16)
        normed_two = rms_rows(hidden.astype(jnp.float32)).astype(jnp.bfloat16)
        activated = jax.nn.gelu(jnp.dot(normed_two, w_up, preferred_element_type=jnp.float32)).astype(jnp.bfloat16)
        down = grouped_product(activated, w_down, N_HEAD)
        layer_out = (hidden.astype(jnp.float32) + down).astype(jnp.bfloat16)
        return (layer_out, jnp.stack([own_keys, own_values], axis=1))
    starts = jnp.arange(block_count, dtype=jnp.int32) * R_DEV
    outputs, pairs = lax.map(one_block, starts)
    return (outputs.reshape(row_total, -1), pairs.reshape(row_total, 2, -1))
```

```python
import functools

import jax
import jax.numpy as jnp
from jax import lax
from jax.experimental import pallas as pl
from jax.experimental.pallas import tpu as pltpu
from jax.sharding import Mesh, PartitionSpec as P

HD = 64
PEERS = 32
CAP = 48
ROWS = 1024
ITEMS = PEERS * CAP
MSG = 64
SAMPLE = ("z", "y")
HEAD = ("x", "core")
VLIM = 48 * 1024 * 1024
F32 = jnp.float32
BF = jnp.bfloat16
NT = (((1,), (1,)), ((), ()))
TN = (((0,), (0,)), ((), ()))


def iota(shape, dim):
    return lax.broadcasted_iota(jnp.int32, shape, dim)


def call(kernel, out, cost, **kw):
    return pl.pallas_call(
        kernel,
        out_shape=out,
        compiler_params=pltpu.CompilerParams(vmem_limit_bytes=VLIM),
        cost_estimate=pl.CostEstimate(flops=cost[0], bytes_accessed=cost[1], transcendentals=0),
        **kw,
    )


def sds(shape, dtype):
    return jax.ShapeDtypeStruct(shape, dtype)


def plan_kernel(cnt_ref, slot_ref, send_ref, par_ref):
    width = 256
    blocks = ROWS // width
    cnt = cnt_ref[...]
    tri = (iota((width, width), 0) <= iota((width, width), 1)).astype(F32).astype(BF)
    ow = iota((PEERS, width), 0)
    groups = []
    for k in range(4):
        for b in range(blocks):
            sl = slot_ref[k : k + 1, b * width : (b + 1) * width]
            live = cnt[:, b * width : (b + 1) * width] > k
            owner = jnp.where(live, sl // ROWS, -1)
            member = (ow == owner).astype(F32)
            groups.append((sl, live, member, b))
    stacked = jnp.concatenate([g[2].astype(BF) for g in groups], axis=0)
    inc = jnp.dot(stacked, tri, preferred_element_type=F32)
    base = jnp.zeros((PEERS, 1), F32)
    total = jnp.zeros((5 * PEERS, CAP), F32)
    parent = iota((1, width), 1)
    for g, (sl, live, member, b) in enumerate(groups):
        run = inc[g * PEERS : (g + 1) * PEERS]
        rank = jnp.sum(member * (run + (base - 1.0)), axis=0, keepdims=True)
        base = base + run[:, width - 1 : width]
        rank = jnp.where(live, rank.astype(jnp.int32), -1)
        place = (iota((CAP, width), 0) == rank).astype(F32).astype(BF)
        local = sl % ROWS
        par = parent + b * width
        left = jnp.concatenate(
            [
                member * (local // 32).astype(F32),
                member * (local % 32).astype(F32),
                member,
                member * (par // 32).astype(F32),
                member * (par % 32).astype(F32),
            ],
            axis=0,
        ).astype(BF)
        total = total + lax.dot_general(left, place, NT, preferred_element_type=F32)
    whole = total.astype(jnp.int32)
    have = whole[2 * PEERS : 3 * PEERS] > 0
    send = jnp.where(have, whole[:PEERS] * 32 + whole[PEERS : 2 * PEERS], -1)
    pars = jnp.where(have, whole[3 * PEERS : 4 * PEERS] * 32 + whole[4 * PEERS :], -1)
    fill = jnp.full((PEERS, 128 - CAP), -1, jnp.int32)
    send_ref[...] = jnp.concatenate([send, fill], axis=1)
    par_ref[...] = jnp.concatenate([pars, fill], axis=1)


def column(lists, count, depth):
    shape = (count, depth, 128)
    picked = jnp.where(
        iota(shape, 1) == iota(shape, 2), jnp.broadcast_to(lists[:, None, :], shape), 0.0
    )
    return jnp.sum(picked, axis=2, keepdims=True).reshape(count * depth, 1)


def expand_kernel(par_ref, k_ref, v_ref, out_ref):
    peers = par_ref.shape[0]
    col = column(par_ref[...].astype(F32), peers, CAP)
    hot = (col == iota((peers * CAP, ROWS), 1).astype(F32)).astype(F32).astype(BF)
    out_ref[:, :ROWS] = jnp.dot(hot, k_ref[...], preferred_element_type=F32).astype(BF)
    out_ref[:, ROWS:] = jnp.dot(hot, v_ref[...], preferred_element_type=F32).astype(BF)


def query_kernel(recv_ref, q_ref, out_ref):
    peers = recv_ref.shape[0]
    col = column(recv_ref[...].astype(F32), peers, CAP)
    hot = (col == iota((peers * CAP, ROWS), 1).astype(F32)).astype(F32).astype(BF)
    out_ref[...] = jnp.dot(hot, q_ref[...], preferred_element_type=F32).astype(BF)


def place_kernel(recv_ref, q_ref, k_ref, back_ref, src_ref, mask_ref, own_ref):
    slot = recv_ref[...]
    high = jnp.where(slot >= 0, slot // 32, -1)
    low = slot % 32
    acc = jnp.zeros((64, 32), F32)
    where_c = iota((32, 128), 1).astype(F32)
    for s in range(PEERS):
        a = (iota((32, 128), 0) == high[s : s + 1, :]).astype(F32)
        b = (iota((32, 128), 0) == low[s : s + 1, :]).astype(F32).astype(BF)
        left = jnp.concatenate([a * float(s), a * where_c], axis=0).astype(BF)
        acc = acc + lax.dot_general(left, b, NT, preferred_element_type=F32)
    wide = jnp.concatenate([acc, jnp.zeros((64, 96), F32)], axis=1)
    src = column(wide[:32], 32, 32)
    place = column(wide[32:], 32, 32)
    pos = src * float(CAP) + place
    lane = iota((ROWS, 128), 1).astype(F32)
    src_ref[...] = (lane == src).astype(F32).astype(BF)
    mask_ref[...] = (lane == place).astype(F32)
    for t in range(ITEMS // 256):
        items = (iota((ROWS, 256), 1) + t * 256).astype(F32)
        back_ref[:, t * 256 : (t + 1) * 256] = (items == pos).astype(F32).astype(BF)
    prod = q_ref[...].astype(F32) * k_ref[...].astype(F32) * (1.0 / HD**0.5)
    s0 = jnp.sum(prod[:, :HD], axis=1, keepdims=True)
    s1 = jnp.sum(prod[:, HD:], axis=1, keepdims=True)
    own_ref[...] = jnp.where(iota((ROWS, 128), 1) < HD, s0, s1)


def attend_kernel(q_ref, kv_ref, out_ref):
    n = q_ref.shape[0]
    peers = n // CAP
    sel_p = iota((16, ROWS), 1) // 128
    sel_h = (iota((16, ROWS), 1) % 128) // HD
    sel = (iota((16, ROWS), 0) == sel_h * 8 + sel_p).astype(F32).astype(BF)
    q = q_ref[...].astype(F32)
    highs, lows = [], []
    for p in range(8):
        prod = q * kv_ref[:, p * 128 : (p + 1) * 128].astype(F32)
        high = prod.astype(BF)
        highs.append(high)
        lows.append((prod - high.astype(F32)).astype(BF))
    score = lax.dot_general(sel, jnp.concatenate(highs, axis=1), NT, preferred_element_type=F32)
    score = score + lax.dot_general(
        sel, jnp.concatenate(lows, axis=1), NT, preferred_element_type=F32
    )
    score = score * (1.0 / HD**0.5)
    weights, rows = [], []
    for h in range(2):
        part = score[h * 8 : (h + 1) * 8]
        top = jnp.max(part, axis=0, keepdims=True)
        expo = jnp.exp(part - top)
        norm = jnp.sum(expo, axis=0, keepdims=True)
        weights.append(expo / norm)
        lse = top + jnp.log(norm)
        for _ in range(3):
            piece = lse.astype(BF).astype(F32)
            rows.append(piece)
            lse = lse - piece
    weight = jnp.concatenate(weights, axis=0).astype(BF)
    wide = lax.dot_general(weight, sel, TN, preferred_element_type=F32)
    ctx = wide[:, :128] * kv_ref[:, ROWS : ROWS + 128].astype(F32)
    for p in range(1, 8):
        ctx = ctx + wide[:, p * 128 : (p + 1) * 128] * kv_ref[
            :, ROWS + p * 128 : ROWS + (p + 1) * 128
        ].astype(F32)
    out_ref[:, :CAP, :] = ctx.astype(BF).reshape(peers, CAP, 128)
    tail = jnp.concatenate(rows + [jnp.zeros((10, n), F32)], axis=0)
    for o in range(peers):
        piece = tail[:, o * CAP : (o + 1) * CAP]
        piece = jnp.concatenate([piece, jnp.zeros((16, 128 - CAP), F32)], axis=1)
        out_ref[o, CAP:, :] = piece.astype(BF)


def merge_kernel(msg_ref, back_ref, src_ref, mask_ref, own_ref, v_ref, out_ref):
    rows = back_ref.shape[0]
    ctx = msg_ref[:, :CAP, :].reshape(ITEMS, 128)
    ctx = jnp.dot(back_ref[...], ctx, preferred_element_type=F32)
    cols = []
    src = src_ref[:, :PEERS]
    for h in range(2):
        lse = jnp.zeros((rows, 128), F32)
        for j in range(3):
            part = msg_ref[:, CAP + h * 3 + j, :].reshape(PEERS, 128)
            lse = lse + jnp.dot(src, part, preferred_element_type=F32)
        cols.append(jnp.sum(lse * mask_ref[...], axis=1, keepdims=True))
    lse = jnp.where(iota((rows, 128), 1) < HD, cols[0], cols[1])
    own = own_ref[...]
    top = jnp.maximum(lse, own)
    a = jnp.exp(lse - top)
    b = jnp.exp(own - top)
    out_ref[...] = ((a * ctx + b * v_ref[...].astype(F32)) / (a + b)).astype(BF)


def ffn_kernel(head_ref, *refs):
    pieces = refs[:8]
    x_ref, wo_ref, wu_ref, wd_ref = refs[8:12]
    same_ref, other_ref, part_ref = refs[12:15]
    att, hid, down = refs[15:18]
    for i in range(8):
        at = pl.multiple_of(head_ref[i] * 128, 128)
        att[:, pl.ds(at, 128)] = pieces[i][...]
    x = x_ref[...].astype(F32)
    hidden = (x + jnp.dot(att[...], wo_ref[...], preferred_element_type=F32)).astype(BF)
    hid[...] = hidden
    hf = hidden.astype(F32)
    scale = lax.rsqrt(jnp.mean(hf * hf, axis=-1, keepdims=True) + 1e-05)
    normed = (hf * scale).astype(BF)
    up = jnp.dot(normed, wu_ref[...], preferred_element_type=F32)
    act = jax.nn.gelu(up).astype(BF)
    down[...] = jnp.dot(act, wd_ref[...], preferred_element_type=F32).astype(BF)
    part_ref[...] = hid[:, pl.ds(pl.multiple_of(head_ref[0] * 128, 128), 128)]
    for i in range(4):
        at = pl.multiple_of(head_ref[i] * 128, 128)
        same_ref[i] = down[:, pl.ds(at, 128)]
        at = pl.multiple_of(head_ref[4 + i] * 128, 128)
        other_ref[i] = down[:, pl.ds(at, 128)]


def shift(x, axis, by, size):
    return lax.ppermute(x, axis, [(i, (i + by) % size) for i in range(size)])


def rms_rows(stream):
    return stream * lax.rsqrt(jnp.mean(stream * stream, axis=-1, keepdims=True) + 1e-05)


def body(stream_in, keys, values, counts, slots, w_qkv, w_out, w_up, w_down):
    wo_full = lax.all_gather(w_out, HEAD, axis=0, tiled=True)
    send, par = call(
        plan_kernel,
        (sds((PEERS, 128), jnp.int32), sds((PEERS, 128), jnp.int32)),
        (4 * 10**8, 10**6),
    )(counts.reshape(1, ROWS), slots.T)
    recv = lax.all_to_all(
        send.reshape(PEERS, 1, 128), SAMPLE, split_axis=0, concat_axis=0, tiled=True
    ).reshape(PEERS, 128)

    stream = stream_in.astype(F32)
    normed = rms_rows(stream).astype(BF)
    projected = jnp.einsum("rd,tdc->trc", normed, w_qkv, preferred_element_type=F32).astype(BF)
    query, own_key, own_value = projected[0], projected[1], projected[2]
    new_kv = jnp.stack([own_key, own_value], axis=1)

    kv = call(
        expand_kernel,
        sds((ITEMS, 2 * ROWS), BF),
        (2 * ITEMS * ROWS * ROWS * 2, 12 * 10**6),
        grid=(4,),
        in_specs=[
            pl.BlockSpec((8, 128), lambda i: (i, 0)),
            pl.BlockSpec((ROWS, ROWS), lambda i: (0, 0)),
            pl.BlockSpec((ROWS, ROWS), lambda i: (0, 0)),
        ],
        out_specs=pl.BlockSpec((8 * CAP, 2 * ROWS), lambda i: (i, 0)),
    )(par, keys.reshape(ROWS, ROWS), values.reshape(ROWS, ROWS))

    q_send = call(
        query_kernel,
        sds((ITEMS, 128), BF),
        (2 * ITEMS * ROWS * 128, 10**6),
        grid=(4,),
        in_specs=[
            pl.BlockSpec((8, 128), lambda i: (i, 0)),
            pl.BlockSpec((ROWS, 128), lambda i: (0, 0)),
        ],
        out_specs=pl.BlockSpec((8 * CAP, 128), lambda i: (i, 0)),
    )(recv, query)
    q_recv = lax.all_to_all(q_send, SAMPLE, split_axis=0, concat_axis=0, tiled=True)

    back, src, mask, own = call(
        place_kernel,
        (
            sds((ROWS, ITEMS), BF),
            sds((ROWS, 128), BF),
            sds((ROWS, 128), F32),
            sds((ROWS, 128), F32),
        ),
        (10**9, 6 * 10**6),
    )(recv, query, own_key)

    msg = call(
        attend_kernel,
        sds((PEERS, MSG, 128), BF),
        (2 * ITEMS * ROWS * 128, 8 * 10**6),
        grid=(4,),
        in_specs=[
            pl.BlockSpec((8 * CAP, 128), lambda i: (i, 0)),
            pl.BlockSpec((8 * CAP, 2 * ROWS), lambda i: (i, 0)),
        ],
        out_specs=pl.BlockSpec((8, MSG, 128), lambda i: (i, 0, 0)),
    )(q_recv, kv)
    answer = lax.all_to_all(msg, SAMPLE, split_axis=0, concat_axis=0, tiled=True)

    whole = lambda *shape: pl.BlockSpec(shape, lambda i: (0,) * len(shape))
    attended = call(
        merge_kernel,
        sds((ROWS, 128), BF),
        (2 * ITEMS * ROWS * 128, 5 * 10**6),
        grid=(4,),
        in_specs=[
            whole(PEERS, MSG, 128),
            pl.BlockSpec((256, ITEMS), lambda i: (i, 0)),
            pl.BlockSpec((256, 128), lambda i: (i, 0)),
            pl.BlockSpec((256, 128), lambda i: (i, 0)),
            pl.BlockSpec((256, 128), lambda i: (i, 0)),
            pl.BlockSpec((256, 128), lambda i: (i, 0)),
        ],
        out_specs=pl.BlockSpec((256, 128), lambda i: (i, 0)),
    )(answer, back, src, mask, own, own_value)

    near = [attended] + [shift(attended, "x", d, 4) for d in (1, 3, 2)]
    far = [shift(piece, "core", 1, 2) for piece in near]
    x = lax.axis_index("x")
    core = lax.axis_index("core")
    xs = jnp.stack([x, (x + 3) % 4, (x + 1) % 4, (x + 2) % 4])
    heads = jnp.concatenate([xs * 2 + core, xs * 2 + 1 - core]).astype(jnp.int32)

    rows = lambda *shape: pl.BlockSpec(shape, lambda i, h: (i,) + (0,) * (len(shape) - 1))
    fixed = lambda *shape: pl.BlockSpec(shape, lambda i, h: (0,) * len(shape))
    blocks = lambda: pl.BlockSpec((4, 256, 128), lambda i, h: (0, i, 0))
    same, other, hidden_part = call(
        ffn_kernel,
        (sds((4, ROWS, 128), BF), sds((4, ROWS, 128), BF), sds((ROWS, 128), BF)),
        (4 * 10**9, 12 * 10**6),
        grid_spec=pltpu.PrefetchScalarGridSpec(
            num_scalar_prefetch=1,
            grid=(4,),
            in_specs=[rows(256, 128)] * 8
            + [rows(256, ROWS), fixed(ROWS, ROWS), fixed(ROWS, 512), fixed(512, ROWS)],
            out_specs=(blocks(), blocks(), rows(256, 128)),
            scratch_shapes=[
                pltpu.VMEM((256, ROWS), BF),
                pltpu.VMEM((256, ROWS), BF),
                pltpu.VMEM((256, ROWS), BF),
            ],
        ),
    )(heads, *near, *far, stream_in, wo_full, w_up, w_down)

    swapped = shift(other, "core", 1, 2)
    pair = same.astype(F32) + swapped.astype(F32)
    sums = pair.astype(BF)
    got = [shift(sums[1], "x", 3, 4), shift(sums[2], "x", 1, 4), shift(sums[3], "x", 2, 4)]
    total = pair[0] + got[0].astype(F32) + got[1].astype(F32) + got[2].astype(F32)
    layer_out = (hidden_part.astype(F32) + total).astype(BF)
    return (layer_out, new_kv)


def solution(mesh):
    grid = Mesh(mesh.devices.reshape(8, 4, 4, 2), ("z", "y", "x", "core"))
    in_specs = (
        P(SAMPLE, None),
        P(SAMPLE, None, HEAD),
        P(SAMPLE, None, HEAD),
        P(SAMPLE),
        P(SAMPLE, None),
        P(None, None, HEAD),
        P(HEAD, None),
        P(None, HEAD),
        P(HEAD, None),
    )
    out_specs = (P(SAMPLE, HEAD), P(SAMPLE, None, HEAD))
    return jax.shard_map(body, mesh=grid, in_specs=in_specs, out_specs=out_specs, check_vma=False)
```

```python
import functools

import jax
import jax.numpy as jnp
from jax import lax
from jax.experimental import pallas as pl
from jax.experimental.pallas import tpu as pltpu
from jax.sharding import Mesh, PartitionSpec as P

HD = 64
PEERS = 32
CAP = 48
ROWS = 1024
ITEMS = PEERS * CAP
MSG = 64
SAMPLE = ("z", "y")
HEAD = ("x", "core")
F32 = jnp.float32
BF = jnp.bfloat16
NT = (((1,), (1,)), ((), ()))
TN = (((0,), (0,)), ((), ()))


def iota(shape, dim):
    return lax.broadcasted_iota(jnp.int32, shape, dim)


def call(kernel, out, cost, vmem=24, **kw):
    return pl.pallas_call(
        kernel,
        out_shape=out,
        compiler_params=pltpu.CompilerParams(vmem_limit_bytes=vmem * 2**20),
        cost_estimate=pl.CostEstimate(flops=cost[0], bytes_accessed=cost[1], transcendentals=0),
        **kw,
    )


def keep(x, space=pltpu.VMEM):
    return pltpu.with_memory_space_constraint(x, space)


def sds(shape, dtype):
    return jax.ShapeDtypeStruct(shape, dtype)


def plan_kernel(cnt_ref, slot_ref, send_ref, par_ref):
    width = 256
    blocks = ROWS // width
    cnt = cnt_ref[...]
    tri = (iota((width, width), 0) <= iota((width, width), 1)).astype(F32).astype(BF)
    ow = iota((PEERS, width), 0)
    groups = []
    for k in range(4):
        for b in range(blocks):
            sl = slot_ref[k : k + 1, b * width : (b + 1) * width]
            live = cnt[:, b * width : (b + 1) * width] > k
            owner = jnp.where(live, sl // ROWS, -1)
            member = (ow == owner).astype(F32)
            groups.append((sl, live, member, b))
    stacked = jnp.concatenate([g[2].astype(BF) for g in groups], axis=0)
    inc = jnp.dot(stacked, tri, preferred_element_type=F32)
    base = jnp.zeros((PEERS, 1), F32)
    total = jnp.zeros((5 * PEERS, CAP), F32)
    parent = iota((1, width), 1)
    for g, (sl, live, member, b) in enumerate(groups):
        run = inc[g * PEERS : (g + 1) * PEERS]
        rank = jnp.sum(member * (run + (base - 1.0)), axis=0, keepdims=True)
        base = base + run[:, width - 1 : width]
        rank = jnp.where(live, rank.astype(jnp.int32), -1)
        place = (iota((CAP, width), 0) == rank).astype(F32).astype(BF)
        local = sl % ROWS
        par = parent + b * width
        left = jnp.concatenate(
            [
                member * (local // 32).astype(F32),
                member * (local % 32).astype(F32),
                member,
                member * (par // 32).astype(F32),
                member * (par % 32).astype(F32),
            ],
            axis=0,
        ).astype(BF)
        total = total + lax.dot_general(left, place, NT, preferred_element_type=F32)
    whole = total.astype(jnp.int32)
    have = whole[2 * PEERS : 3 * PEERS] > 0
    send = jnp.where(have, whole[:PEERS] * 32 + whole[PEERS : 2 * PEERS], -1)
    pars = jnp.where(have, whole[3 * PEERS : 4 * PEERS] * 32 + whole[4 * PEERS :], -1)
    fill = jnp.full((PEERS, 128 - CAP), -1, jnp.int32)
    send_ref[...] = jnp.concatenate([send, fill], axis=1)
    par_ref[...] = jnp.concatenate([pars, fill], axis=1)


def pack_kernel(up_ref, down_ref, wo_ref, right_ref, left_ref, stage, sems):
    writes = []
    for n in range(2):
        half = pl.ds(n * 256, 256)
        pairs = [(down_ref.at[half], stage.at[n, pl.ds(256, 256)])]
        pairs.append((wo_ref, stage.at[n, pl.ds(512, 128)]))
        for k in range(4):
            block = pl.ds(k * 256, 256)
            pairs.append((up_ref.at[block, half], stage.at[n, pl.ds(0, 256), block]))
        copies = [
            pltpu.make_async_copy(a, b, sems.at[n * 7 + i]) for i, (a, b) in enumerate(pairs)
        ]
        for copy in copies:
            copy.start()
        writes.append((copies, (right_ref, left_ref)[n]))
    ends = []
    for n, (copies, target) in enumerate(writes):
        for copy in copies:
            copy.wait()
        end = pltpu.make_async_copy(stage.at[n], target, sems.at[n * 7 + 6])
        end.start()
        ends.append(end)
    for end in ends:
        end.wait()


def column(lists, count, depth):
    shape = (count, depth, 128)
    picked = jnp.where(
        iota(shape, 1) == iota(shape, 2), jnp.broadcast_to(lists[:, None, :], shape), 0.0
    )
    return jnp.sum(picked, axis=2, keepdims=True).reshape(count * depth, 1)


def expand_kernel(par_ref, k_ref, v_ref, out_ref):
    peers = par_ref.shape[0]
    col = column(par_ref[...].astype(F32), peers, CAP)
    hot = (col == iota((peers * CAP, ROWS), 1).astype(F32)).astype(F32).astype(BF)
    out_ref[:, :ROWS] = jnp.dot(hot, k_ref[...], preferred_element_type=F32).astype(BF)
    out_ref[:, ROWS:] = jnp.dot(hot, v_ref[...], preferred_element_type=F32).astype(BF)


def query_kernel(recv_ref, q_ref, out_ref):
    peers = recv_ref.shape[0]
    col = column(recv_ref[...].astype(F32), peers, CAP)
    hot = (col == iota((peers * CAP, ROWS), 1).astype(F32)).astype(F32).astype(BF)
    out_ref[...] = jnp.dot(hot, q_ref[...], preferred_element_type=F32).astype(BF)


def place_kernel(recv_ref, q_ref, k_ref, out_ref):
    slot = recv_ref[...]
    high = jnp.where(slot >= 0, slot // 32, -1)
    low = slot % 32
    acc = jnp.zeros((64, 32), F32)
    where_c = iota((32, 128), 1).astype(F32)
    for s in range(PEERS):
        a = (iota((32, 128), 0) == high[s : s + 1, :]).astype(F32)
        b = (iota((32, 128), 0) == low[s : s + 1, :]).astype(F32).astype(BF)
        left = jnp.concatenate([a * float(s), a * where_c], axis=0).astype(BF)
        acc = acc + lax.dot_general(left, b, NT, preferred_element_type=F32)
    wide = jnp.concatenate([acc, jnp.zeros((64, 96), F32)], axis=1)
    src = column(wide[:32], 32, 32)
    place = column(wide[32:], 32, 32)
    prod = q_ref[...].astype(F32) * k_ref[...].astype(F32) * (1.0 / HD**0.5)
    s0 = jnp.sum(prod[:, :HD], axis=1, keepdims=True)
    s1 = jnp.sum(prod[:, HD:], axis=1, keepdims=True)
    lane = iota((ROWS, 128), 1)
    out_ref[...] = jnp.where(
        lane == 0, src, jnp.where(lane == 1, place, jnp.where(lane == 2, s0, s1))
    )


def attend_kernel(q_ref, kv_ref, out_ref):
    n = q_ref.shape[0]
    peers = n // CAP
    sel_p = iota((16, ROWS), 1) // 128
    sel_h = (iota((16, ROWS), 1) % 128) // HD
    sel = (iota((16, ROWS), 0) == sel_h * 8 + sel_p).astype(F32).astype(BF)
    q = q_ref[...].astype(F32)
    highs, lows = [], []
    for p in range(8):
        prod = q * kv_ref[:, p * 128 : (p + 1) * 128].astype(F32)
        high = prod.astype(BF)
        highs.append(high)
        lows.append((prod - high.astype(F32)).astype(BF))
    score = lax.dot_general(sel, jnp.concatenate(highs, axis=1), NT, preferred_element_type=F32)
    score = score + lax.dot_general(
        sel, jnp.concatenate(lows, axis=1), NT, preferred_element_type=F32
    )
    score = score * (1.0 / HD**0.5)
    weights, rows = [], []
    for h in range(2):
        part = score[h * 8 : (h + 1) * 8]
        top = jnp.max(part, axis=0, keepdims=True)
        expo = jnp.exp(part - top)
        norm = jnp.sum(expo, axis=0, keepdims=True)
        weights.append(expo / norm)
        lse = top + jnp.log(norm)
        for _ in range(3):
            piece = lse.astype(BF).astype(F32)
            rows.append(piece)
            lse = lse - piece
    weight = jnp.concatenate(weights, axis=0).astype(BF)
    wide = lax.dot_general(weight, sel, TN, preferred_element_type=F32)
    ctx = wide[:, :128] * kv_ref[:, ROWS : ROWS + 128].astype(F32)
    for p in range(1, 8):
        ctx = ctx + wide[:, p * 128 : (p + 1) * 128] * kv_ref[
            :, ROWS + p * 128 : ROWS + (p + 1) * 128
        ].astype(F32)
    out_ref[:, :CAP, :] = ctx.astype(BF).reshape(peers, CAP, 128)
    tail = jnp.concatenate(rows + [jnp.zeros((10, n), F32)], axis=0)
    for o in range(peers):
        piece = tail[:, o * CAP : (o + 1) * CAP]
        piece = jnp.concatenate([piece, jnp.zeros((16, 128 - CAP), F32)], axis=1)
        out_ref[o, CAP:, :] = piece.astype(BF)


def merge_kernel(info_ref, msg_ref, place_ref, v_ref, mine_ref, theirs_ref):
    rows = 256
    outs = [r.at[pl.ds(n * rows, rows)] for r in (mine_ref, theirs_ref) for n in range(2)]
    ctx_all = msg_ref[:, :CAP, :].reshape(ITEMS, 128)
    parts = []
    for h in range(2):
        for j in range(3):
            parts.append(msg_ref[:, CAP + h * 3 + j, :].reshape(PEERS, 128))
    parts = jnp.concatenate(parts, axis=1)
    for i, out in enumerate(outs):
        block = (info_ref[1] if i < 2 else 1 - info_ref[1]) + 2 * (i % 2)
        at = pl.ds(pl.multiple_of(block * rows, rows), rows)
        known = place_ref[at, :]
        src, place = known[:, 0:1], known[:, 1:2]
        lane = iota((rows, 128), 1)
        lanes = lane.astype(F32)
        pos = src * float(CAP) + place
        hot = (iota((rows, ITEMS), 1).astype(F32) == pos).astype(F32).astype(BF)
        ctx = jnp.dot(hot, ctx_all, preferred_element_type=F32)
        from_src = (iota((rows, PEERS), 1).astype(F32) == src).astype(F32).astype(BF)
        lists = jnp.dot(from_src, parts, preferred_element_type=F32)
        cols = []
        for h in range(2):
            base = h * 384
            lse = lists[:, base : base + 128] + lists[:, base + 128 : base + 256]
            lse = lse + lists[:, base + 256 : base + 384]
            lse = jnp.where(lanes == place, lse, 0.0)
            cols.append(jnp.sum(lse, axis=1, keepdims=True))
        lse = jnp.where(lane < HD, cols[0], cols[1])
        own = jnp.where(lane < HD, known[:, 2:3], known[:, 3:4])
        top = jnp.maximum(lse, own)
        a = jnp.exp(lse - top)
        b = jnp.exp(own - top)
        out[...] = ((a * ctx + b * v_ref[at, :].astype(F32)) / (a + b)).astype(BF)


def project_kernel(info_ref, *refs):
    rows = jnp.concatenate([r[...] for r in refs[:4]], axis=1)
    weight = jnp.concatenate([r[...] for r in refs[4:8]], axis=0)
    refs[8][...] = jnp.dot(rows, weight, preferred_element_type=F32).astype(BF)


def ffn_kernel(
    info_ref, x0_ref, x1_ref, p_ref, r_ref, up_ref, down_ref, right_ref, left_ref, *refs
):
    same_ref, other_ref, ups, downs, hid, acc, sems = refs
    pairs = [(up_ref, ups.at[0]), (down_ref, downs.at[0])]
    for n, src in enumerate((right_ref, left_ref)):
        for k in range(4):
            block = pl.ds(k * 256, 256)
            pairs.append((src.at[pl.ds(0, 256), block], ups.at[1, block, pl.ds(n * 256, 256)]))
        pairs.append((src.at[pl.ds(256, 256)], downs.at[1, pl.ds(n * 256, 256)]))
    copies = [pltpu.make_async_copy(a, b, sems.at[i]) for i, (a, b) in enumerate(pairs)]
    for copy in copies:
        copy.start()
    normed = []
    for n, x_ref in enumerate((x0_ref, x1_ref)):
        at = pl.ds(n * 256, 256)
        attn = p_ref[at].astype(F32) + r_ref[at].astype(F32)
        hidden = (x_ref[...].astype(F32) + attn).astype(BF).astype(F32)
        scale = lax.rsqrt(jnp.mean(hidden * hidden, axis=-1, keepdims=True) + 1e-05)
        normed.append((hidden * scale).astype(BF))
        hid[at] = jnp.where(info_ref[0] // 2 == n, hidden, 0.0)
    for unit in range(2):
        for n in range(2):
            at = pl.ds(n * 256, 256)
            if n == 0:
                for copy in (copies[:1], copies[2:6] + copies[7:11])[unit]:
                    copy.wait()
            up = jnp.dot(normed[n], ups[unit], preferred_element_type=F32)
            act = jax.nn.gelu(up).astype(BF)
            if n == 0:
                for copy in (copies[1:2], [copies[6], copies[11]])[unit]:
                    copy.wait()
            down = jnp.dot(act, downs[unit], preferred_element_type=F32)
            if unit == 0:
                acc[at] = down
            else:
                acc[at] += down
    core = info_ref[2]
    for d in range(4):
        head = ((info_ref[0] + d) % 4) * 2
        at = pl.ds(pl.multiple_of((head + core) * 128, 128), 128)
        same_ref[d] = hid[:, at] + acc[:, at]
        at = pl.ds(pl.multiple_of((head + 1 - core) * 128, 128), 128)
        other_ref[d] = acc[:, at].astype(BF)


def final_kernel(same_ref, other_ref, o0, o1, o2, o3):
    for i, out in enumerate((o0, o1, o2, o3)):
        out[...] = (same_ref[i] + other_ref[i].astype(F32)).astype(BF)


def place_rows_kernel(info_ref, p0, p1, p2, p3, out_ref):
    for n in range(2):
        at = pl.ds(n * 256, 256)
        for parity, a, b in ((info_ref[1], p0, p2), (1 - info_ref[1], p1, p3)):
            to = pl.multiple_of((parity + 2 * n) * 256, 256)
            out_ref[pl.ds(to, 256), :] = (a[at].astype(F32) + b[at].astype(F32)).astype(BF)


def shift(x, axis, by, size):
    return lax.ppermute(x, axis, [(i, (i + by) % size) for i in range(size)])


def rms_rows(stream):
    return stream * lax.rsqrt(jnp.mean(stream * stream, axis=-1, keepdims=True) + 1e-05)


def body(stream_in, keys, values, counts, slots, w_qkv, w_out, w_up, w_down):
    vmem = pl.BlockSpec(memory_space=pltpu.VMEM)
    hbm = pl.BlockSpec(memory_space=pltpu.HBM)
    x = lax.axis_index("x")
    core = lax.axis_index("core")
    info = jnp.stack([x, x % 2, core]).astype(jnp.int32)

    send, par = call(
        plan_kernel,
        (pltpu.HBM((PEERS, 128), jnp.int32), pltpu.VMEM((PEERS, 128), jnp.int32)),
        (4 * 10**8, 10**6),
    )(keep(counts.reshape(1, ROWS), pltpu.HBM), keep(slots.T, pltpu.HBM))
    for_right, for_left = call(
        pack_kernel,
        (pltpu.HBM((640, ROWS), BF), pltpu.HBM((640, ROWS), BF)),
        (0, 5 * 10**6),
        in_specs=[hbm, hbm, hbm],
        out_specs=(hbm, hbm),
        scratch_shapes=[pltpu.VMEM((2, 640, ROWS), BF), pltpu.SemaphoreType.DMA((14,))],
    )(*(keep(w, pltpu.HBM) for w in (w_up, w_down, w_out)))
    left = shift(for_right, "x", 1, 4)
    right = shift(for_left, "x", 3, 4)
    wo_two = shift(w_out, "x", 2, 4)
    recv = lax.all_to_all(
        send.reshape(PEERS, 1, 128), SAMPLE, split_axis=0, concat_axis=0, tiled=True
    ).reshape(PEERS, 128)

    stream = stream_in.astype(F32)
    normed = rms_rows(stream).astype(BF)
    projected = jnp.einsum("rd,tdc->trc", normed, w_qkv, preferred_element_type=F32).astype(BF)
    query, own_key, own_value = projected[0], projected[1], projected[2]
    new_kv = jnp.stack([own_key, own_value], axis=1)

    flat_keys, flat_values = keys.reshape(ROWS, ROWS), values.reshape(ROWS, ROWS)
    kv = call(
        expand_kernel,
        pltpu.HBM((ITEMS, 2 * ROWS), BF),
        (2 * ITEMS * ROWS * ROWS * 2, 12 * 10**6),
        grid=(4,),
        in_specs=[
            pl.BlockSpec((8, 128), lambda i: (i, 0)),
            pl.BlockSpec((ROWS, ROWS), lambda i: (0, 0)),
            pl.BlockSpec((ROWS, ROWS), lambda i: (0, 0)),
        ],
        out_specs=pl.BlockSpec((8 * CAP, 2 * ROWS), lambda i: (i, 0)),
    )(keep(par), flat_keys, flat_values)

    q_send = call(
        query_kernel,
        pltpu.HBM((ITEMS, 128), BF),
        (2 * ITEMS * ROWS * 128, 10**6),
        grid=(4,),
        in_specs=[
            pl.BlockSpec((8, 128), lambda i: (i, 0)),
            pl.BlockSpec((ROWS, 128), lambda i: (0, 0)),
        ],
        out_specs=pl.BlockSpec((8 * CAP, 128), lambda i: (i, 0)),
    )(recv, query)
    q_recv = lax.all_to_all(q_send, SAMPLE, split_axis=0, concat_axis=0, tiled=True)

    places = call(place_kernel, pltpu.HBM((ROWS, 128), F32), (10**9, 2 * 10**6))(recv, query, own_key)

    msg = call(
        attend_kernel,
        pltpu.HBM((PEERS, MSG, 128), BF),
        (2 * ITEMS * ROWS * 128, 8 * 10**6),
        grid=(4,),
        in_specs=[
            pl.BlockSpec((8 * CAP, 128), lambda i: (i, 0)),
            pl.BlockSpec((8 * CAP, 2 * ROWS), lambda i: (i, 0)),
        ],
        out_specs=pl.BlockSpec((8, MSG, 128), lambda i: (i, 0, 0)),
    )(q_recv, keep(kv, pltpu.HBM))
    answer = lax.all_to_all(msg, SAMPLE, split_axis=0, concat_axis=0, tiled=True)
    fixed = lambda *shape: pl.BlockSpec(shape, lambda i, h: (0,) * len(shape))
    block = lambda n: pl.BlockSpec((256, ROWS), lambda i, h: (h[1] + 2 * n, 0))
    pair = sds((512, 128), BF)
    smem = pl.BlockSpec(memory_space=pltpu.SMEM)
    mine, theirs = call(
        merge_kernel,
        (pair, pair),
        (2 * ITEMS * ROWS * 128, 5 * 10**6),
        in_specs=[smem] + [vmem] * 3,
        out_specs=(vmem, vmem),
    )(info, answer, keep(places, pltpu.HBM), own_value)

    from_left = shift(theirs, "x", 1, 4)
    from_right = shift(theirs, "x", 3, 4)
    from_two = shift(mine, "x", 2, 4)
    last = lambda at: pl.BlockSpec((128, ROWS), lambda i, h: (at, 0))
    partial = call(
        project_kernel,
        sds((512, ROWS), BF),
        (6 * 10**8, 3 * 10**6),
        grid_spec=pltpu.PrefetchScalarGridSpec(
            num_scalar_prefetch=1,
            grid=(1,),
            in_specs=[fixed(512, 128)] * 4 + [last(0), last(4), last(4), last(0)],
            out_specs=fixed(512, ROWS),
        ),
    )(info, mine, from_left, from_right, from_two, w_out, left, right, wo_two)
    partner = shift(partial, "core", 1, 2)

    same, other = call(
        ffn_kernel,
        (sds((4, 512, 128), F32), sds((4, 512, 128), BF)),
        (2 * 10**9, 10 * 10**6),
        grid_spec=pltpu.PrefetchScalarGridSpec(
            num_scalar_prefetch=1,
            grid=(1,),
            in_specs=[block(0), block(1), fixed(512, ROWS), fixed(512, ROWS)] + [hbm] * 4,
            out_specs=(fixed(4, 512, 128), fixed(4, 512, 128)),
            scratch_shapes=[
                pltpu.VMEM((2, ROWS, 512), BF),
                pltpu.VMEM((2, 512, ROWS), BF),
                pltpu.VMEM((512, ROWS), F32),
                pltpu.VMEM((512, ROWS), F32),
                pltpu.SemaphoreType.DMA((12,)),
            ],
        ),
    )(
        info,
        stream_in,
        stream_in,
        partial,
        partner,
        *(keep(w, pltpu.HBM) for w in (w_up, w_down, right, left)),
    )

    swapped = shift(other, "core", 1, 2)
    done = call(final_kernel, (pair,) * 4, (10**6, 10**6))(same, swapped)
    parts = [done[0]] + [shift(done[d], "x", d, 4) for d in (1, 2, 3)]
    layer_out = call(
        place_rows_kernel,
        sds((ROWS, 128), BF),
        (10**6, 5 * 10**5),
        in_specs=[smem] + [vmem] * 4,
        out_specs=vmem,
    )(info, *parts)
    return (layer_out, new_kv)


def solution(mesh):
    grid = Mesh(mesh.devices.reshape(8, 4, 4, 2), ("z", "y", "x", "core"))
    in_specs = (
        P(SAMPLE, None),
        P(SAMPLE, None, HEAD),
        P(SAMPLE, None, HEAD),
        P(SAMPLE),
        P(SAMPLE, None),
        P(None, None, HEAD),
        P(HEAD, None),
        P(None, HEAD),
        P(HEAD, None),
    )
    out_specs = (P(SAMPLE, HEAD), P(SAMPLE, None, HEAD))
    return jax.shard_map(body, mesh=grid, in_specs=in_specs, out_specs=out_specs, check_vma=False)
```

```python
import functools

import jax
import jax.numpy as jnp
from jax import lax
from jax.experimental import pallas as pl
from jax.experimental.pallas import tpu as pltpu
from jax.sharding import Mesh, PartitionSpec as P

HD = 64
PEERS = 32
CAP = 48
ROWS = 1024
ITEMS = PEERS * CAP
MSG = 64
LOW = 16
FULL = PEERS // 2
REST = CAP - LOW
SAMPLE = ("z", "y")
HEAD = ("x", "core")
F32 = jnp.float32
BF = jnp.bfloat16
NT = (((1,), (1,)), ((), ()))
TN = (((0,), (0,)), ((), ()))


def iota(shape, dim):
    return lax.broadcasted_iota(jnp.int32, shape, dim)


def call(kernel, out, cost, vmem=24, **kw):
    return pl.pallas_call(
        kernel,
        out_shape=out,
        compiler_params=pltpu.CompilerParams(vmem_limit_bytes=vmem * 2**20),
        cost_estimate=pl.CostEstimate(flops=cost[0], bytes_accessed=cost[1], transcendentals=0),
        **kw,
    )


def keep(x, space=pltpu.VMEM):
    return pltpu.with_memory_space_constraint(x, space)


def sds(shape, dtype):
    return jax.ShapeDtypeStruct(shape, dtype)


def full_peers(last):
    rows, cols = iota((PEERS, PEERS), 0), iota((PEERS, PEERS), 1)
    order = jnp.sum(jnp.where(rows < cols, last, 0.0), axis=0, keepdims=True)
    flag = jnp.sum(jnp.where(rows == cols, last, 0.0), axis=0, keepdims=True)
    hit = iota((FULL, PEERS), 0).astype(F32) == order
    return jnp.where(hit, flag, 0.0).astype(BF)


def peer_numbers(chosen):
    numbers = iota((PEERS, 128), 0).astype(F32).astype(BF)
    return jnp.dot(chosen, numbers, preferred_element_type=F32).astype(jnp.int32)


def plan_kernel(cnt_ref, slot_ref, send_ref, par_ref, full_ref):
    width = 256
    blocks = ROWS // width
    cnt = cnt_ref[...]
    tri = (iota((width, width), 0) <= iota((width, width), 1)).astype(F32).astype(BF)
    ow = iota((PEERS, width), 0)
    groups = []
    for k in range(4):
        for b in range(blocks):
            sl = slot_ref[k : k + 1, b * width : (b + 1) * width]
            live = cnt[:, b * width : (b + 1) * width] > k
            owner = jnp.where(live, sl // ROWS, -1)
            member = (ow == owner).astype(F32)
            groups.append((sl, live, member, b))
    stacked = jnp.concatenate([g[2].astype(BF) for g in groups], axis=0)
    inc = jnp.dot(stacked, tri, preferred_element_type=F32)
    base = jnp.zeros((PEERS, 1), F32)
    total = jnp.zeros((5 * PEERS, CAP), F32)
    parent = iota((1, width), 1)
    for g, (sl, live, member, b) in enumerate(groups):
        run = inc[g * PEERS : (g + 1) * PEERS]
        rank = jnp.sum(member * (run + (base - 1.0)), axis=0, keepdims=True)
        base = base + run[:, width - 1 : width]
        rank = jnp.where(live, rank.astype(jnp.int32), -1)
        place = (iota((CAP, width), 0) == rank).astype(F32).astype(BF)
        local = sl % ROWS
        par = parent + b * width
        left = jnp.concatenate(
            [
                member * (local // 32).astype(F32),
                member * (local % 32).astype(F32),
                member,
                member * (par // 32).astype(F32),
                member * (par % 32).astype(F32),
            ],
            axis=0,
        ).astype(BF)
        total = total + lax.dot_general(left, place, NT, preferred_element_type=F32)
    whole = total.astype(jnp.int32)
    have = whole[2 * PEERS : 3 * PEERS] > 0
    send = jnp.where(have, whole[:PEERS] * 32 + whole[PEERS : 2 * PEERS], -1)
    fill = jnp.full((PEERS, 128 - CAP), -1, jnp.int32)
    send_ref[...] = jnp.concatenate([send, fill], axis=1)
    chosen = full_peers(jnp.where(have[:, CAP - 1 :], 1.0, 0.0))
    full_ref[...] = peer_numbers(chosen)
    high, low = total[3 * PEERS : 4 * PEERS], total[4 * PEERS :]
    rest = 32.0 * jnp.dot(chosen, high.astype(BF), preferred_element_type=F32)
    rest = rest + jnp.dot(chosen, low.astype(BF), preferred_element_type=F32)
    par_ref[:PEERS, :LOW] = high[:, :LOW] * 32.0 + low[:, :LOW]
    par_ref[:PEERS, LOW:] = jnp.zeros((PEERS, 128 - LOW), F32)
    par_ref[PEERS:, :REST] = rest[:, LOW:]
    par_ref[PEERS:, REST:] = jnp.zeros((FULL, 128 - REST), F32)


def pack_kernel(up_ref, down_ref, wo_ref, right_ref, left_ref, stage, sems):
    writes = []
    for n in range(2):
        half = pl.ds(n * 256, 256)
        pairs = [(down_ref.at[half], stage.at[n, pl.ds(256, 256)])]
        pairs.append((wo_ref, stage.at[n, pl.ds(512, 128)]))
        for k in range(4):
            block = pl.ds(k * 256, 256)
            pairs.append((up_ref.at[block, half], stage.at[n, pl.ds(0, 256), block]))
        copies = [
            pltpu.make_async_copy(a, b, sems.at[n * 7 + i]) for i, (a, b) in enumerate(pairs)
        ]
        for copy in copies:
            copy.start()
        writes.append((copies, (right_ref, left_ref)[n]))
    ends = []
    for n, (copies, target) in enumerate(writes):
        for copy in copies:
            copy.wait()
        end = pltpu.make_async_copy(stage.at[n], target, sems.at[n * 7 + 6])
        end.start()
        ends.append(end)
    for end in ends:
        end.wait()


def column(lists, count, depth):
    shape = (count, depth, 128)
    picked = jnp.where(
        iota(shape, 1) == iota(shape, 2), jnp.broadcast_to(lists[:, None, :], shape), 0.0
    )
    return jnp.sum(picked, axis=2, keepdims=True).reshape(count * depth, 1)


def expand_kernel(par_ref, k_ref, v_ref, out_ref, col_ref):
    step = pl.program_id(0)

    @pl.when(step < 2)
    def _():
        lists = par_ref[pl.ds(pl.multiple_of(step * 16, 16), 16), :]
        col_ref[...] = jnp.broadcast_to(column(lists, 16, LOW), (256, 128))

    @pl.when(step >= 2)
    def _():
        lists = par_ref[pl.ds(pl.multiple_of(PEERS + (step - 2) * 8, 8), 8), :]
        col_ref[...] = jnp.broadcast_to(column(lists, 8, REST), (256, 128))

    hot = (col_ref[:, 0:1] == iota((256, ROWS), 1).astype(F32)).astype(F32).astype(BF)
    out_ref[:, :ROWS] = jnp.dot(hot, k_ref[...], preferred_element_type=F32).astype(BF)
    out_ref[:, ROWS:] = jnp.dot(hot, v_ref[...], preferred_element_type=F32).astype(BF)


def query_kernel(recv_ref, q_ref, out_ref):
    peers = recv_ref.shape[0]
    col = column(recv_ref[...].astype(F32), peers, CAP)
    hot = (col == iota((peers * CAP, ROWS), 1).astype(F32)).astype(F32).astype(BF)
    out_ref[...] = jnp.dot(hot, q_ref[...], preferred_element_type=F32).astype(BF)


def place_kernel(recv_ref, q_ref, k_ref, out_ref, full_ref):
    slot = recv_ref[...]
    last = jnp.where(slot[:, CAP - 1 : CAP] >= 0, 1.0, 0.0)
    full_ref[...] = peer_numbers(full_peers(last))
    below = iota((PEERS, PEERS), 1) < iota((PEERS, PEERS), 0)
    order = jnp.dot(
        below.astype(F32).astype(BF),
        jnp.broadcast_to(last, (PEERS, 128)).astype(BF),
        preferred_element_type=F32,
    )
    high = jnp.where(slot >= 0, slot // 32, -1)
    low = slot % 32
    acc = jnp.zeros((96, 32), F32)
    where_c = iota((32, 128), 1).astype(F32)
    for s in range(PEERS):
        a = (iota((32, 128), 0) == high[s : s + 1, :]).astype(F32)
        b = (iota((32, 128), 0) == low[s : s + 1, :]).astype(F32).astype(BF)
        left = jnp.concatenate([a * float(s), a * where_c, a * order[s : s + 1]], axis=0)
        acc = acc + lax.dot_general(left.astype(BF), b, NT, preferred_element_type=F32)
    wide = jnp.concatenate([acc, jnp.zeros((96, 96), F32)], axis=1)
    src, place, rank = (column(wide[n * 32 : n * 32 + 32], 32, 32) for n in range(3))
    rest = float(PEERS * LOW - LOW) + rank * float(REST) + place
    pos = jnp.where(place < float(LOW), src * float(LOW) + place, rest)
    prod = q_ref[...].astype(F32) * k_ref[...].astype(F32) * (1.0 / HD**0.5)
    s0 = jnp.sum(prod[:, :HD], axis=1, keepdims=True)
    s1 = jnp.sum(prod[:, HD:], axis=1, keepdims=True)
    lane = iota((ROWS, 128), 1)
    known = jnp.where(lane == 0, src, jnp.where(lane == 1, place, pos))
    out_ref[...] = jnp.where(lane == 3, s0, jnp.where(lane == 4, s1, known))


def attend_kernel(full_ref, q_ref, kv_ref, out_ref, rows_ref):
    n = 256
    step = pl.program_id(0)

    @pl.when(step < 2)
    def _():
        rows_ref[...] = q_ref[pl.ds(step * 16, 16), :LOW, :].reshape(n, 128)

    @pl.when(step >= 2)
    def _():
        for k in range(8):
            peer = full_ref[(step - 2) * 8 + k, 0]
            rows = q_ref[pl.ds(peer, 1), LOW:, :].reshape(REST, 128)
            rows_ref[k * REST : (k + 1) * REST, :] = rows

    sel_p = iota((16, ROWS), 1) // 128
    sel_h = (iota((16, ROWS), 1) % 128) // HD
    sel = (iota((16, ROWS), 0) == sel_h * 8 + sel_p).astype(F32).astype(BF)
    q = rows_ref[...].astype(F32)
    highs, lows = [], []
    for p in range(8):
        prod = q * kv_ref[:, p * 128 : (p + 1) * 128].astype(F32)
        high = prod.astype(BF)
        highs.append(high)
        lows.append((prod - high.astype(F32)).astype(BF))
    score = lax.dot_general(sel, jnp.concatenate(highs, axis=1), NT, preferred_element_type=F32)
    score = score + lax.dot_general(
        sel, jnp.concatenate(lows, axis=1), NT, preferred_element_type=F32
    )
    score = score * (1.0 / HD**0.5)
    weights, parts = [], []
    for h in range(2):
        part = score[h * 8 : (h + 1) * 8]
        top = jnp.max(part, axis=0, keepdims=True)
        expo = jnp.exp(part - top)
        norm = jnp.sum(expo, axis=0, keepdims=True)
        weights.append(expo / norm)
        lse = top + jnp.log(norm)
        for _ in range(3):
            piece = lse.astype(BF).astype(F32)
            parts.append(piece)
            lse = lse - piece
    weight = jnp.concatenate(weights, axis=0).astype(BF)
    wide = lax.dot_general(weight, sel, TN, preferred_element_type=F32)
    ctx = wide[:, :128] * kv_ref[:, ROWS : ROWS + 128].astype(F32)
    for p in range(1, 8):
        ctx = ctx + wide[:, p * 128 : (p + 1) * 128] * kv_ref[
            :, ROWS + p * 128 : ROWS + (p + 1) * 128
        ].astype(F32)
    ctx = ctx.astype(BF)
    tail = jnp.concatenate(parts + [jnp.zeros((10, n), F32)], axis=0)

    @pl.when(step < 2)
    def _():
        peers = pl.ds(step * 16, 16)
        out_ref[peers, :LOW, :] = ctx.reshape(16, LOW, 128)
        out_ref[peers, LOW:CAP, :] = jnp.zeros((16, REST, 128), BF)
        for k in range(16):
            piece = tail[:, k * LOW : (k + 1) * LOW]
            piece = jnp.concatenate([piece, jnp.zeros((16, 128 - LOW), F32)], axis=1)
            out_ref[pl.ds(step * 16 + k, 1), CAP:, :] = piece.astype(BF).reshape(1, 16, 128)

    @pl.when(step >= 2)
    def _():
        for k in range(8):
            peer = pl.ds(full_ref[(step - 2) * 8 + k, 0], 1)
            rows = ctx[k * REST : (k + 1) * REST].reshape(1, REST, 128)
            out_ref[peer, LOW:CAP, :] = rows
            piece = tail[:, k * REST : (k + 1) * REST]
            before, after = jnp.zeros((16, LOW), F32), jnp.zeros((16, 128 - CAP), F32)
            piece = jnp.concatenate([before, piece, after], axis=1).astype(BF)
            out_ref[peer, CAP:, :] = out_ref[peer, CAP:, :] + piece.reshape(1, 16, 128)


def merge_kernel(
    info_ref, full_ref, msg_ref, place_ref, v_ref, mine_ref, theirs_ref, ctx_ref
):
    rows = 256
    low = PEERS * LOW
    ctx_ref[:low, :] = msg_ref[:, :LOW, :].reshape(low, 128)
    for k in range(FULL):
        got = msg_ref[pl.ds(full_ref[k, 0], 1), LOW:CAP, :].reshape(REST, 128)
        ctx_ref[low + k * REST : low + (k + 1) * REST, :] = got
    outs = [r.at[pl.ds(n * rows, rows)] for r in (mine_ref, theirs_ref) for n in range(2)]
    parts = []
    for h in range(2):
        for j in range(3):
            parts.append(msg_ref[:, CAP + h * 3 + j, :].reshape(PEERS, 128))
    parts = jnp.concatenate(parts, axis=1)
    for i, out in enumerate(outs):
        block = (info_ref[1] if i < 2 else 1 - info_ref[1]) + 2 * (i % 2)
        at = pl.ds(pl.multiple_of(block * rows, rows), rows)
        known = place_ref[at, :]
        src, place = known[:, 0:1], known[:, 1:2]
        lane = iota((rows, 128), 1)
        lanes = lane.astype(F32)
        hot = (iota((rows, ROWS), 1).astype(F32) == known[:, 2:3]).astype(F32).astype(BF)
        ctx = jnp.dot(hot, ctx_ref[...], preferred_element_type=F32)
        from_src = (iota((rows, PEERS), 1).astype(F32) == src).astype(F32).astype(BF)
        lists = jnp.dot(from_src, parts, preferred_element_type=F32)
        cols = []
        for h in range(2):
            base = h * 384
            lse = lists[:, base : base + 128] + lists[:, base + 128 : base + 256]
            lse = lse + lists[:, base + 256 : base + 384]
            lse = jnp.where(lanes == place, lse, 0.0)
            cols.append(jnp.sum(lse, axis=1, keepdims=True))
        lse = jnp.where(lane < HD, cols[0], cols[1])
        own = jnp.where(lane < HD, known[:, 3:4], known[:, 4:5])
        top = jnp.maximum(lse, own)
        a = jnp.exp(lse - top)
        b = jnp.exp(own - top)
        out[...] = ((a * ctx + b * v_ref[at, :].astype(F32)) / (a + b)).astype(BF)


def project_kernel(info_ref, *refs):
    rows = jnp.concatenate([r[...] for r in refs[:4]], axis=1)
    weight = jnp.concatenate([r[...] for r in refs[4:8]], axis=0)
    refs[8][...] = jnp.dot(rows, weight, preferred_element_type=F32).astype(BF)


def ffn_kernel(
    info_ref, x0_ref, x1_ref, p_ref, r_ref, up_ref, down_ref, right_ref, left_ref, *refs
):
    same_ref, other_ref, ups, downs, hid, acc, sems = refs
    pairs = [(up_ref, ups.at[0]), (down_ref, downs.at[0])]
    for n, src in enumerate((right_ref, left_ref)):
        for k in range(4):
            block = pl.ds(k * 256, 256)
            pairs.append((src.at[pl.ds(0, 256), block], ups.at[1, block, pl.ds(n * 256, 256)]))
        pairs.append((src.at[pl.ds(256, 256)], downs.at[1, pl.ds(n * 256, 256)]))
    copies = [pltpu.make_async_copy(a, b, sems.at[i]) for i, (a, b) in enumerate(pairs)]
    for copy in copies:
        copy.start()
    normed = []
    for n, x_ref in enumerate((x0_ref, x1_ref)):
        at = pl.ds(n * 256, 256)
        attn = p_ref[at].astype(F32) + r_ref[at].astype(F32)
        hidden = (x_ref[...].astype(F32) + attn).astype(BF).astype(F32)
        scale = lax.rsqrt(jnp.mean(hidden * hidden, axis=-1, keepdims=True) + 1e-05)
        normed.append((hidden * scale).astype(BF))
        hid[at] = jnp.where(info_ref[0] // 2 == n, hidden, 0.0)
    for unit in range(2):
        for n in range(2):
            at = pl.ds(n * 256, 256)
            if n == 0:
                for copy in (copies[:1], copies[2:6] + copies[7:11])[unit]:
                    copy.wait()
            up = jnp.dot(normed[n], ups[unit], preferred_element_type=F32)
            act = jax.nn.gelu(up).astype(BF)
            if n == 0:
                for copy in (copies[1:2], [copies[6], copies[11]])[unit]:
                    copy.wait()
            down = jnp.dot(act, downs[unit], preferred_element_type=F32)
            if unit == 0:
                acc[at] = down
            else:
                acc[at] += down
    core = info_ref[2]
    for d in range(4):
        head = ((info_ref[0] + d) % 4) * 2
        at = pl.ds(pl.multiple_of((head + core) * 128, 128), 128)
        same_ref[d] = hid[:, at] + acc[:, at]
        at = pl.ds(pl.multiple_of((head + 1 - core) * 128, 128), 128)
        other_ref[d] = acc[:, at].astype(BF)


def final_kernel(same_ref, other_ref, o0, o1, o2, o3):
    for i, out in enumerate((o0, o1, o2, o3)):
        out[...] = (same_ref[i] + other_ref[i].astype(F32)).astype(BF)


def place_rows_kernel(info_ref, p0, p1, p2, p3, out_ref):
    for n in range(2):
        at = pl.ds(n * 256, 256)
        for parity, a, b in ((info_ref[1], p0, p2), (1 - info_ref[1], p1, p3)):
            to = pl.multiple_of((parity + 2 * n) * 256, 256)
            out_ref[pl.ds(to, 256), :] = (a[at].astype(F32) + b[at].astype(F32)).astype(BF)


def shift(x, axis, by, size):
    return lax.ppermute(x, axis, [(i, (i + by) % size) for i in range(size)])


def rms_rows(stream):
    return stream * lax.rsqrt(jnp.mean(stream * stream, axis=-1, keepdims=True) + 1e-05)


def body(stream_in, keys, values, counts, slots, w_qkv, w_out, w_up, w_down):
    vmem = pl.BlockSpec(memory_space=pltpu.VMEM)
    hbm = pl.BlockSpec(memory_space=pltpu.HBM)
    x = lax.axis_index("x")
    core = lax.axis_index("core")
    info = keep(jnp.stack([x, x % 2, core]).astype(jnp.int32), pltpu.HBM)

    send, par, my_full = call(
        plan_kernel,
        (
            pltpu.HBM((PEERS, 128), jnp.int32),
            pltpu.HBM((PEERS + FULL, 128), F32),
            pltpu.HBM((FULL, 128), jnp.int32),
        ),
        (4 * 10**8, 10**6),
    )(keep(counts.reshape(1, ROWS), pltpu.HBM), keep(slots.T, pltpu.HBM))
    for_right, for_left = call(
        pack_kernel,
        (pltpu.HBM((640, ROWS), BF), pltpu.HBM((640, ROWS), BF)),
        (0, 5 * 10**6),
        in_specs=[hbm, hbm, hbm],
        out_specs=(hbm, hbm),
        scratch_shapes=[pltpu.VMEM((2, 640, ROWS), BF), pltpu.SemaphoreType.DMA((14,))],
    )(*(keep(w, pltpu.HBM) for w in (w_up, w_down, w_out)))
    left = shift(for_right, "x", 1, 4)
    right = shift(for_left, "x", 3, 4)
    wo_two = shift(w_out, "x", 2, 4)
    recv = lax.all_to_all(
        send.reshape(PEERS, 1, 128), SAMPLE, split_axis=0, concat_axis=0, tiled=True
    ).reshape(PEERS, 128)

    stream = stream_in.astype(F32)
    normed = rms_rows(stream).astype(BF)
    projected = jnp.einsum("rd,tdc->trc", normed, w_qkv, preferred_element_type=F32).astype(BF)
    query, own_key, own_value = projected[0], projected[1], projected[2]
    new_kv = jnp.stack([own_key, own_value], axis=1)

    flat_keys, flat_values = keys.reshape(ROWS, ROWS), values.reshape(ROWS, ROWS)
    kv = call(
        expand_kernel,
        pltpu.HBM((ROWS, 2 * ROWS), BF),
        (2 * ROWS * ROWS * ROWS * 2, 12 * 10**6),
        grid=(4,),
        in_specs=[
            pl.BlockSpec((PEERS + FULL, 128), lambda i: (0, 0)),
            pl.BlockSpec((ROWS, ROWS), lambda i: (0, 0)),
            pl.BlockSpec((ROWS, ROWS), lambda i: (0, 0)),
        ],
        out_specs=pl.BlockSpec((256, 2 * ROWS), lambda i: (i, 0)),
        scratch_shapes=[pltpu.VMEM((256, 128), F32)],
    )(keep(par, pltpu.HBM), flat_keys, flat_values)

    q_send = call(
        query_kernel,
        pltpu.HBM((ITEMS, 128), BF),
        (2 * ITEMS * ROWS * 128, 10**6),
        grid=(4,),
        in_specs=[
            pl.BlockSpec((8, 128), lambda i: (i, 0)),
            pl.BlockSpec((ROWS, 128), lambda i: (0, 0)),
        ],
        out_specs=pl.BlockSpec((8 * CAP, 128), lambda i: (i, 0)),
    )(recv, query)
    q_recv = lax.all_to_all(q_send, SAMPLE, split_axis=0, concat_axis=0, tiled=True)

    smem = pl.BlockSpec(memory_space=pltpu.SMEM)
    places, your_full = call(
        place_kernel,
        (pltpu.HBM((ROWS, 128), F32), pltpu.HBM((FULL, 128), jnp.int32)),
        (10**9, 2 * 10**6),
    )(recv, keep(query, pltpu.HBM), keep(own_key, pltpu.HBM))

    msg = call(
        attend_kernel,
        pltpu.HBM((PEERS, MSG, 128), BF),
        (2 * ROWS * ROWS * 128, 8 * 10**6),
        grid=(4,),
        in_specs=[
            smem,
            pl.BlockSpec((PEERS, CAP, 128), lambda i: (0, 0, 0)),
            pl.BlockSpec((256, 2 * ROWS), lambda i: (i, 0)),
        ],
        out_specs=pl.BlockSpec((PEERS, MSG, 128), lambda i: (0, 0, 0)),
        scratch_shapes=[pltpu.VMEM((256, 128), BF)],
    )(keep(my_full, pltpu.HBM), q_recv.reshape(PEERS, CAP, 128), keep(kv, pltpu.HBM))
    answer = lax.all_to_all(msg, SAMPLE, split_axis=0, concat_axis=0, tiled=True)
    fixed = lambda *shape: pl.BlockSpec(shape, lambda i, h: (0,) * len(shape))
    block = lambda n: pl.BlockSpec((256, ROWS), lambda i, h: (h[1] + 2 * n, 0))
    pair = sds((512, 128), BF)
    mine, theirs = call(
        merge_kernel,
        (pair, pair),
        (2 * ITEMS * ROWS * 128, 5 * 10**6),
        in_specs=[smem, smem] + [vmem] * 3,
        out_specs=(vmem, vmem),
        scratch_shapes=[pltpu.VMEM((ROWS, 128), BF)],
    )(info, *(keep(a, pltpu.HBM) for a in (your_full, answer, places, own_value)))

    from_left = shift(theirs, "x", 1, 4)
    from_right = shift(theirs, "x", 3, 4)
    from_two = shift(mine, "x", 2, 4)
    last = lambda at: pl.BlockSpec((128, ROWS), lambda i, h: (at, 0))
    partial = call(
        project_kernel,
        sds((512, ROWS), BF),
        (6 * 10**8, 3 * 10**6),
        grid_spec=pltpu.PrefetchScalarGridSpec(
            num_scalar_prefetch=1,
            grid=(1,),
            in_specs=[fixed(512, 128)] * 4 + [last(0), last(4), last(4), last(0)],
            out_specs=fixed(512, ROWS),
        ),
    )(info, mine, from_left, from_right, from_two, w_out, left, right, wo_two)
    partner = shift(partial, "core", 1, 2)

    same, other = call(
        ffn_kernel,
        (sds((4, 512, 128), F32), sds((4, 512, 128), BF)),
        (2 * 10**9, 10 * 10**6),
        grid_spec=pltpu.PrefetchScalarGridSpec(
            num_scalar_prefetch=1,
            grid=(1,),
            in_specs=[block(0), block(1), fixed(512, ROWS), fixed(512, ROWS)] + [hbm] * 4,
            out_specs=(fixed(4, 512, 128), fixed(4, 512, 128)),
            scratch_shapes=[
                pltpu.VMEM((2, ROWS, 512), BF),
                pltpu.VMEM((2, 512, ROWS), BF),
                pltpu.VMEM((512, ROWS), F32),
                pltpu.VMEM((512, ROWS), F32),
                pltpu.SemaphoreType.DMA((12,)),
            ],
        ),
    )(
        info,
        stream_in,
        stream_in,
        partial,
        partner,
        *(keep(w, pltpu.HBM) for w in (w_up, w_down, right, left)),
    )

    swapped = shift(other, "core", 1, 2)
    done = call(final_kernel, (pair,) * 4, (10**6, 10**6))(same, swapped)
    parts = [done[0]] + [shift(done[d], "x", d, 4) for d in (1, 2, 3)]
    layer_out = call(
        place_rows_kernel,
        sds((ROWS, 128), BF),
        (10**6, 5 * 10**5),
        in_specs=[smem] + [vmem] * 4,
        out_specs=vmem,
    )(info, *parts)
    return (layer_out, new_kv)


def solution(mesh):
    grid = Mesh(mesh.devices.reshape(8, 4, 4, 2), ("z", "y", "x", "core"))
    in_specs = (
        P(SAMPLE, None),
        P(SAMPLE, None, HEAD),
        P(SAMPLE, None, HEAD),
        P(SAMPLE),
        P(SAMPLE, None),
        P(None, None, HEAD),
        P(HEAD, None),
        P(None, HEAD),
        P(HEAD, None),
    )
    out_specs = (P(SAMPLE, HEAD), P(SAMPLE, None, HEAD))
    return jax.shard_map(body, mesh=grid, in_specs=in_specs, out_specs=out_specs, check_vma=False)
```

```python
import functools

import jax
import jax.numpy as jnp
from jax import lax
from jax.experimental import pallas as pl
from jax.experimental.pallas import tpu as pltpu
from jax.sharding import Mesh, PartitionSpec as P

HD = 64
PEERS = 32
CAP = 48
ROWS = 1024
ITEMS = PEERS * CAP
MSG = 64
LOW = 16
FULL = PEERS // 2
REST = CAP - LOW
SAMPLE = ("z", "y")
HEAD = ("x", "core")
F32 = jnp.float32
BF = jnp.bfloat16
NT = (((1,), (1,)), ((), ()))
TN = (((0,), (0,)), ((), ()))


def iota(shape, dim):
    return lax.broadcasted_iota(jnp.int32, shape, dim)


def call(kernel, out, cost, vmem=24, **kw):
    return pl.pallas_call(
        kernel,
        out_shape=out,
        compiler_params=pltpu.CompilerParams(vmem_limit_bytes=vmem * 2**20),
        cost_estimate=pl.CostEstimate(flops=cost[0], bytes_accessed=cost[1], transcendentals=0),
        **kw,
    )


def keep(x, space=pltpu.VMEM):
    return pltpu.with_memory_space_constraint(x, space)


def sds(shape, dtype):
    return jax.ShapeDtypeStruct(shape, dtype)


def full_peers(last):
    rows, cols = iota((PEERS, PEERS), 0), iota((PEERS, PEERS), 1)
    order = jnp.sum(jnp.where(rows < cols, last, 0.0), axis=0, keepdims=True)
    flag = jnp.sum(jnp.where(rows == cols, last, 0.0), axis=0, keepdims=True)
    hit = iota((FULL, PEERS), 0).astype(F32) == order
    return jnp.where(hit, flag, 0.0).astype(BF)


def peer_numbers(chosen):
    numbers = iota((PEERS, 128), 0).astype(F32).astype(BF)
    return jnp.dot(chosen, numbers, preferred_element_type=F32).astype(jnp.int32)


def plan_kernel(cnt_ref, slot_ref, send_ref, par_ref, full_ref):
    width = 256
    blocks = ROWS // width
    cnt = cnt_ref[...]
    tri = (iota((width, width), 0) <= iota((width, width), 1)).astype(F32).astype(BF)
    ow = iota((PEERS, width), 0)
    groups = []
    for k in range(4):
        for b in range(blocks):
            sl = slot_ref[k : k + 1, b * width : (b + 1) * width]
            live = cnt[:, b * width : (b + 1) * width] > k
            owner = jnp.where(live, sl // ROWS, -1)
            member = (ow == owner).astype(F32)
            groups.append((sl, live, member, b))
    stacked = jnp.concatenate([g[2].astype(BF) for g in groups], axis=0)
    inc = jnp.dot(stacked, tri, preferred_element_type=F32)
    base = jnp.zeros((PEERS, 1), F32)
    total = jnp.zeros((5 * PEERS, CAP), F32)
    parent = iota((1, width), 1)
    for g, (sl, live, member, b) in enumerate(groups):
        run = inc[g * PEERS : (g + 1) * PEERS]
        rank = jnp.sum(member * (run + (base - 1.0)), axis=0, keepdims=True)
        base = base + run[:, width - 1 : width]
        rank = jnp.where(live, rank.astype(jnp.int32), -1)
        place = (iota((CAP, width), 0) == rank).astype(F32).astype(BF)
        local = sl % ROWS
        par = parent + b * width
        left = jnp.concatenate(
            [
                member * (local // 32).astype(F32),
                member * (local % 32).astype(F32),
                member,
                member * (par // 32).astype(F32),
                member * (par % 32).astype(F32),
            ],
            axis=0,
        ).astype(BF)
        total = total + lax.dot_general(left, place, NT, preferred_element_type=F32)
    whole = total.astype(jnp.int32)
    have = whole[2 * PEERS : 3 * PEERS] > 0
    send = jnp.where(have, whole[:PEERS] * 32 + whole[PEERS : 2 * PEERS], -1)
    fill = jnp.full((PEERS, 128 - CAP), -1, jnp.int32)
    send_ref[...] = jnp.concatenate([send, fill], axis=1)
    chosen = full_peers(jnp.where(have[:, CAP - 1 :], 1.0, 0.0))
    full_ref[...] = peer_numbers(chosen)
    high, low = total[3 * PEERS : 4 * PEERS], total[4 * PEERS :]
    rest = 32.0 * jnp.dot(chosen, high.astype(BF), preferred_element_type=F32)
    rest = rest + jnp.dot(chosen, low.astype(BF), preferred_element_type=F32)
    par_ref[:PEERS, :LOW] = high[:, :LOW] * 32.0 + low[:, :LOW]
    par_ref[:PEERS, LOW:] = jnp.zeros((PEERS, 128 - LOW), F32)
    par_ref[PEERS:, :REST] = rest[:, LOW:]
    par_ref[PEERS:, REST:] = jnp.zeros((FULL, 128 - REST), F32)


def pack_kernel(up_ref, down_ref, wo_ref, right_ref, left_ref, stage, sems):
    writes = []
    for n in range(2):
        half = pl.ds(n * 256, 256)
        pairs = [(down_ref.at[half], stage.at[n, pl.ds(256, 256)])]
        pairs.append((wo_ref, stage.at[n, pl.ds(512, 128)]))
        for k in range(4):
            block = pl.ds(k * 256, 256)
            pairs.append((up_ref.at[block, half], stage.at[n, pl.ds(0, 256), block]))
        copies = [
            pltpu.make_async_copy(a, b, sems.at[n * 7 + i]) for i, (a, b) in enumerate(pairs)
        ]
        for copy in copies:
            copy.start()
        writes.append((copies, (right_ref, left_ref)[n]))
    ends = []
    for n, (copies, target) in enumerate(writes):
        for copy in copies:
            copy.wait()
        end = pltpu.make_async_copy(stage.at[n], target, sems.at[n * 7 + 6])
        end.start()
        ends.append(end)
    for end in ends:
        end.wait()


def column(lists, count, depth):
    shape = (count, depth, 128)
    picked = jnp.where(
        iota(shape, 1) == iota(shape, 2), jnp.broadcast_to(lists[:, None, :], shape), 0.0
    )
    return jnp.sum(picked, axis=2, keepdims=True).reshape(count * depth, 1)


def expand_kernel(par_ref, k_ref, v_ref, out_ref, col_ref):
    step = pl.program_id(0)

    @pl.when(step < 2)
    def _():
        lists = par_ref[pl.ds(pl.multiple_of(step * 16, 16), 16), :]
        col_ref[...] = jnp.broadcast_to(column(lists, 16, LOW), (256, 128))

    @pl.when(step >= 2)
    def _():
        lists = par_ref[pl.ds(pl.multiple_of(PEERS + (step - 2) * 8, 8), 8), :]
        col_ref[...] = jnp.broadcast_to(column(lists, 8, REST), (256, 128))

    hot = (col_ref[:, 0:1] == iota((256, ROWS), 1).astype(F32)).astype(F32).astype(BF)
    out_ref[:, :ROWS] = jnp.dot(hot, k_ref[...], preferred_element_type=F32).astype(BF)
    out_ref[:, ROWS:] = jnp.dot(hot, v_ref[...], preferred_element_type=F32).astype(BF)


def query_kernel(recv_ref, q_ref, out_ref, stage, sems):
    lists = recv_ref[...].astype(F32)
    slots = iota((8 * CAP, ROWS), 1).astype(F32)
    copies = []
    for n in range(4):
        at = pl.ds(n * 8 * CAP, 8 * CAP)
        col = column(lists[n * 8 : n * 8 + 8], 8, CAP)
        hot = (col == slots).astype(F32).astype(BF)
        stage[at] = jnp.dot(hot, q_ref[...], preferred_element_type=F32).astype(BF)
        copy = pltpu.make_async_copy(stage.at[at], out_ref.at[at], sems.at[n])
        copy.start()
        copies.append(copy)
    for copy in copies:
        copy.wait()


def place_kernel(recv_ref, q_ref, k_ref, out_ref, full_ref):
    slot = recv_ref[...]
    last = jnp.where(slot[:, CAP - 1 : CAP] >= 0, 1.0, 0.0)
    full_ref[...] = peer_numbers(full_peers(last))
    below = iota((PEERS, PEERS), 1) < iota((PEERS, PEERS), 0)
    order = jnp.dot(
        below.astype(F32).astype(BF),
        jnp.broadcast_to(last, (PEERS, 128)).astype(BF),
        preferred_element_type=F32,
    )
    high = jnp.where(slot >= 0, slot // 32, -1)
    low = slot % 32
    acc = jnp.zeros((96, 32), F32)
    where_c = iota((32, 128), 1).astype(F32)
    for s in range(PEERS):
        a = (iota((32, 128), 0) == high[s : s + 1, :]).astype(F32)
        b = (iota((32, 128), 0) == low[s : s + 1, :]).astype(F32).astype(BF)
        left = jnp.concatenate([a * float(s), a * where_c, a * order[s : s + 1]], axis=0)
        acc = acc + lax.dot_general(left.astype(BF), b, NT, preferred_element_type=F32)
    wide = jnp.concatenate([acc, jnp.zeros((96, 96), F32)], axis=1)
    src, place, rank = (column(wide[n * 32 : n * 32 + 32], 32, 32) for n in range(3))
    rest = float(PEERS * LOW - LOW) + rank * float(REST) + place
    pos = jnp.where(place < float(LOW), src * float(LOW) + place, rest)
    prod = q_ref[...].astype(F32) * k_ref[...].astype(F32) * (1.0 / HD**0.5)
    s0 = jnp.sum(prod[:, :HD], axis=1, keepdims=True)
    s1 = jnp.sum(prod[:, HD:], axis=1, keepdims=True)
    high = jnp.floor(pos * (1.0 / 32.0))
    pieces = [high, pos - high * 32.0, place, src]
    for value in (s0, s1):
        for _ in range(3):
            piece = value.astype(BF).astype(F32)
            pieces.append(piece)
            value = value - piece
    lane = iota((ROWS, 128), 1)
    known = jnp.zeros((ROWS, 128), F32)
    for n, piece in enumerate(pieces):
        known = jnp.where(lane == n, piece, known)
    out_ref[...] = known.astype(BF)


def attend_kernel(full_hbm, q_ref, kv_ref, out_ref, kv, rows_ref, stage, full_ref, sems):
    n = 256
    listing = pltpu.make_async_copy(full_hbm, full_ref, sems.at[9])
    listing.start()
    copies = []
    for part in range(2):
        for i in range(4):
            src = kv_ref.at[pl.ds(i * n, n), pl.ds(part * ROWS, ROWS)]
            dst = kv.at[i, :, pl.ds(part * ROWS, ROWS)]
            copies.append(pltpu.make_async_copy(src, dst, sems.at[part * 4 + i]))
    for copy in copies:
        copy.start()
    split = PEERS * LOW
    rows_ref[:split, :] = q_ref[:, :LOW, :].reshape(split, 128)
    listing.wait()
    peers = [pl.ds(full_ref[k, 0], 1) for k in range(FULL)]
    for k, peer in enumerate(peers):
        at = split + k * REST
        rows_ref[at : at + REST, :] = q_ref[peer, LOW:, :].reshape(REST, 128)
    sel_p = iota((16, ROWS), 1) // 128
    sel_h = (iota((16, ROWS), 1) % 128) // HD
    sel = (iota((16, ROWS), 0) == sel_h * 8 + sel_p).astype(F32).astype(BF)
    sum_p = iota((ROWS, 128), 0) // 128
    sum_h = (iota((ROWS, 128), 0) % 128) // HD
    sums = (iota((ROWS, 128), 1) == sum_h * 8 + sum_p).astype(F32).astype(BF)
    scores = []
    for i in range(4):
        q = rows_ref[i * n : (i + 1) * n, :].astype(F32)
        copies[i].wait()
        score = jnp.zeros((n, 128), F32)
        for p in range(0, 8, 2):
            highs, lows = [], []
            for t in (p, p + 1):
                prod = q * kv[i, :, t * 128 : (t + 1) * 128].astype(F32)
                high = prod.astype(BF)
                highs.append(high)
                lows.append((prod - high.astype(F32)).astype(BF))
            part = sums[p * 128 : (p + 2) * 128]
            highs, lows = jnp.concatenate(highs, axis=1), jnp.concatenate(lows, axis=1)
            score = score + jnp.dot(highs, part, preferred_element_type=F32)
            score = score + jnp.dot(lows, part, preferred_element_type=F32)
        scores.append(score.T[:16])
    score = jnp.concatenate(scores, axis=1) * (1.0 / HD**0.5)
    weights, parts = [], []
    for h in range(2):
        part = score[h * 8 : (h + 1) * 8]
        top = jnp.max(part, axis=0, keepdims=True)
        expo = jnp.exp(part - top)
        norm = jnp.sum(expo, axis=0, keepdims=True)
        weights.append(expo / norm)
        lse = top + jnp.log(norm)
        for _ in range(3):
            piece = lse.astype(BF).astype(F32)
            parts.append(piece)
            lse = lse - piece
    weight = jnp.concatenate(weights, axis=0).astype(BF)
    tail = jnp.concatenate(parts + [jnp.zeros((10, ROWS), F32)], axis=0)
    stage[:, LOW:CAP, :] = jnp.zeros((PEERS, REST, 128), BF)
    for k in range(PEERS):
        piece = tail[:, k * LOW : (k + 1) * LOW]
        piece = jnp.concatenate([piece, jnp.zeros((16, 128 - LOW), F32)], axis=1)
        stage[k, CAP:, :] = piece.astype(BF)
    for i in range(4):
        wide = lax.dot_general(
            weight[:, i * n : (i + 1) * n], sel, TN, preferred_element_type=F32
        )
        copies[4 + i].wait()
        ctx = jnp.zeros((n, 128), F32)
        for p in range(8):
            value = kv[i, :, ROWS + p * 128 : ROWS + (p + 1) * 128].astype(F32)
            ctx = ctx + wide[:, p * 128 : (p + 1) * 128] * value
        ctx = ctx.astype(BF)
        if i < 2:
            stage[i * 16 : (i + 1) * 16, :LOW, :] = ctx.reshape(16, LOW, 128)
        else:
            for k in range(8):
                peer = peers[(i - 2) * 8 + k]
                stage[peer, LOW:CAP, :] = ctx[k * REST : (k + 1) * REST].reshape(1, REST, 128)
    for k, peer in enumerate(peers):
        at = split + k * REST
        before, after = jnp.zeros((16, LOW), F32), jnp.zeros((16, 128 - CAP), F32)
        piece = jnp.concatenate([before, tail[:, at : at + REST], after], axis=1).astype(BF)
        stage[peer, CAP:, :] = stage[peer, CAP:, :] + piece.reshape(1, 16, 128)
    end = pltpu.make_async_copy(stage, out_ref, sems.at[8])
    end.start()
    end.wait()


def merge_kernel(
    full_hbm, msg_hbm, place_hbm, v_hbm, mine_ref, theirs_ref, msg_ref, place_ref, v_ref, ctx_ref,
    full_ref, sems
):
    rows = 256
    outs = [r.at[pl.ds(n * rows, rows)] for r in (mine_ref, theirs_ref) for n in range(2)]
    pairs = [(full_hbm, full_ref), (msg_hbm, msg_ref), (place_hbm, place_ref), (v_hbm, v_ref)]
    fetch = [pltpu.make_async_copy(a, b, sems.at[i]) for i, (a, b) in enumerate(pairs)]
    for copy in fetch:
        copy.start()
    piece, lane = iota((128, 512), 0), iota((128, 512), 1)
    use = jnp.where(lane < 128, jnp.where(piece == 0, 32.0, jnp.where(piece == 1, 1.0, 0.0)), 0.0)
    use = use + jnp.where((lane // 128 == 1) & (piece == 2), 1.0, 0.0)
    use = use + jnp.where((lane // 128 == 2) & (piece == 3), 1.0, 0.0)
    scores = (lane >= 384) & (piece >= 4) & (piece < 10)
    head = (lane - 384) // HD
    use = use + jnp.where(scores & ((piece - 4) // 3 == head), 1.0, 0.0)
    use = use.astype(BF)
    lanes = iota((rows, 128), 1).astype(F32)
    entry = iota((rows, PEERS * 16), 1)
    of_source = (entry // 16).astype(F32)
    of_head = entry % 16 // 3
    for copy in fetch:
        copy.wait()
    low = PEERS * LOW
    ctx_ref[:low, :] = msg_ref[:, :LOW, :].reshape(low, 128)
    for k in range(FULL):
        got = msg_ref[pl.ds(full_ref[k, 0], 1), LOW:CAP, :].reshape(REST, 128)
        ctx_ref[low + k * REST : low + (k + 1) * REST, :] = got
    parts = msg_ref[:, CAP:, :].reshape(PEERS * 16, 128)
    parity = lax.axis_index("x") % 2
    for i, out in enumerate(outs):
        block = (parity if i < 2 else 1 - parity) + 2 * (i % 2)
        at = pl.ds(pl.multiple_of(block * rows, rows), rows)
        known = jnp.dot(place_ref[at, :], use, preferred_element_type=F32)
        pos, own = known[:, :128], known[:, 384:]
        hot = [(lanes + float(t * 128) == pos).astype(F32).astype(BF) for t in range(8)]
        hot = jnp.concatenate(hot, axis=1)
        ctx = jnp.dot(hot, ctx_ref[...], preferred_element_type=F32)
        hit = of_source == jnp.concatenate([known[:, 256:384]] * 4, axis=1)
        here = lanes == known[:, 128:256]
        cols = []
        for h in range(2):
            pick = jnp.where(hit & (of_head == h), 1.0, 0.0).astype(BF)
            lists = jnp.dot(pick, parts, preferred_element_type=F32)
            cols.append(jnp.sum(jnp.where(here, lists, 0.0), axis=1, keepdims=True))
        lse = jnp.where(lanes < HD, cols[0], cols[1])
        top = jnp.maximum(lse, own)
        a = jnp.exp(lse - top)
        b = jnp.exp(own - top)
        out[...] = ((a * ctx + b * v_ref[at, :].astype(F32)) / (a + b)).astype(BF)


def project_kernel(a0, a1, a2, a3, own_ref, two_ref, left_ref, right_ref, out_ref, near, sems):
    copies = [
        pltpu.make_async_copy(r.at[pl.ds(512, 128)], near.at[pl.ds(n * 128, 128)], sems.at[n])
        for n, r in enumerate((left_ref, right_ref))
    ]
    for copy in copies:
        copy.start()
    rows = jnp.concatenate([a0[...], a3[...]], axis=1)
    weight = jnp.concatenate([own_ref[...], two_ref[...]], axis=0)
    total = jnp.dot(rows, weight, preferred_element_type=F32)
    rows = jnp.concatenate([a1[...], a2[...]], axis=1)
    for copy in copies:
        copy.wait()
    total = total + jnp.dot(rows, near[...], preferred_element_type=F32)
    out_ref[...] = total.astype(BF)


def ffn_kernel(
    x_ref, p_ref, r_ref, up_ref, down_ref, right_ref, left_ref, same_ref, other_ref, ups, downs,
    hid, acc, sems
):
    pairs = []
    for n, src in enumerate((right_ref, left_ref)):
        for k in range(4):
            block = pl.ds(k * 256, 256)
            pairs.append((src.at[pl.ds(0, 256), block], ups.at[block, pl.ds(n * 256, 256)]))
    for n, src in enumerate((right_ref, left_ref)):
        pairs.append((src.at[pl.ds(256, 256)], downs.at[pl.ds(n * 256, 256)]))
    copies = [pltpu.make_async_copy(a, b, sems.at[i]) for i, (a, b) in enumerate(pairs)]
    for copy in copies:
        copy.start()
    x = lax.axis_index("x")
    core = lax.axis_index("core")
    normed = []
    for n in range(2):
        at = pl.ds(n * 256, 256)
        attn = p_ref[at].astype(F32) + r_ref[at].astype(F32)
        rows = pl.ds(pl.multiple_of((x % 2 + 2 * n) * 256, 256), 256)
        hidden = (x_ref[rows, :].astype(F32) + attn).astype(BF).astype(F32)
        scale = lax.rsqrt(jnp.mean(hidden * hidden, axis=-1, keepdims=True) + 1e-05)
        normed.append((hidden * scale).astype(BF))
        hid[at] = jnp.where(x // 2 == n, hidden, 0.0)
    normed = jnp.concatenate(normed, axis=0)
    act = jax.nn.gelu(jnp.dot(normed, up_ref[...], preferred_element_type=F32)).astype(BF)
    total = jnp.dot(act, down_ref[...], preferred_element_type=F32)
    for copy in copies[:8]:
        copy.wait()
    act = jax.nn.gelu(jnp.dot(normed, ups[...], preferred_element_type=F32)).astype(BF)
    for copy in copies[8:]:
        copy.wait()
    acc[...] = total + jnp.dot(act, downs[...], preferred_element_type=F32)
    for d in range(4):
        head = ((x + d) % 4) * 2
        at = pl.ds(pl.multiple_of((head + core) * 128, 128), 128)
        same_ref[d] = hid[:, at] + acc[:, at]
        at = pl.ds(pl.multiple_of((head + 1 - core) * 128, 128), 128)
        other_ref[d] = acc[:, at].astype(BF)


def final_kernel(same_ref, other_ref, o0, o1, o2, o3):
    for i, out in enumerate((o0, o1, o2, o3)):
        out[...] = (same_ref[i] + other_ref[i].astype(F32)).astype(BF)


def place_rows_kernel(p0, p1, p2, p3, out_ref):
    mine = lax.axis_index("x") % 2
    for n in range(2):
        at = pl.ds(n * 256, 256)
        for parity, a, b in ((mine, p0, p2), (1 - mine, p1, p3)):
            to = pl.multiple_of((parity + 2 * n) * 256, 256)
            out_ref[pl.ds(to, 256), :] = (a[at].astype(F32) + b[at].astype(F32)).astype(BF)


def shift(x, axis, by, size):
    return lax.ppermute(x, axis, [(i, (i + by) % size) for i in range(size)])


def rms_rows(stream):
    return stream * lax.rsqrt(jnp.mean(stream * stream, axis=-1, keepdims=True) + 1e-05)


def body(stream_in, keys, values, counts, slots, w_qkv, w_out, w_up, w_down):
    vmem = pl.BlockSpec(memory_space=pltpu.VMEM)
    hbm = pl.BlockSpec(memory_space=pltpu.HBM)
    send, par, my_full = call(
        plan_kernel,
        (
            pltpu.HBM((PEERS, 128), jnp.int32),
            pltpu.HBM((PEERS + FULL, 128), F32),
            pltpu.HBM((FULL, 128), jnp.int32),
        ),
        (4 * 10**8, 10**6),
    )(keep(counts.reshape(1, ROWS), pltpu.HBM), keep(slots.T, pltpu.HBM))
    for_right, for_left = call(
        pack_kernel,
        (pltpu.HBM((640, ROWS), BF), pltpu.HBM((640, ROWS), BF)),
        (0, 5 * 10**6),
        in_specs=[hbm, hbm, hbm],
        out_specs=(hbm, hbm),
        scratch_shapes=[pltpu.VMEM((2, 640, ROWS), BF), pltpu.SemaphoreType.DMA((14,))],
    )(*(keep(w, pltpu.HBM) for w in (w_up, w_down, w_out)))
    left = shift(for_right, "x", 1, 4)
    right = shift(for_left, "x", 3, 4)
    wo_two = shift(w_out, "x", 2, 4)
    recv = lax.all_to_all(
        send.reshape(PEERS, 1, 128), SAMPLE, split_axis=0, concat_axis=0, tiled=True
    ).reshape(PEERS, 128)

    stream = stream_in.astype(F32)
    normed = rms_rows(stream).astype(BF)
    projected = jnp.einsum("rd,tdc->trc", normed, w_qkv, preferred_element_type=F32).astype(BF)
    query, own_key, own_value = projected[0], projected[1], projected[2]
    new_kv = jnp.stack([own_key, own_value], axis=1)

    flat_keys, flat_values = keys.reshape(ROWS, ROWS), values.reshape(ROWS, ROWS)
    kv = call(
        expand_kernel,
        pltpu.HBM((ROWS, 2 * ROWS), BF),
        (2 * ROWS * ROWS * ROWS * 2, 12 * 10**6),
        grid=(4,),
        in_specs=[
            pl.BlockSpec((PEERS + FULL, 128), lambda i: (0, 0)),
            pl.BlockSpec((ROWS, ROWS), lambda i: (0, 0)),
            pl.BlockSpec((ROWS, ROWS), lambda i: (0, 0)),
        ],
        out_specs=pl.BlockSpec((256, 2 * ROWS), lambda i: (i, 0)),
        scratch_shapes=[pltpu.VMEM((256, 128), F32)],
    )(keep(par, pltpu.HBM), flat_keys, flat_values)

    q_send = call(
        query_kernel,
        pltpu.HBM((ITEMS, 128), BF),
        (2 * ITEMS * ROWS * 128, 10**6),
        in_specs=[vmem, vmem],
        out_specs=hbm,
        scratch_shapes=[pltpu.VMEM((ITEMS, 128), BF), pltpu.SemaphoreType.DMA((4,))],
    )(recv, query)
    q_recv = lax.all_to_all(q_send, SAMPLE, split_axis=0, concat_axis=0, tiled=True)

    places, your_full = call(
        place_kernel,
        (pltpu.HBM((ROWS, 128), BF), pltpu.HBM((FULL, 128), jnp.int32)),
        (10**9, 2 * 10**6),
    )(recv, keep(query, pltpu.HBM), keep(own_key, pltpu.HBM))

    msg = call(
        attend_kernel,
        pltpu.HBM((PEERS, MSG, 128), BF),
        (2 * ROWS * ROWS * 128, 8 * 10**6),
        in_specs=[hbm, vmem, hbm],
        out_specs=hbm,
        scratch_shapes=[
            pltpu.VMEM((4, 256, 2 * ROWS), BF),
            pltpu.VMEM((ROWS, 128), BF),
            pltpu.VMEM((PEERS, MSG, 128), BF),
            pltpu.SMEM((FULL, 128), jnp.int32),
            pltpu.SemaphoreType.DMA((10,)),
        ],
    )(keep(my_full, pltpu.HBM), q_recv.reshape(PEERS, CAP, 128), keep(kv, pltpu.HBM))
    answer = lax.all_to_all(msg, SAMPLE, split_axis=0, concat_axis=0, tiled=True)
    pair = sds((512, 128), BF)
    mine, theirs = call(
        merge_kernel,
        (pair, pair),
        (2 * ITEMS * ROWS * 128, 5 * 10**6),
        in_specs=[hbm] * 4,
        out_specs=(vmem, vmem),
        scratch_shapes=[
            pltpu.VMEM((PEERS, MSG, 128), BF),
            pltpu.VMEM((ROWS, 128), BF),
            pltpu.VMEM((ROWS, 128), BF),
            pltpu.VMEM((ROWS, 128), BF),
            pltpu.SMEM((FULL, 128), jnp.int32),
            pltpu.SemaphoreType.DMA((4,)),
        ],
    )(*(keep(a, pltpu.HBM) for a in (your_full, answer, places, own_value)))

    from_left = shift(theirs, "x", 1, 4)
    from_right = shift(theirs, "x", 3, 4)
    from_two = shift(mine, "x", 2, 4)
    partial = call(
        project_kernel,
        sds((512, ROWS), BF),
        (6 * 10**8, 3 * 10**6),
        in_specs=[vmem] * 6 + [hbm] * 2,
        out_specs=vmem,
        scratch_shapes=[pltpu.VMEM((256, ROWS), BF), pltpu.SemaphoreType.DMA((2,))],
    )(
        mine,
        from_left,
        from_right,
        from_two,
        keep(w_out),
        keep(wo_two),
        keep(left, pltpu.HBM),
        keep(right, pltpu.HBM),
    )
    partner = shift(partial, "core", 1, 2)

    same, other = call(
        ffn_kernel,
        (sds((4, 512, 128), F32), sds((4, 512, 128), BF)),
        (2 * 10**9, 10 * 10**6),
        in_specs=[vmem] * 5 + [hbm] * 2,
        out_specs=(vmem, vmem),
        scratch_shapes=[
            pltpu.VMEM((ROWS, 512), BF),
            pltpu.VMEM((512, ROWS), BF),
            pltpu.VMEM((512, ROWS), F32),
            pltpu.VMEM((512, ROWS), F32),
            pltpu.SemaphoreType.DMA((10,)),
        ],
    )(
        stream_in,
        partial,
        partner,
        keep(w_up),
        keep(w_down),
        keep(right, pltpu.HBM),
        keep(left, pltpu.HBM),
    )

    swapped = shift(other, "core", 1, 2)
    done = call(final_kernel, (pair,) * 4, (10**6, 10**6))(same, swapped)
    parts = [done[0]] + [shift(done[d], "x", d, 4) for d in (1, 2, 3)]
    layer_out = call(
        place_rows_kernel,
        sds((ROWS, 128), BF),
        (10**6, 5 * 10**5),
        in_specs=[vmem] * 4,
        out_specs=vmem,
    )(*parts)
    return (layer_out, new_kv)


def solution(mesh):
    grid = Mesh(mesh.devices.reshape(8, 4, 4, 2), ("z", "y", "x", "core"))
    in_specs = (
        P(SAMPLE, None),
        P(SAMPLE, None, HEAD),
        P(SAMPLE, None, HEAD),
        P(SAMPLE),
        P(SAMPLE, None),
        P(None, None, HEAD),
        P(HEAD, None),
        P(None, HEAD),
        P(HEAD, None),
    )
    out_specs = (P(SAMPLE, HEAD), P(SAMPLE, None, HEAD))
    return jax.shard_map(body, mesh=grid, in_specs=in_specs, out_specs=out_specs, check_vma=False)
```

```python
import functools

import jax
import jax.numpy as jnp
from jax import lax
from jax.experimental import pallas as pl
from jax.experimental.pallas import tpu as pltpu
from jax.sharding import Mesh, PartitionSpec as P

HD = 64
PEERS = 32
CAP = 48
ROWS = 1024
ITEMS = PEERS * CAP
MSG = 64
LOW = 16
FULL = PEERS // 2
REST = CAP - LOW
SAMPLE = ("z", "y")
HEAD = ("x", "core")
F32 = jnp.float32
BF = jnp.bfloat16
NT = (((1,), (1,)), ((), ()))
TN = (((0,), (0,)), ((), ()))


def iota(shape, dim):
    return lax.broadcasted_iota(jnp.int32, shape, dim)


def call(kernel, out, cost, vmem=24, **kw):
    return pl.pallas_call(
        kernel,
        out_shape=out,
        compiler_params=pltpu.CompilerParams(vmem_limit_bytes=vmem * 2**20),
        cost_estimate=pl.CostEstimate(flops=cost[0], bytes_accessed=cost[1], transcendentals=0),
        **kw,
    )


def keep(x, space=pltpu.VMEM):
    return pltpu.with_memory_space_constraint(x, space)


def sds(shape, dtype):
    return jax.ShapeDtypeStruct(shape, dtype)


def full_peers(last):
    rows, cols = iota((PEERS, PEERS), 0), iota((PEERS, PEERS), 1)
    order = jnp.sum(jnp.where(rows < cols, last, 0.0), axis=0, keepdims=True)
    flag = jnp.sum(jnp.where(rows == cols, last, 0.0), axis=0, keepdims=True)
    hit = iota((FULL, PEERS), 0).astype(F32) == order
    return jnp.where(hit, flag, 0.0).astype(BF)


def peer_numbers(chosen):
    numbers = iota((PEERS, 128), 0).astype(F32).astype(BF)
    return jnp.dot(chosen, numbers, preferred_element_type=F32).astype(jnp.int32)


def plan_kernel(cnt_ref, slot_ref, send_ref, par_ref, full_ref):
    width = 256
    blocks = ROWS // width
    cnt = cnt_ref[...]
    tri = (iota((width, width), 0) <= iota((width, width), 1)).astype(F32).astype(BF)
    ow = iota((PEERS, width), 0)
    groups = []
    for k in range(4):
        for b in range(blocks):
            sl = slot_ref[k : k + 1, b * width : (b + 1) * width]
            live = cnt[:, b * width : (b + 1) * width] > k
            owner = jnp.where(live, sl // ROWS, -1)
            member = (ow == owner).astype(F32)
            groups.append((sl, live, member, b))
    stacked = jnp.concatenate([g[2].astype(BF) for g in groups], axis=0)
    inc = jnp.dot(stacked, tri, preferred_element_type=F32)
    base = jnp.zeros((PEERS, 1), F32)
    total = jnp.zeros((5 * PEERS, CAP), F32)
    parent = iota((1, width), 1)
    for g, (sl, live, member, b) in enumerate(groups):
        run = inc[g * PEERS : (g + 1) * PEERS]
        rank = jnp.sum(member * (run + (base - 1.0)), axis=0, keepdims=True)
        base = base + run[:, width - 1 : width]
        rank = jnp.where(live, rank.astype(jnp.int32), -1)
        place = (iota((CAP, width), 0) == rank).astype(F32).astype(BF)
        local = sl % ROWS
        par = parent + b * width
        left = jnp.concatenate(
            [
                member * (local // 32).astype(F32),
                member * (local % 32).astype(F32),
                member,
                member * (par // 32).astype(F32),
                member * (par % 32).astype(F32),
            ],
            axis=0,
        ).astype(BF)
        total = total + lax.dot_general(left, place, NT, preferred_element_type=F32)
    whole = total.astype(jnp.int32)
    have = whole[2 * PEERS : 3 * PEERS] > 0
    send = jnp.where(have, whole[:PEERS] * 32 + whole[PEERS : 2 * PEERS], -1)
    fill = jnp.full((PEERS, 128 - CAP), -1, jnp.int32)
    send_ref[...] = jnp.concatenate([send, fill], axis=1)
    chosen = full_peers(jnp.where(have[:, CAP - 1 :], 1.0, 0.0))
    full_ref[...] = peer_numbers(chosen)
    high, low = total[3 * PEERS : 4 * PEERS], total[4 * PEERS :]
    rest = 32.0 * jnp.dot(chosen, high.astype(BF), preferred_element_type=F32)
    rest = rest + jnp.dot(chosen, low.astype(BF), preferred_element_type=F32)
    par_ref[:PEERS, :LOW] = high[:, :LOW] * 32.0 + low[:, :LOW]
    par_ref[:PEERS, LOW:] = jnp.zeros((PEERS, 128 - LOW), F32)
    par_ref[PEERS:, :REST] = rest[:, LOW:]
    par_ref[PEERS:, REST:] = jnp.zeros((FULL, 128 - REST), F32)


def pack_kernel(up_ref, down_ref, wo_ref, right_ref, left_ref, stage, sems):
    loads, stores = [], []
    for n, out in enumerate((right_ref, left_ref)):
        half = pl.ds(n * 256, 256)
        pairs = [(up_ref.at[pl.ds(k * 256, 256), half], pl.ds(k * 256, 256)) for k in range(4)]
        pairs = [(a, stage.at[n, pl.ds(0, 256), b]) for a, b in pairs]
        pairs.append((down_ref.at[half], stage.at[n, pl.ds(256, 256)]))
        pairs.append((wo_ref, stage.at[n, pl.ds(512, 128)]))
        loads.append(
            [pltpu.make_async_copy(a, b, sems.at[n * 9 + i]) for i, (a, b) in enumerate(pairs)]
        )
        parts = [pl.ds(0, 256), pl.ds(256, 256), pl.ds(512, 128)]
        stores.append(
            [
                pltpu.make_async_copy(stage.at[n, p], out.at[p], sems.at[n * 9 + 6 + i])
                for i, p in enumerate(parts)
            ]
        )
    for copy in loads[0] + loads[1]:
        copy.start()
    for n in range(2):
        for i in range(3):
            for copy in (loads[n][:4], loads[n][4:5], loads[n][5:])[i]:
                copy.wait()
            stores[n][i].start()
    for copy in stores[0] + stores[1]:
        copy.wait()


def column(lists, count, depth):
    shape = (count, depth, 128)
    picked = jnp.where(
        iota(shape, 1) == iota(shape, 2), jnp.broadcast_to(lists[:, None, :], shape), 0.0
    )
    return jnp.sum(picked, axis=2, keepdims=True).reshape(count * depth, 1)


def expand_kernel(par_ref, k_hbm, v_hbm, out_ref, raw, flat, hot_ref, stage, sems):
    n = 256
    loads = [
        pltpu.make_async_copy(a, raw.at[t], sems.at[t]) for t, a in enumerate((k_hbm, v_hbm))
    ]
    for copy in loads:
        copy.start()
    low = column(par_ref[:PEERS, :], PEERS, LOW)
    rest = column(par_ref[PEERS:, :], FULL, REST)
    parents = iota((n, ROWS), 1).astype(F32)
    for i in range(4):
        col = low[i * n : (i + 1) * n] if i < 2 else rest[(i - 2) * n : (i - 1) * n]
        hot_ref[i] = (col == parents).astype(F32).astype(BF)
    copies = []

    def gather(t, i):
        got = jnp.dot(hot_ref[i], flat[t], preferred_element_type=F32)
        stage[t, i] = got.astype(BF)
        to = out_ref.at[pl.ds(i * n, n), pl.ds(t * ROWS, ROWS)]
        copies.append(pltpu.make_async_copy(stage.at[t, i], to, sems.at[2 + t * 4 + i]))
        copies[-1].start()

    loads[0].wait()
    flat[0] = raw[0].reshape(ROWS, ROWS)
    gather(0, 0)
    gather(0, 1)
    loads[1].wait()
    flat[1] = raw[1].reshape(ROWS, ROWS)
    gather(0, 2)
    gather(0, 3)
    for i in range(4):
        gather(1, i)
    for copy in copies:
        copy.wait()


def row_scales(x):
    x = x.astype(F32)
    return lax.rsqrt(jnp.mean(x * x, axis=-1, keepdims=True) + 1e-05)


def project_query_kernel(x_ref, w_ref, out_ref):
    for n in range(4):
        at = pl.ds(n * 256, 256)
        got = jnp.dot(x_ref[at], w_ref[0], preferred_element_type=F32)
        out_ref[at] = (got * row_scales(x_ref[at])).astype(BF)


def query_kernel(recv_ref, q_ref, after_ref, out_ref, stage, sems):
    lists = recv_ref[...].astype(F32)
    slots = iota((8 * CAP, ROWS), 1).astype(F32)
    copies = []
    for n in range(4):
        at = pl.ds(n * 8 * CAP, 8 * CAP)
        col = column(lists[n * 8 : n * 8 + 8], 8, CAP)
        hot = (col == slots).astype(F32).astype(BF)
        stage[at] = jnp.dot(hot, q_ref[...], preferred_element_type=F32).astype(BF)
        copy = pltpu.make_async_copy(stage.at[at], out_ref.at[at], sems.at[n])
        copy.start()
        copies.append(copy)
    for copy in copies:
        copy.wait()


def place_kernel(recv_ref, x_ref, w_ref, q_ref, out_ref, full_ref, own_k_ref, own_v_ref):
    for n in range(4):
        at = pl.ds(n * 256, 256)
        scale = row_scales(x_ref[at])
        for t, own_ref in ((1, own_k_ref), (2, own_v_ref)):
            got = jnp.dot(x_ref[at], w_ref[t], preferred_element_type=F32)
            own_ref[at] = (got * scale).astype(BF)
    slot = recv_ref[...]
    last = jnp.where(slot[:, CAP - 1 : CAP] >= 0, 1.0, 0.0)
    full_ref[...] = peer_numbers(full_peers(last))
    below = iota((PEERS, PEERS), 1) < iota((PEERS, PEERS), 0)
    order = jnp.dot(
        below.astype(F32).astype(BF),
        jnp.broadcast_to(last, (PEERS, 128)).astype(BF),
        preferred_element_type=F32,
    )
    high = jnp.where(slot >= 0, slot // 32, -1)
    low = slot % 32
    acc = jnp.zeros((96, 32), F32)
    where_c = iota((32, 128), 1).astype(F32)
    for s in range(PEERS):
        a = (iota((32, 128), 0) == high[s : s + 1, :]).astype(F32)
        b = (iota((32, 128), 0) == low[s : s + 1, :]).astype(F32).astype(BF)
        left = jnp.concatenate([a * float(s), a * where_c, a * order[s : s + 1]], axis=0)
        acc = acc + lax.dot_general(left.astype(BF), b, NT, preferred_element_type=F32)
    wide = jnp.concatenate([acc, jnp.zeros((96, 96), F32)], axis=1)
    src, place, rank = (column(wide[n * 32 : n * 32 + 32], 32, 32) for n in range(3))
    rest = float(PEERS * LOW - LOW) + rank * float(REST) + place
    pos = jnp.where(place < float(LOW), src * float(LOW) + place, rest)
    prod = q_ref[...].astype(F32) * own_k_ref[...].astype(F32) * (1.0 / HD**0.5)
    s0 = jnp.sum(prod[:, :HD], axis=1, keepdims=True)
    s1 = jnp.sum(prod[:, HD:], axis=1, keepdims=True)
    high = jnp.floor(pos * (1.0 / 32.0))
    pieces = [high, pos - high * 32.0, place, src]
    for value in (s0, s1):
        for _ in range(3):
            piece = value.astype(BF).astype(F32)
            pieces.append(piece)
            value = value - piece
    lane = iota((ROWS, 128), 1)
    known = jnp.zeros((ROWS, 128), F32)
    for n, piece in enumerate(pieces):
        known = jnp.where(lane == n, piece, known)
    out_ref[...] = known.astype(BF)


def attend_kernel(full_hbm, q_ref, kv_ref, out_ref, kv, rows_ref, stage, full_ref, sems):
    n = 256
    listing = pltpu.make_async_copy(full_hbm, full_ref, sems.at[9])
    listing.start()
    copies = []
    for part in range(2):
        for i in range(4):
            src = kv_ref.at[pl.ds(i * n, n), pl.ds(part * ROWS, ROWS)]
            dst = kv.at[i, :, pl.ds(part * ROWS, ROWS)]
            copies.append(pltpu.make_async_copy(src, dst, sems.at[part * 4 + i]))
    for copy in copies:
        copy.start()
    split = PEERS * LOW
    rows_ref[:split, :] = q_ref[:, :LOW, :].reshape(split, 128)
    listing.wait()
    peers = [pl.ds(full_ref[k, 0], 1) for k in range(FULL)]
    for k, peer in enumerate(peers):
        at = split + k * REST
        rows_ref[at : at + REST, :] = q_ref[peer, LOW:, :].reshape(REST, 128)
    sel_p = iota((16, ROWS), 1) // 128
    sel_h = (iota((16, ROWS), 1) % 128) // HD
    sel = (iota((16, ROWS), 0) == sel_h * 8 + sel_p).astype(F32).astype(BF)
    sum_p = iota((ROWS, 128), 0) // 128
    sum_h = (iota((ROWS, 128), 0) % 128) // HD
    sums = (iota((ROWS, 128), 1) == sum_h * 8 + sum_p).astype(F32).astype(BF)
    scores = []
    for i in range(4):
        q = rows_ref[i * n : (i + 1) * n, :].astype(F32)
        copies[i].wait()
        score = jnp.zeros((n, 128), F32)
        for p in range(0, 8, 2):
            highs, lows = [], []
            for t in (p, p + 1):
                prod = q * kv[i, :, t * 128 : (t + 1) * 128].astype(F32)
                high = prod.astype(BF)
                highs.append(high)
                lows.append((prod - high.astype(F32)).astype(BF))
            part = sums[p * 128 : (p + 2) * 128]
            highs, lows = jnp.concatenate(highs, axis=1), jnp.concatenate(lows, axis=1)
            score = score + jnp.dot(highs, part, preferred_element_type=F32)
            score = score + jnp.dot(lows, part, preferred_element_type=F32)
        scores.append(score.T[:16])
    score = jnp.concatenate(scores, axis=1) * (1.0 / HD**0.5)
    weights, parts = [], []
    for h in range(2):
        part = score[h * 8 : (h + 1) * 8]
        top = jnp.max(part, axis=0, keepdims=True)
        expo = jnp.exp(part - top)
        norm = jnp.sum(expo, axis=0, keepdims=True)
        weights.append(expo / norm)
        lse = top + jnp.log(norm)
        for _ in range(3):
            piece = lse.astype(BF).astype(F32)
            parts.append(piece)
            lse = lse - piece
    weight = jnp.concatenate(weights, axis=0).astype(BF)
    tail = jnp.concatenate(parts + [jnp.zeros((10, ROWS), F32)], axis=0)
    stage[:, LOW:CAP, :] = jnp.zeros((PEERS, REST, 128), BF)
    for k in range(PEERS):
        piece = tail[:, k * LOW : (k + 1) * LOW]
        piece = jnp.concatenate([piece, jnp.zeros((16, 128 - LOW), F32)], axis=1)
        stage[k, CAP:, :] = piece.astype(BF)
    for i in range(4):
        wide = lax.dot_general(
            weight[:, i * n : (i + 1) * n], sel, TN, preferred_element_type=F32
        )
        copies[4 + i].wait()
        ctx = jnp.zeros((n, 128), F32)
        for p in range(8):
            value = kv[i, :, ROWS + p * 128 : ROWS + (p + 1) * 128].astype(F32)
            ctx = ctx + wide[:, p * 128 : (p + 1) * 128] * value
        ctx = ctx.astype(BF)
        if i < 2:
            stage[i * 16 : (i + 1) * 16, :LOW, :] = ctx.reshape(16, LOW, 128)
        else:
            for k in range(8):
                peer = peers[(i - 2) * 8 + k]
                stage[peer, LOW:CAP, :] = ctx[k * REST : (k + 1) * REST].reshape(1, REST, 128)
    for k, peer in enumerate(peers):
        at = split + k * REST
        before, after = jnp.zeros((16, LOW), F32), jnp.zeros((16, 128 - CAP), F32)
        piece = jnp.concatenate([before, tail[:, at : at + REST], after], axis=1).astype(BF)
        stage[peer, CAP:, :] = stage[peer, CAP:, :] + piece.reshape(1, 16, 128)
    end = pltpu.make_async_copy(stage, out_ref, sems.at[8])
    end.start()
    end.wait()


def merge_kernel(
    full_hbm, msg_hbm, place_hbm, v_hbm, mine_ref, theirs_ref, msg_ref, place_ref, v_ref, ctx_ref,
    full_ref, sems
):
    rows = 256
    outs = [r.at[pl.ds(n * rows, rows)] for r in (mine_ref, theirs_ref) for n in range(2)]
    pairs = [(full_hbm, full_ref), (msg_hbm, msg_ref), (place_hbm, place_ref), (v_hbm, v_ref)]
    fetch = [pltpu.make_async_copy(a, b, sems.at[i]) for i, (a, b) in enumerate(pairs)]
    for copy in fetch:
        copy.start()
    piece, lane = iota((128, 512), 0), iota((128, 512), 1)
    use = jnp.where(lane < 128, jnp.where(piece == 0, 32.0, jnp.where(piece == 1, 1.0, 0.0)), 0.0)
    use = use + jnp.where((lane // 128 == 1) & (piece == 2), 1.0, 0.0)
    use = use + jnp.where((lane // 128 == 2) & (piece == 3), 1.0, 0.0)
    scores = (lane >= 384) & (piece >= 4) & (piece < 10)
    head = (lane - 384) // HD
    use = use + jnp.where(scores & ((piece - 4) // 3 == head), 1.0, 0.0)
    use = use.astype(BF)
    lanes = iota((rows, 128), 1).astype(F32)
    entry = iota((rows, PEERS * 16), 1)
    of_source = (entry // 16).astype(F32)
    of_head = entry % 16 // 3
    for copy in fetch:
        copy.wait()
    low = PEERS * LOW
    ctx_ref[:low, :] = msg_ref[:, :LOW, :].reshape(low, 128)
    for k in range(FULL):
        got = msg_ref[pl.ds(full_ref[k, 0], 1), LOW:CAP, :].reshape(REST, 128)
        ctx_ref[low + k * REST : low + (k + 1) * REST, :] = got
    parts = msg_ref[:, CAP:, :].reshape(PEERS * 16, 128)
    parity = lax.axis_index("x") % 2
    for i, out in enumerate(outs):
        block = (parity if i < 2 else 1 - parity) + 2 * (i % 2)
        at = pl.ds(pl.multiple_of(block * rows, rows), rows)
        known = jnp.dot(place_ref[at, :], use, preferred_element_type=F32)
        pos, own = known[:, :128], known[:, 384:]
        hot = [(lanes + float(t * 128) == pos).astype(F32).astype(BF) for t in range(8)]
        hot = jnp.concatenate(hot, axis=1)
        ctx = jnp.dot(hot, ctx_ref[...], preferred_element_type=F32)
        hit = of_source == jnp.concatenate([known[:, 256:384]] * 4, axis=1)
        here = lanes == known[:, 128:256]
        cols = []
        for h in range(2):
            pick = jnp.where(hit & (of_head == h), 1.0, 0.0).astype(BF)
            lists = jnp.dot(pick, parts, preferred_element_type=F32)
            cols.append(jnp.sum(jnp.where(here, lists, 0.0), axis=1, keepdims=True))
        lse = jnp.where(lanes < HD, cols[0], cols[1])
        top = jnp.maximum(lse, own)
        a = jnp.exp(lse - top)
        b = jnp.exp(own - top)
        out[...] = ((a * ctx + b * v_ref[at, :].astype(F32)) / (a + b)).astype(BF)


def project_kernel(a0, a1, a2, a3, own_ref, two_ref, left_ref, right_ref, out_ref, near, sems):
    copies = [
        pltpu.make_async_copy(r.at[pl.ds(512, 128)], near.at[pl.ds(n * 128, 128)], sems.at[n])
        for n, r in enumerate((left_ref, right_ref))
    ]
    for copy in copies:
        copy.start()
    rows = jnp.concatenate([a0[...], a3[...]], axis=1)
    weight = jnp.concatenate([own_ref[...], two_ref[...]], axis=0)
    total = jnp.dot(rows, weight, preferred_element_type=F32)
    rows = jnp.concatenate([a1[...], a2[...]], axis=1)
    for copy in copies:
        copy.wait()
    total = total + jnp.dot(rows, near[...], preferred_element_type=F32)
    out_ref[...] = total.astype(BF)


def ffn_kernel(
    x_ref, p_ref, r_ref, up_ref, down_ref, right_ref, left_ref, same_ref, other_ref, ups, downs,
    hid, acc, sems
):
    pairs = []
    for n, src in enumerate((right_ref, left_ref)):
        for k in range(4):
            block = pl.ds(k * 256, 256)
            pairs.append((src.at[pl.ds(0, 256), block], ups.at[block, pl.ds(n * 256, 256)]))
    for n, src in enumerate((right_ref, left_ref)):
        pairs.append((src.at[pl.ds(256, 256)], downs.at[pl.ds(n * 256, 256)]))
    copies = [pltpu.make_async_copy(a, b, sems.at[i]) for i, (a, b) in enumerate(pairs)]
    for copy in copies:
        copy.start()
    x = lax.axis_index("x")
    core = lax.axis_index("core")
    normed = []
    for n in range(2):
        at = pl.ds(n * 256, 256)
        attn = p_ref[at].astype(F32) + r_ref[at].astype(F32)
        rows = pl.ds(pl.multiple_of((x % 2 + 2 * n) * 256, 256), 256)
        hidden = (x_ref[rows, :].astype(F32) + attn).astype(BF).astype(F32)
        scale = lax.rsqrt(jnp.mean(hidden * hidden, axis=-1, keepdims=True) + 1e-05)
        normed.append((hidden * scale).astype(BF))
        hid[at] = jnp.where(x // 2 == n, hidden, 0.0)
    normed = jnp.concatenate(normed, axis=0)
    act = jax.nn.gelu(jnp.dot(normed, up_ref[...], preferred_element_type=F32)).astype(BF)
    total = jnp.dot(act, down_ref[...], preferred_element_type=F32)
    for copy in copies[:8]:
        copy.wait()
    act = jax.nn.gelu(jnp.dot(normed, ups[...], preferred_element_type=F32)).astype(BF)
    for copy in copies[8:]:
        copy.wait()
    acc[...] = total + jnp.dot(act, downs[...], preferred_element_type=F32)
    for d in range(4):
        head = ((x + d) % 4) * 2
        at = pl.ds(pl.multiple_of((head + core) * 128, 128), 128)
        same_ref[d] = hid[:, at] + acc[:, at]
        at = pl.ds(pl.multiple_of((head + 1 - core) * 128, 128), 128)
        other_ref[d] = acc[:, at].astype(BF)


def final_kernel(same_ref, other_ref, o0, o1, o2, o3):
    for i, out in enumerate((o0, o1, o2, o3)):
        out[...] = (same_ref[i] + other_ref[i].astype(F32)).astype(BF)


def place_rows_kernel(p0, p1, p2, p3, out_ref):
    mine = lax.axis_index("x") % 2
    for n in range(2):
        at = pl.ds(n * 256, 256)
        for parity, a, b in ((mine, p0, p2), (1 - mine, p1, p3)):
            to = pl.multiple_of((parity + 2 * n) * 256, 256)
            out_ref[pl.ds(to, 256), :] = (a[at].astype(F32) + b[at].astype(F32)).astype(BF)


def shift(x, axis, by, size):
    return lax.ppermute(x, axis, [(i, (i + by) % size) for i in range(size)])


def body(stream_in, keys, values, counts, slots, w_qkv, w_out, w_up, w_down):
    vmem = pl.BlockSpec(memory_space=pltpu.VMEM)
    hbm = pl.BlockSpec(memory_space=pltpu.HBM)
    send, par, my_full = call(
        plan_kernel,
        (
            pltpu.HBM((PEERS, 128), jnp.int32),
            pltpu.HBM((PEERS + FULL, 128), F32),
            pltpu.HBM((FULL, 128), jnp.int32),
        ),
        (4 * 10**8, 10**6),
    )(keep(counts.reshape(1, ROWS), pltpu.HBM), keep(slots.T, pltpu.HBM))
    recv = lax.all_to_all(
        send.reshape(PEERS, 1, 128), SAMPLE, split_axis=0, concat_axis=0, tiled=True
    ).reshape(PEERS, 128)

    query = call(
        project_query_kernel,
        sds((ROWS, 128), BF),
        (3 * 10**8, 3 * 10**6),
        in_specs=[vmem, vmem],
        out_specs=vmem,
    )(stream_in, w_qkv)
    for_right, for_left = call(
        pack_kernel,
        (pltpu.HBM((640, ROWS), BF), pltpu.HBM((640, ROWS), BF)),
        (0, 5 * 10**6),
        in_specs=[hbm] * 3,
        out_specs=(hbm, hbm),
        scratch_shapes=[pltpu.VMEM((2, 640, ROWS), BF), pltpu.SemaphoreType.DMA((18,))],
    )(*(keep(w, pltpu.HBM) for w in (w_up, w_down, w_out)))
    q_send = call(
        query_kernel,
        pltpu.HBM((ITEMS, 128), BF),
        (2 * ITEMS * ROWS * 128, 10**6),
        in_specs=[vmem, vmem, hbm],
        out_specs=hbm,
        scratch_shapes=[pltpu.VMEM((ITEMS, 128), BF), pltpu.SemaphoreType.DMA((4,))],
    )(recv, query, keep(for_left, pltpu.HBM))
    kv = call(
        expand_kernel,
        pltpu.HBM((ROWS, 2 * ROWS), BF),
        (2 * ROWS * ROWS * ROWS * 2, 12 * 10**6),
        in_specs=[vmem, hbm, hbm],
        out_specs=hbm,
        scratch_shapes=[
            pltpu.VMEM((2, ROWS, 8, 128), BF),
            pltpu.VMEM((2, ROWS, ROWS), BF),
            pltpu.VMEM((4, 256, ROWS), BF),
            pltpu.VMEM((2, 4, 256, ROWS), BF),
            pltpu.SemaphoreType.DMA((10,)),
        ],
    )(*(keep(a, pltpu.HBM) for a in (par, keys, values)))
    left = shift(for_right, "x", 1, 4)
    right = shift(for_left, "x", 3, 4)
    wo_two = shift(w_out, "x", 2, 4)

    q_recv = lax.all_to_all(q_send, SAMPLE, split_axis=0, concat_axis=0, tiled=True)

    places, your_full, own_key, own_value = call(
        place_kernel,
        (
            pltpu.HBM((ROWS, 128), BF),
            pltpu.HBM((FULL, 128), jnp.int32),
            sds((ROWS, 128), BF),
            pltpu.HBM((ROWS, 128), BF),
        ),
        (2 * 10**9, 4 * 10**6),
    )(recv, stream_in, w_qkv, keep(query, pltpu.HBM))
    new_kv = jnp.stack([own_key, own_value], axis=1)

    msg = call(
        attend_kernel,
        pltpu.HBM((PEERS, MSG, 128), BF),
        (2 * ROWS * ROWS * 128, 8 * 10**6),
        in_specs=[hbm, vmem, hbm],
        out_specs=hbm,
        scratch_shapes=[
            pltpu.VMEM((4, 256, 2 * ROWS), BF),
            pltpu.VMEM((ROWS, 128), BF),
            pltpu.VMEM((PEERS, MSG, 128), BF),
            pltpu.SMEM((FULL, 128), jnp.int32),
            pltpu.SemaphoreType.DMA((10,)),
        ],
    )(keep(my_full, pltpu.HBM), q_recv.reshape(PEERS, CAP, 128), keep(kv, pltpu.HBM))
    answer = lax.all_to_all(msg, SAMPLE, split_axis=0, concat_axis=0, tiled=True)
    pair = sds((512, 128), BF)
    mine, theirs = call(
        merge_kernel,
        (pair, pair),
        (2 * ITEMS * ROWS * 128, 5 * 10**6),
        in_specs=[hbm] * 4,
        out_specs=(vmem, vmem),
        scratch_shapes=[
            pltpu.VMEM((PEERS, MSG, 128), BF),
            pltpu.VMEM((ROWS, 128), BF),
            pltpu.VMEM((ROWS, 128), BF),
            pltpu.VMEM((ROWS, 128), BF),
            pltpu.SMEM((FULL, 128), jnp.int32),
            pltpu.SemaphoreType.DMA((4,)),
        ],
    )(*(keep(a, pltpu.HBM) for a in (your_full, answer, places, own_value)))

    from_left = shift(theirs, "x", 1, 4)
    from_right = shift(theirs, "x", 3, 4)
    from_two = shift(mine, "x", 2, 4)
    partial = call(
        project_kernel,
        sds((512, ROWS), BF),
        (6 * 10**8, 3 * 10**6),
        in_specs=[vmem] * 6 + [hbm] * 2,
        out_specs=vmem,
        scratch_shapes=[pltpu.VMEM((256, ROWS), BF), pltpu.SemaphoreType.DMA((2,))],
    )(
        mine,
        from_left,
        from_right,
        from_two,
        keep(w_out),
        keep(wo_two),
        keep(left, pltpu.HBM),
        keep(right, pltpu.HBM),
    )
    partner = shift(partial, "core", 1, 2)

    same, other = call(
        ffn_kernel,
        (sds((4, 512, 128), F32), sds((4, 512, 128), BF)),
        (2 * 10**9, 10 * 10**6),
        in_specs=[vmem] * 5 + [hbm] * 2,
        out_specs=(vmem, vmem),
        scratch_shapes=[
            pltpu.VMEM((ROWS, 512), BF),
            pltpu.VMEM((512, ROWS), BF),
            pltpu.VMEM((512, ROWS), F32),
            pltpu.VMEM((512, ROWS), F32),
            pltpu.SemaphoreType.DMA((10,)),
        ],
    )(
        stream_in,
        partial,
        partner,
        keep(w_up),
        keep(w_down),
        keep(right, pltpu.HBM),
        keep(left, pltpu.HBM),
    )

    swapped = shift(other, "core", 1, 2)
    done = call(final_kernel, (pair,) * 4, (10**6, 10**6))(same, swapped)
    parts = [done[0]] + [shift(done[d], "x", d, 4) for d in (1, 2, 3)]
    layer_out = call(
        place_rows_kernel,
        sds((ROWS, 128), BF),
        (10**6, 5 * 10**5),
        in_specs=[vmem] * 4,
        out_specs=vmem,
    )(*parts)
    return (layer_out, new_kv)


def solution(mesh):
    grid = Mesh(mesh.devices.reshape(8, 4, 4, 2), ("z", "y", "x", "core"))
    in_specs = (
        P(SAMPLE, None),
        P(SAMPLE, None, HEAD),
        P(SAMPLE, None, HEAD),
        P(SAMPLE),
        P(SAMPLE, None),
        P(None, None, HEAD),
        P(HEAD, None),
        P(None, HEAD),
        P(HEAD, None),
    )
    out_specs = (P(SAMPLE, HEAD), P(SAMPLE, None, HEAD))
    return jax.shard_map(body, mesh=grid, in_specs=in_specs, out_specs=out_specs, check_vma=False)
```

```python
import functools

import jax
import jax.numpy as jnp
from jax import lax
from jax.experimental import pallas as pl
from jax.experimental.pallas import tpu as pltpu
from jax.sharding import Mesh, PartitionSpec as P

HD = 64
PEERS = 32
CAP = 48
ROWS = 1024
ITEMS = PEERS * CAP
MSG = 64
LOW = 16
FULL = PEERS // 2
REST = CAP - LOW
SAMPLE = ("z", "y")
HEAD = ("x", "core")
F32 = jnp.float32
BF = jnp.bfloat16
NT = (((1,), (1,)), ((), ()))
TN = (((0,), (0,)), ((), ()))


def iota(shape, dim):
    return lax.broadcasted_iota(jnp.int32, shape, dim)


def call(kernel, out, cost, vmem=24, **kw):
    return pl.pallas_call(
        kernel,
        out_shape=out,
        compiler_params=pltpu.CompilerParams(vmem_limit_bytes=vmem * 2**20),
        cost_estimate=pl.CostEstimate(flops=cost[0], bytes_accessed=cost[1], transcendentals=0),
        **kw,
    )


def keep(x, space=pltpu.VMEM):
    return pltpu.with_memory_space_constraint(x, space)


def sds(shape, dtype):
    return jax.ShapeDtypeStruct(shape, dtype)


def full_peers(last):
    rows, cols = iota((PEERS, PEERS), 0), iota((PEERS, PEERS), 1)
    order = jnp.sum(jnp.where(rows < cols, last, 0.0), axis=0, keepdims=True)
    flag = jnp.sum(jnp.where(rows == cols, last, 0.0), axis=0, keepdims=True)
    hit = iota((FULL, PEERS), 0).astype(F32) == order
    return jnp.where(hit, flag, 0.0).astype(BF)


def peer_numbers(chosen):
    numbers = iota((PEERS, 128), 0).astype(F32).astype(BF)
    return jnp.dot(chosen, numbers, preferred_element_type=F32).astype(jnp.int32)


def plan_kernel(cnt_ref, slot_ref, send_ref, par_ref, full_ref):
    width = 256
    blocks = ROWS // width
    cnt = cnt_ref[...]
    tri = (iota((width, width), 0) <= iota((width, width), 1)).astype(F32).astype(BF)
    ow = iota((PEERS, width), 0)
    groups = []
    for k in range(4):
        for b in range(blocks):
            sl = slot_ref[k : k + 1, b * width : (b + 1) * width]
            live = cnt[:, b * width : (b + 1) * width] > k
            owner = jnp.where(live, sl // ROWS, -1)
            member = (ow == owner).astype(F32)
            groups.append((sl, live, member, b))
    stacked = jnp.concatenate([g[2].astype(BF) for g in groups], axis=0)
    inc = jnp.dot(stacked, tri, preferred_element_type=F32)
    base = jnp.zeros((PEERS, 1), F32)
    total = jnp.zeros((5 * PEERS, CAP), F32)
    parent = iota((1, width), 1)
    for g, (sl, live, member, b) in enumerate(groups):
        run = inc[g * PEERS : (g + 1) * PEERS]
        rank = jnp.sum(member * (run + (base - 1.0)), axis=0, keepdims=True)
        base = base + run[:, width - 1 : width]
        rank = jnp.where(live, rank.astype(jnp.int32), -1)
        place = (iota((CAP, width), 0) == rank).astype(F32).astype(BF)
        local = sl % ROWS
        par = parent + b * width
        left = jnp.concatenate(
            [
                member * (local // 32).astype(F32),
                member * (local % 32).astype(F32),
                member,
                member * (par // 32).astype(F32),
                member * (par % 32).astype(F32),
            ],
            axis=0,
        ).astype(BF)
        total = total + lax.dot_general(left, place, NT, preferred_element_type=F32)
    whole = total.astype(jnp.int32)
    have = whole[2 * PEERS : 3 * PEERS] > 0
    send = jnp.where(have, whole[:PEERS] * 32 + whole[PEERS : 2 * PEERS], -1)
    fill = jnp.full((PEERS, 128 - CAP), -1, jnp.int32)
    send_ref[...] = jnp.concatenate([send, fill], axis=1)
    chosen = full_peers(jnp.where(have[:, CAP - 1 :], 1.0, 0.0))
    full_ref[...] = peer_numbers(chosen)
    high, low = total[3 * PEERS : 4 * PEERS], total[4 * PEERS :]
    rest = 32.0 * jnp.dot(chosen, high.astype(BF), preferred_element_type=F32)
    rest = rest + jnp.dot(chosen, low.astype(BF), preferred_element_type=F32)
    first = (high[:, :LOW] * 32.0 + low[:, :LOW]).astype(jnp.int32)
    par_ref[:PEERS, :LOW] = first
    par_ref[:PEERS, LOW:] = jnp.zeros((PEERS, 128 - LOW), jnp.int32)
    par_ref[PEERS:, :REST] = rest[:, LOW:].astype(jnp.int32)
    par_ref[PEERS:, REST:] = jnp.zeros((FULL, 128 - REST), jnp.int32)


def pack_kernel(up_ref, down_ref, wo_ref, right_ref, left_ref, stage, sems):
    loads, stores = [], []
    for n, out in enumerate((right_ref, left_ref)):
        half = pl.ds(n * 256, 256)
        pairs = [(up_ref.at[pl.ds(k * 256, 256), half], pl.ds(k * 256, 256)) for k in range(4)]
        pairs = [(a, stage.at[n, pl.ds(0, 256), b]) for a, b in pairs]
        pairs.append((down_ref.at[half], stage.at[n, pl.ds(256, 256)]))
        pairs.append((wo_ref, stage.at[n, pl.ds(512, 128)]))
        loads.append(
            [pltpu.make_async_copy(a, b, sems.at[n * 9 + i]) for i, (a, b) in enumerate(pairs)]
        )
        parts = [pl.ds(0, 256), pl.ds(256, 256), pl.ds(512, 128)]
        stores.append(
            [
                pltpu.make_async_copy(stage.at[n, p], out.at[p], sems.at[n * 9 + 6 + i])
                for i, p in enumerate(parts)
            ]
        )
    for copy in loads[0] + loads[1]:
        copy.start()
    for n in range(2):
        for i in range(3):
            for copy in (loads[n][:4], loads[n][4:5], loads[n][5:])[i]:
                copy.wait()
            stores[n][i].start()
    for copy in stores[0] + stores[1]:
        copy.wait()


def column(lists, count, depth):
    shape = (count, depth, 128)
    picked = jnp.where(
        iota(shape, 1) == iota(shape, 2), jnp.broadcast_to(lists[:, None, :], shape), 0.0
    )
    return jnp.sum(picked, axis=2, keepdims=True).reshape(count * depth, 1)


def expand_kernel(par_hbm, k_hbm, v_hbm, out_ref, raw, got, stage, par, sems):
    n = 256
    lists = pltpu.make_async_copy(par_hbm, par, sems.at[10])
    lists.start()
    loads = [
        pltpu.make_async_copy(a, raw.at[t], sems.at[t]) for t, a in enumerate((k_hbm, v_hbm))
    ]
    for copy in loads:
        copy.start()
    lists.wait()
    copies = []
    for t in range(2):
        loads[t].wait()

        def first(o, carry):
            for c in range(LOW):
                got[t, o * LOW + c] = raw[t, par[o, c]]
            return carry

        def rest(k, carry):
            for c in range(REST):
                got[t, PEERS * LOW + k * REST + c] = raw[t, par[PEERS + k, c]]
            return carry

        lax.fori_loop(0, PEERS, first, 0)
        lax.fori_loop(0, FULL, rest, 0)
        for i in range(4):
            stage[t, i] = got[t, i * n : (i + 1) * n].reshape(n, ROWS)
            to = out_ref.at[pl.ds(i * n, n), pl.ds(t * ROWS, ROWS)]
            copy = pltpu.make_async_copy(stage.at[t, i], to, sems.at[2 + t * 4 + i])
            copy.start()
            copies.append(copy)
    for copy in copies:
        copy.wait()


def row_scales(x):
    x = x.astype(F32)
    return lax.rsqrt(jnp.mean(x * x, axis=-1, keepdims=True) + 1e-05)


def project_query_kernel(x_ref, w_ref, out_ref):
    for n in range(4):
        at = pl.ds(n * 256, 256)
        got = jnp.dot(x_ref[at], w_ref[0], preferred_element_type=F32)
        out_ref[at] = (got * row_scales(x_ref[at])).astype(BF)


def query_kernel(recv_ref, q_ref, after_ref, out_ref, stage, sems):
    lists = recv_ref[...].astype(F32)
    slots = iota((8 * CAP, ROWS), 1).astype(F32)
    copies = []
    for n in range(4):
        at = pl.ds(n * 8 * CAP, 8 * CAP)
        col = column(lists[n * 8 : n * 8 + 8], 8, CAP)
        hot = (col == slots).astype(F32).astype(BF)
        stage[at] = jnp.dot(hot, q_ref[...], preferred_element_type=F32).astype(BF)
        copy = pltpu.make_async_copy(stage.at[at], out_ref.at[at], sems.at[n])
        copy.start()
        copies.append(copy)
    for copy in copies:
        copy.wait()


def place_kernel(recv_ref, x_ref, w_ref, q_ref, out_ref, full_ref, own_k_ref, own_v_ref):
    for n in range(4):
        at = pl.ds(n * 256, 256)
        scale = row_scales(x_ref[at])
        for t, own_ref in ((1, own_k_ref), (2, own_v_ref)):
            got = jnp.dot(x_ref[at], w_ref[t], preferred_element_type=F32)
            own_ref[at] = (got * scale).astype(BF)
    slot = recv_ref[...]
    last = jnp.where(slot[:, CAP - 1 : CAP] >= 0, 1.0, 0.0)
    full_ref[...] = peer_numbers(full_peers(last))
    below = iota((PEERS, PEERS), 1) < iota((PEERS, PEERS), 0)
    order = jnp.dot(
        below.astype(F32).astype(BF),
        jnp.broadcast_to(last, (PEERS, 128)).astype(BF),
        preferred_element_type=F32,
    )
    high = jnp.where(slot >= 0, slot // 32, -1)
    low = slot % 32
    acc = jnp.zeros((96, 32), F32)
    where_c = iota((32, 128), 1).astype(F32)
    for s in range(PEERS):
        a = (iota((32, 128), 0) == high[s : s + 1, :]).astype(F32)
        b = (iota((32, 128), 0) == low[s : s + 1, :]).astype(F32).astype(BF)
        left = jnp.concatenate([a * float(s), a * where_c, a * order[s : s + 1]], axis=0)
        acc = acc + lax.dot_general(left.astype(BF), b, NT, preferred_element_type=F32)
    wide = jnp.concatenate([acc, jnp.zeros((96, 96), F32)], axis=1)
    src, place, rank = (column(wide[n * 32 : n * 32 + 32], 32, 32) for n in range(3))
    rest = float(PEERS * LOW - LOW) + rank * float(REST) + place
    pos = jnp.where(place < float(LOW), src * float(LOW) + place, rest)
    prod = q_ref[...].astype(F32) * own_k_ref[...].astype(F32) * (1.0 / HD**0.5)
    s0 = jnp.sum(prod[:, :HD], axis=1, keepdims=True)
    s1 = jnp.sum(prod[:, HD:], axis=1, keepdims=True)
    high = jnp.floor(pos * (1.0 / 32.0))
    pieces = [high, pos - high * 32.0, place, src]
    for value in (s0, s1):
        for _ in range(3):
            piece = value.astype(BF).astype(F32)
            pieces.append(piece)
            value = value - piece
    lane = iota((ROWS, 128), 1)
    known = jnp.zeros((ROWS, 128), F32)
    for n, piece in enumerate(pieces):
        known = jnp.where(lane == n, piece, known)
    out_ref[...] = known.astype(BF)


def attend_kernel(full_hbm, q_ref, kv_ref, out_ref, kv, rows_ref, stage, full_ref, sems):
    n = 256
    listing = pltpu.make_async_copy(full_hbm, full_ref, sems.at[9])
    listing.start()
    copies = []
    for part in range(2):
        for i in range(4):
            src = kv_ref.at[pl.ds(i * n, n), pl.ds(part * ROWS, ROWS)]
            dst = kv.at[i, :, pl.ds(part * ROWS, ROWS)]
            copies.append(pltpu.make_async_copy(src, dst, sems.at[part * 4 + i]))
    for copy in copies:
        copy.start()
    split = PEERS * LOW
    rows_ref[:split, :] = q_ref[:, :LOW, :].reshape(split, 128)
    listing.wait()
    peers = [pl.ds(full_ref[k, 0], 1) for k in range(FULL)]
    for k, peer in enumerate(peers):
        at = split + k * REST
        rows_ref[at : at + REST, :] = q_ref[peer, LOW:, :].reshape(REST, 128)
    sel_p = iota((16, ROWS), 1) // 128
    sel_h = (iota((16, ROWS), 1) % 128) // HD
    sel = (iota((16, ROWS), 0) == sel_h * 8 + sel_p).astype(F32).astype(BF)
    sum_p = iota((ROWS, 128), 0) // 128
    sum_h = (iota((ROWS, 128), 0) % 128) // HD
    sums = (iota((ROWS, 128), 1) == sum_h * 8 + sum_p).astype(F32).astype(BF)
    scores = []
    for i in range(4):
        q = rows_ref[i * n : (i + 1) * n, :].astype(F32)
        copies[i].wait()
        score = jnp.zeros((n, 128), F32)
        for p in range(0, 8, 2):
            highs, lows = [], []
            for t in (p, p + 1):
                prod = q * kv[i, :, t * 128 : (t + 1) * 128].astype(F32)
                high = prod.astype(BF)
                highs.append(high)
                lows.append((prod - high.astype(F32)).astype(BF))
            part = sums[p * 128 : (p + 2) * 128]
            highs, lows = jnp.concatenate(highs, axis=1), jnp.concatenate(lows, axis=1)
            score = score + jnp.dot(highs, part, preferred_element_type=F32)
            score = score + jnp.dot(lows, part, preferred_element_type=F32)
        scores.append(score.T[:16])
    score = jnp.concatenate(scores, axis=1) * (1.0 / HD**0.5)
    weights, parts = [], []
    for h in range(2):
        part = score[h * 8 : (h + 1) * 8]
        top = jnp.max(part, axis=0, keepdims=True)
        expo = jnp.exp(part - top)
        norm = jnp.sum(expo, axis=0, keepdims=True)
        weights.append(expo / norm)
        lse = top + jnp.log(norm)
        for _ in range(3):
            piece = lse.astype(BF).astype(F32)
            parts.append(piece)
            lse = lse - piece
    weight = jnp.concatenate(weights, axis=0).astype(BF)
    tail = jnp.concatenate(parts + [jnp.zeros((10, ROWS), F32)], axis=0)
    stage[:, LOW:CAP, :] = jnp.zeros((PEERS, REST, 128), BF)
    for k in range(PEERS):
        piece = tail[:, k * LOW : (k + 1) * LOW]
        piece = jnp.concatenate([piece, jnp.zeros((16, 128 - LOW), F32)], axis=1)
        stage[k, CAP:, :] = piece.astype(BF)
    for i in range(4):
        wide = lax.dot_general(
            weight[:, i * n : (i + 1) * n], sel, TN, preferred_element_type=F32
        )
        copies[4 + i].wait()
        ctx = jnp.zeros((n, 128), F32)
        for p in range(8):
            value = kv[i, :, ROWS + p * 128 : ROWS + (p + 1) * 128].astype(F32)
            ctx = ctx + wide[:, p * 128 : (p + 1) * 128] * value
        ctx = ctx.astype(BF)
        if i < 2:
            stage[i * 16 : (i + 1) * 16, :LOW, :] = ctx.reshape(16, LOW, 128)
        else:
            for k in range(8):
                peer = peers[(i - 2) * 8 + k]
                stage[peer, LOW:CAP, :] = ctx[k * REST : (k + 1) * REST].reshape(1, REST, 128)
    for k, peer in enumerate(peers):
        at = split + k * REST
        before, after = jnp.zeros((16, LOW), F32), jnp.zeros((16, 128 - CAP), F32)
        piece = jnp.concatenate([before, tail[:, at : at + REST], after], axis=1).astype(BF)
        stage[peer, CAP:, :] = stage[peer, CAP:, :] + piece.reshape(1, 16, 128)
    end = pltpu.make_async_copy(stage, out_ref, sems.at[8])
    end.start()
    end.wait()


def merge_kernel(
    full_hbm, msg_hbm, place_hbm, v_hbm, mine_ref, theirs_ref, msg_ref, place_ref, v_ref, ctx_ref,
    full_ref, sems
):
    rows = 256
    outs = [r.at[pl.ds(n * rows, rows)] for r in (mine_ref, theirs_ref) for n in range(2)]
    pairs = [(full_hbm, full_ref), (msg_hbm, msg_ref), (place_hbm, place_ref), (v_hbm, v_ref)]
    fetch = [pltpu.make_async_copy(a, b, sems.at[i]) for i, (a, b) in enumerate(pairs)]
    for copy in fetch:
        copy.start()
    piece, lane = iota((128, 512), 0), iota((128, 512), 1)
    use = jnp.where(lane < 128, jnp.where(piece == 0, 32.0, jnp.where(piece == 1, 1.0, 0.0)), 0.0)
    use = use + jnp.where((lane // 128 == 1) & (piece == 2), 1.0, 0.0)
    use = use + jnp.where((lane // 128 == 2) & (piece == 3), 1.0, 0.0)
    scores = (lane >= 384) & (piece >= 4) & (piece < 10)
    head = (lane - 384) // HD
    use = use + jnp.where(scores & ((piece - 4) // 3 == head), 1.0, 0.0)
    use = use.astype(BF)
    lanes = iota((rows, 128), 1).astype(F32)
    entry = iota((rows, PEERS * 16), 1)
    of_source = (entry // 16).astype(F32)
    of_head = entry % 16 // 3
    for copy in fetch:
        copy.wait()
    low = PEERS * LOW
    ctx_ref[:low, :] = msg_ref[:, :LOW, :].reshape(low, 128)
    for k in range(FULL):
        got = msg_ref[pl.ds(full_ref[k, 0], 1), LOW:CAP, :].reshape(REST, 128)
        ctx_ref[low + k * REST : low + (k + 1) * REST, :] = got
    parts = msg_ref[:, CAP:, :].reshape(PEERS * 16, 128)
    parity = lax.axis_index("x") % 2
    for i, out in enumerate(outs):
        block = (parity if i < 2 else 1 - parity) + 2 * (i % 2)
        at = pl.ds(pl.multiple_of(block * rows, rows), rows)
        known = jnp.dot(place_ref[at, :], use, preferred_element_type=F32)
        pos, own = known[:, :128], known[:, 384:]
        hot = [(lanes + float(t * 128) == pos).astype(F32).astype(BF) for t in range(8)]
        hot = jnp.concatenate(hot, axis=1)
        ctx = jnp.dot(hot, ctx_ref[...], preferred_element_type=F32)
        hit = of_source == jnp.concatenate([known[:, 256:384]] * 4, axis=1)
        here = lanes == known[:, 128:256]
        cols = []
        for h in range(2):
            pick = jnp.where(hit & (of_head == h), 1.0, 0.0).astype(BF)
            lists = jnp.dot(pick, parts, preferred_element_type=F32)
            cols.append(jnp.sum(jnp.where(here, lists, 0.0), axis=1, keepdims=True))
        lse = jnp.where(lanes < HD, cols[0], cols[1])
        top = jnp.maximum(lse, own)
        a = jnp.exp(lse - top)
        b = jnp.exp(own - top)
        out[...] = ((a * ctx + b * v_ref[at, :].astype(F32)) / (a + b)).astype(BF)


def project_kernel(a0, a1, a2, a3, own_ref, two_ref, left_ref, right_ref, out_ref, near, sems):
    copies = [
        pltpu.make_async_copy(r.at[pl.ds(512, 128)], near.at[pl.ds(n * 128, 128)], sems.at[n])
        for n, r in enumerate((left_ref, right_ref))
    ]
    for copy in copies:
        copy.start()
    rows = jnp.concatenate([a0[...], a3[...]], axis=1)
    weight = jnp.concatenate([own_ref[...], two_ref[...]], axis=0)
    total = jnp.dot(rows, weight, preferred_element_type=F32)
    rows = jnp.concatenate([a1[...], a2[...]], axis=1)
    for copy in copies:
        copy.wait()
    total = total + jnp.dot(rows, near[...], preferred_element_type=F32)
    out_ref[...] = total.astype(BF)


def ffn_kernel(
    x_ref, p_ref, r_ref, up_ref, down_ref, right_ref, left_ref, same_ref, other_ref, ups, downs,
    hid, acc, sems
):
    pairs = []
    for n, src in enumerate((right_ref, left_ref)):
        for k in range(4):
            block = pl.ds(k * 256, 256)
            pairs.append((src.at[pl.ds(0, 256), block], ups.at[block, pl.ds(n * 256, 256)]))
    for n, src in enumerate((right_ref, left_ref)):
        pairs.append((src.at[pl.ds(256, 256)], downs.at[pl.ds(n * 256, 256)]))
    copies = [pltpu.make_async_copy(a, b, sems.at[i]) for i, (a, b) in enumerate(pairs)]
    for copy in copies:
        copy.start()
    x = lax.axis_index("x")
    core = lax.axis_index("core")
    normed = []
    for n in range(2):
        at = pl.ds(n * 256, 256)
        attn = p_ref[at].astype(F32) + r_ref[at].astype(F32)
        rows = pl.ds(pl.multiple_of((x % 2 + 2 * n) * 256, 256), 256)
        hidden = (x_ref[rows, :].astype(F32) + attn).astype(BF).astype(F32)
        scale = lax.rsqrt(jnp.mean(hidden * hidden, axis=-1, keepdims=True) + 1e-05)
        normed.append((hidden * scale).astype(BF))
        hid[at] = jnp.where(x // 2 == n, hidden, 0.0)
    normed = jnp.concatenate(normed, axis=0)
    act = jax.nn.gelu(jnp.dot(normed, up_ref[...], preferred_element_type=F32)).astype(BF)
    total = jnp.dot(act, down_ref[...], preferred_element_type=F32)
    for copy in copies[:8]:
        copy.wait()
    act = jax.nn.gelu(jnp.dot(normed, ups[...], preferred_element_type=F32)).astype(BF)
    for copy in copies[8:]:
        copy.wait()
    acc[...] = total + jnp.dot(act, downs[...], preferred_element_type=F32)
    for d in range(4):
        head = ((x + d) % 4) * 2
        at = pl.ds(pl.multiple_of((head + core) * 128, 128), 128)
        same_ref[d] = hid[:, at] + acc[:, at]
        at = pl.ds(pl.multiple_of((head + 1 - core) * 128, 128), 128)
        other_ref[d] = acc[:, at].astype(BF)


def final_kernel(same_ref, other_ref, o0, o1, o2, o3):
    for i, out in enumerate((o0, o1, o2, o3)):
        out[...] = (same_ref[i] + other_ref[i].astype(F32)).astype(BF)


def place_rows_kernel(p0, p1, p2, p3, out_ref):
    mine = lax.axis_index("x") % 2
    for n in range(2):
        at = pl.ds(n * 256, 256)
        for parity, a, b in ((mine, p0, p2), (1 - mine, p1, p3)):
            to = pl.multiple_of((parity + 2 * n) * 256, 256)
            out_ref[pl.ds(to, 256), :] = (a[at].astype(F32) + b[at].astype(F32)).astype(BF)


def shift(x, axis, by, size):
    return lax.ppermute(x, axis, [(i, (i + by) % size) for i in range(size)])


def body(stream_in, keys, values, counts, slots, w_qkv, w_out, w_up, w_down):
    vmem = pl.BlockSpec(memory_space=pltpu.VMEM)
    hbm = pl.BlockSpec(memory_space=pltpu.HBM)
    send, par, my_full = call(
        plan_kernel,
        (
            pltpu.HBM((PEERS, 128), jnp.int32),
            pltpu.HBM((PEERS + FULL, 128), jnp.int32),
            pltpu.HBM((FULL, 128), jnp.int32),
        ),
        (4 * 10**8, 10**6),
    )(keep(counts.reshape(1, ROWS), pltpu.HBM), keep(slots.T, pltpu.HBM))
    recv = lax.all_to_all(
        send.reshape(PEERS, 1, 128), SAMPLE, split_axis=0, concat_axis=0, tiled=True
    ).reshape(PEERS, 128)

    query = call(
        project_query_kernel,
        sds((ROWS, 128), BF),
        (3 * 10**8, 3 * 10**6),
        in_specs=[vmem, vmem],
        out_specs=vmem,
    )(stream_in, w_qkv)
    for_right, for_left = call(
        pack_kernel,
        (pltpu.HBM((640, ROWS), BF), pltpu.HBM((640, ROWS), BF)),
        (0, 5 * 10**6),
        in_specs=[hbm] * 3,
        out_specs=(hbm, hbm),
        scratch_shapes=[pltpu.VMEM((2, 640, ROWS), BF), pltpu.SemaphoreType.DMA((18,))],
    )(*(keep(w, pltpu.HBM) for w in (w_up, w_down, w_out)))
    q_send = call(
        query_kernel,
        pltpu.HBM((ITEMS, 128), BF),
        (2 * ITEMS * ROWS * 128, 10**6),
        in_specs=[vmem, vmem, hbm],
        out_specs=hbm,
        scratch_shapes=[pltpu.VMEM((ITEMS, 128), BF), pltpu.SemaphoreType.DMA((4,))],
    )(recv, query, keep(for_left, pltpu.HBM))
    kv = call(
        expand_kernel,
        pltpu.HBM((ROWS, 2 * ROWS), BF),
        (2 * ROWS * ROWS * ROWS * 2, 12 * 10**6),
        in_specs=[hbm, hbm, hbm],
        out_specs=hbm,
        scratch_shapes=[
            pltpu.VMEM((2, ROWS, 8, 128), BF),
            pltpu.VMEM((2, ROWS, 8, 128), BF),
            pltpu.VMEM((2, 4, 256, ROWS), BF),
            pltpu.SMEM((PEERS + FULL, 128), jnp.int32),
            pltpu.SemaphoreType.DMA((11,)),
        ],
    )(*(keep(a, pltpu.HBM) for a in (par, keys, values)))
    left = shift(for_right, "x", 1, 4)
    right = shift(for_left, "x", 3, 4)
    wo_two = shift(w_out, "x", 2, 4)

    q_recv = lax.all_to_all(q_send, SAMPLE, split_axis=0, concat_axis=0, tiled=True)

    places, your_full, own_key, own_value = call(
        place_kernel,
        (
            pltpu.HBM((ROWS, 128), BF),
            pltpu.HBM((FULL, 128), jnp.int32),
            sds((ROWS, 128), BF),
            pltpu.HBM((ROWS, 128), BF),
        ),
        (2 * 10**9, 4 * 10**6),
    )(recv, stream_in, w_qkv, keep(query, pltpu.HBM))
    new_kv = jnp.stack([own_key, own_value], axis=1)

    msg = call(
        attend_kernel,
        pltpu.HBM((PEERS, MSG, 128), BF),
        (2 * ROWS * ROWS * 128, 8 * 10**6),
        in_specs=[hbm, vmem, hbm],
        out_specs=hbm,
        scratch_shapes=[
            pltpu.VMEM((4, 256, 2 * ROWS), BF),
            pltpu.VMEM((ROWS, 128), BF),
            pltpu.VMEM((PEERS, MSG, 128), BF),
            pltpu.SMEM((FULL, 128), jnp.int32),
            pltpu.SemaphoreType.DMA((10,)),
        ],
    )(keep(my_full, pltpu.HBM), q_recv.reshape(PEERS, CAP, 128), keep(kv, pltpu.HBM))
    answer = lax.all_to_all(msg, SAMPLE, split_axis=0, concat_axis=0, tiled=True)
    pair = sds((512, 128), BF)
    mine, theirs = call(
        merge_kernel,
        (pair, pair),
        (2 * ITEMS * ROWS * 128, 5 * 10**6),
        in_specs=[hbm] * 4,
        out_specs=(vmem, vmem),
        scratch_shapes=[
            pltpu.VMEM((PEERS, MSG, 128), BF),
            pltpu.VMEM((ROWS, 128), BF),
            pltpu.VMEM((ROWS, 128), BF),
            pltpu.VMEM((ROWS, 128), BF),
            pltpu.SMEM((FULL, 128), jnp.int32),
            pltpu.SemaphoreType.DMA((4,)),
        ],
    )(*(keep(a, pltpu.HBM) for a in (your_full, answer, places, own_value)))

    from_left = shift(theirs, "x", 1, 4)
    from_right = shift(theirs, "x", 3, 4)
    from_two = shift(mine, "x", 2, 4)
    partial = call(
        project_kernel,
        sds((512, ROWS), BF),
        (6 * 10**8, 3 * 10**6),
        in_specs=[vmem] * 6 + [hbm] * 2,
        out_specs=vmem,
        scratch_shapes=[pltpu.VMEM((256, ROWS), BF), pltpu.SemaphoreType.DMA((2,))],
    )(
        mine,
        from_left,
        from_right,
        from_two,
        keep(w_out),
        keep(wo_two),
        keep(left, pltpu.HBM),
        keep(right, pltpu.HBM),
    )
    partner = shift(partial, "core", 1, 2)

    same, other = call(
        ffn_kernel,
        (sds((4, 512, 128), F32), sds((4, 512, 128), BF)),
        (2 * 10**9, 10 * 10**6),
        in_specs=[vmem] * 5 + [hbm] * 2,
        out_specs=(vmem, vmem),
        scratch_shapes=[
            pltpu.VMEM((ROWS, 512), BF),
            pltpu.VMEM((512, ROWS), BF),
            pltpu.VMEM((512, ROWS), F32),
            pltpu.VMEM((512, ROWS), F32),
            pltpu.SemaphoreType.DMA((10,)),
        ],
    )(
        stream_in,
        partial,
        partner,
        keep(w_up),
        keep(w_down),
        keep(right, pltpu.HBM),
        keep(left, pltpu.HBM),
    )

    swapped = shift(other, "core", 1, 2)
    done = call(final_kernel, (pair,) * 4, (10**6, 10**6))(same, swapped)
    parts = [done[0]] + [shift(done[d], "x", d, 4) for d in (1, 2, 3)]
    layer_out = call(
        place_rows_kernel,
        sds((ROWS, 128), BF),
        (10**6, 5 * 10**5),
        in_specs=[vmem] * 4,
        out_specs=vmem,
    )(*parts)
    return (layer_out, new_kv)


def solution(mesh):
    grid = Mesh(mesh.devices.reshape(8, 4, 4, 2), ("z", "y", "x", "core"))
    in_specs = (
        P(SAMPLE, None),
        P(SAMPLE, None, HEAD),
        P(SAMPLE, None, HEAD),
        P(SAMPLE),
        P(SAMPLE, None),
        P(None, None, HEAD),
        P(HEAD, None),
        P(None, HEAD),
        P(HEAD, None),
    )
    out_specs = (P(SAMPLE, HEAD), P(SAMPLE, None, HEAD))
    return jax.shard_map(body, mesh=grid, in_specs=in_specs, out_specs=out_specs, check_vma=False)
```

```python
import functools

import jax
import jax.numpy as jnp
from jax import lax
from jax.experimental import pallas as pl
from jax.experimental.pallas import tpu as pltpu
from jax.sharding import Mesh, PartitionSpec as P

HD = 64
PEERS = 32
CAP = 48
ROWS = 1024
ITEMS = PEERS * CAP
MSG = 56
TAIL = MSG - CAP
LOW = 16
FULL = PEERS // 2
REST = CAP - LOW
SAMPLE = ("z", "y")
HEAD = ("x", "core")
F32 = jnp.float32
BF = jnp.bfloat16
NT = (((1,), (1,)), ((), ()))
TN = (((0,), (0,)), ((), ()))


def iota(shape, dim):
    return lax.broadcasted_iota(jnp.int32, shape, dim)


def call(kernel, out, cost, vmem=24, **kw):
    return pl.pallas_call(
        kernel,
        out_shape=out,
        compiler_params=pltpu.CompilerParams(vmem_limit_bytes=vmem * 2**20),
        cost_estimate=pl.CostEstimate(flops=cost[0], bytes_accessed=cost[1], transcendentals=0),
        **kw,
    )


def keep(x, space=pltpu.VMEM):
    return pltpu.with_memory_space_constraint(x, space)


def sds(shape, dtype):
    return jax.ShapeDtypeStruct(shape, dtype)


def full_peers(last):
    rows, cols = iota((PEERS, PEERS), 0), iota((PEERS, PEERS), 1)
    order = jnp.sum(jnp.where(rows < cols, last, 0.0), axis=0, keepdims=True)
    flag = jnp.sum(jnp.where(rows == cols, last, 0.0), axis=0, keepdims=True)
    hit = iota((FULL, PEERS), 0).astype(F32) == order
    return jnp.where(hit, flag, 0.0).astype(BF)


def peer_numbers(chosen):
    numbers = iota((PEERS, 128), 0).astype(F32).astype(BF)
    return jnp.dot(chosen, numbers, preferred_element_type=F32).astype(jnp.int32)


def plan_kernel(cnt_ref, slot_ref, send_ref, par_ref, full_ref):
    width = 256
    blocks = ROWS // width
    cnt = cnt_ref[...]
    tri = (iota((width, width), 0) <= iota((width, width), 1)).astype(F32).astype(BF)
    ow = iota((PEERS, width), 0)
    groups = []
    for k in range(4):
        for b in range(blocks):
            sl = slot_ref[k : k + 1, b * width : (b + 1) * width]
            live = cnt[:, b * width : (b + 1) * width] > k
            owner = jnp.where(live, sl // ROWS, -1)
            member = (ow == owner).astype(F32)
            groups.append((sl, live, member, b))
    stacked = jnp.concatenate([g[2].astype(BF) for g in groups], axis=0)
    inc = jnp.dot(stacked, tri, preferred_element_type=F32)
    base = jnp.zeros((PEERS, 1), F32)
    total = jnp.zeros((5 * PEERS, CAP), F32)
    parent = iota((1, width), 1)
    for g, (sl, live, member, b) in enumerate(groups):
        run = inc[g * PEERS : (g + 1) * PEERS]
        rank = jnp.sum(member * (run + (base - 1.0)), axis=0, keepdims=True)
        base = base + run[:, width - 1 : width]
        rank = jnp.where(live, rank.astype(jnp.int32), -1)
        place = (iota((CAP, width), 0) == rank).astype(F32).astype(BF)
        local = sl % ROWS
        par = parent + b * width
        left = jnp.concatenate(
            [
                member * (local // 32).astype(F32),
                member * (local % 32).astype(F32),
                member,
                member * (par // 32).astype(F32),
                member * (par % 32).astype(F32),
            ],
            axis=0,
        ).astype(BF)
        total = total + lax.dot_general(left, place, NT, preferred_element_type=F32)
    whole = total.astype(jnp.int32)
    have = whole[2 * PEERS : 3 * PEERS] > 0
    send = jnp.where(have, whole[:PEERS] * 32 + whole[PEERS : 2 * PEERS], -1)
    fill = jnp.full((PEERS, 128 - CAP), -1, jnp.int32)
    send_ref[...] = jnp.concatenate([send, fill], axis=1)
    chosen = full_peers(jnp.where(have[:, CAP - 1 :], 1.0, 0.0))
    full_ref[...] = peer_numbers(chosen)
    high, low = total[3 * PEERS : 4 * PEERS], total[4 * PEERS :]
    rest = 32.0 * jnp.dot(chosen, high.astype(BF), preferred_element_type=F32)
    rest = rest + jnp.dot(chosen, low.astype(BF), preferred_element_type=F32)
    first = (high[:, :LOW] * 32.0 + low[:, :LOW]).astype(jnp.int32)
    par_ref[:PEERS, :LOW] = first
    par_ref[:PEERS, LOW:] = jnp.zeros((PEERS, 128 - LOW), jnp.int32)
    par_ref[PEERS:, :REST] = rest[:, LOW:].astype(jnp.int32)
    par_ref[PEERS:, REST:] = jnp.zeros((FULL, 128 - REST), jnp.int32)


def pack_kernel(up_ref, down_ref, wo_ref, right_ref, left_ref, stage, sems):
    loads, stores = [], []
    for n, out in enumerate((right_ref, left_ref)):
        half = pl.ds(n * 256, 256)
        pairs = [(up_ref.at[pl.ds(k * 256, 256), half], pl.ds(k * 256, 256)) for k in range(4)]
        pairs = [(a, stage.at[n, pl.ds(0, 256), b]) for a, b in pairs]
        pairs.append((down_ref.at[half], stage.at[n, pl.ds(256, 256)]))
        pairs.append((wo_ref, stage.at[n, pl.ds(512, 128)]))
        loads.append(
            [pltpu.make_async_copy(a, b, sems.at[n * 9 + i]) for i, (a, b) in enumerate(pairs)]
        )
        parts = [pl.ds(0, 256), pl.ds(256, 256), pl.ds(512, 128)]
        stores.append(
            [
                pltpu.make_async_copy(stage.at[n, p], out.at[p], sems.at[n * 9 + 6 + i])
                for i, p in enumerate(parts)
            ]
        )
    for copy in loads[0] + loads[1]:
        copy.start()
    for n in range(2):
        for i in range(3):
            for copy in (loads[n][:4], loads[n][4:5], loads[n][5:])[i]:
                copy.wait()
            stores[n][i].start()
    for copy in stores[0] + stores[1]:
        copy.wait()


def column(lists, count, depth):
    shape = (count, depth, 128)
    picked = jnp.where(
        iota(shape, 1) == iota(shape, 2), jnp.broadcast_to(lists[:, None, :], shape), 0.0
    )
    return jnp.sum(picked, axis=2, keepdims=True).reshape(count * depth, 1)


def expand_kernel(par_hbm, k_hbm, v_hbm, out_ref, raw, got, stage, par, sems):
    n = 256
    lists = pltpu.make_async_copy(par_hbm, par, sems.at[10])
    lists.start()
    loads = [
        pltpu.make_async_copy(a, raw.at[t], sems.at[t]) for t, a in enumerate((k_hbm, v_hbm))
    ]
    for copy in loads:
        copy.start()
    lists.wait()
    copies = []
    for t in range(2):
        loads[t].wait()

        def first(o, carry):
            for c in range(LOW):
                got[t, o * LOW + c] = raw[t, par[o, c]]
            return carry

        def rest(k, carry):
            for c in range(REST):
                got[t, PEERS * LOW + k * REST + c] = raw[t, par[PEERS + k, c]]
            return carry

        lax.fori_loop(0, PEERS, first, 0)
        lax.fori_loop(0, FULL, rest, 0)
        for i in range(4):
            stage[t, i] = got[t, i * n : (i + 1) * n].reshape(n, ROWS)
            to = out_ref.at[pl.ds(i * n, n), pl.ds(t * ROWS, ROWS)]
            copy = pltpu.make_async_copy(stage.at[t, i], to, sems.at[2 + t * 4 + i])
            copy.start()
            copies.append(copy)
    for copy in copies:
        copy.wait()


def row_scales(x):
    x = x.astype(F32)
    return lax.rsqrt(jnp.mean(x * x, axis=-1, keepdims=True) + 1e-05)


def project_query_kernel(x_ref, w_ref, out_ref):
    for n in range(4):
        at = pl.ds(n * 256, 256)
        got = jnp.dot(x_ref[at], w_ref[0], preferred_element_type=F32)
        out_ref[at] = (got * row_scales(x_ref[at])).astype(BF)


def query_kernel(recv_ref, q_ref, after_ref, out_ref, stage, sems):
    lists = recv_ref[...].astype(F32)
    slots = iota((8 * CAP, ROWS), 1).astype(F32)
    copies = []
    for n in range(4):
        at = pl.ds(n * 8 * CAP, 8 * CAP)
        col = column(lists[n * 8 : n * 8 + 8], 8, CAP)
        hot = (col == slots).astype(F32).astype(BF)
        stage[at] = jnp.dot(hot, q_ref[...], preferred_element_type=F32).astype(BF)
        copy = pltpu.make_async_copy(stage.at[at], out_ref.at[at], sems.at[n])
        copy.start()
        copies.append(copy)
    for copy in copies:
        copy.wait()


def place_kernel(recv_ref, x_ref, w_ref, q_ref, out_ref, full_ref, own_k_ref, own_v_ref):
    for n in range(4):
        at = pl.ds(n * 256, 256)
        scale = row_scales(x_ref[at])
        for t, own_ref in ((1, own_k_ref), (2, own_v_ref)):
            got = jnp.dot(x_ref[at], w_ref[t], preferred_element_type=F32)
            own_ref[at] = (got * scale).astype(BF)
    slot = recv_ref[...]
    last = jnp.where(slot[:, CAP - 1 : CAP] >= 0, 1.0, 0.0)
    full_ref[...] = peer_numbers(full_peers(last))
    below = iota((PEERS, PEERS), 1) < iota((PEERS, PEERS), 0)
    order = jnp.dot(
        below.astype(F32).astype(BF),
        jnp.broadcast_to(last, (PEERS, 128)).astype(BF),
        preferred_element_type=F32,
    )
    high = jnp.where(slot >= 0, slot // 32, -1)
    low = slot % 32
    acc = jnp.zeros((96, 32), F32)
    where_c = iota((32, 128), 1).astype(F32)
    for s in range(PEERS):
        a = (iota((32, 128), 0) == high[s : s + 1, :]).astype(F32)
        b = (iota((32, 128), 0) == low[s : s + 1, :]).astype(F32).astype(BF)
        left = jnp.concatenate([a * float(s), a * where_c, a * order[s : s + 1]], axis=0)
        acc = acc + lax.dot_general(left.astype(BF), b, NT, preferred_element_type=F32)
    wide = jnp.concatenate([acc, jnp.zeros((96, 96), F32)], axis=1)
    src, place, rank = (column(wide[n * 32 : n * 32 + 32], 32, 32) for n in range(3))
    rest = float(PEERS * LOW - LOW) + rank * float(REST) + place
    pos = jnp.where(place < float(LOW), src * float(LOW) + place, rest)
    prod = q_ref[...].astype(F32) * own_k_ref[...].astype(F32) * (1.0 / HD**0.5)
    s0 = jnp.sum(prod[:, :HD], axis=1, keepdims=True)
    s1 = jnp.sum(prod[:, HD:], axis=1, keepdims=True)
    high = jnp.floor(pos * (1.0 / 32.0))
    pieces = [high, pos - high * 32.0, place, src]
    for value in (s0, s1):
        for _ in range(3):
            piece = value.astype(BF).astype(F32)
            pieces.append(piece)
            value = value - piece
    lane = iota((ROWS, 128), 1)
    known = jnp.zeros((ROWS, 128), F32)
    for n, piece in enumerate(pieces):
        known = jnp.where(lane == n, piece, known)
    out_ref[...] = known.astype(BF)


def attend_kernel(full_hbm, q_ref, kv_ref, out_ref, kv, rows_ref, stage, full_ref, sems):
    n = 256
    listing = pltpu.make_async_copy(full_hbm, full_ref, sems.at[9])
    listing.start()
    copies = []
    for part in range(2):
        for i in range(4):
            src = kv_ref.at[pl.ds(i * n, n), pl.ds(part * ROWS, ROWS)]
            dst = kv.at[i, :, pl.ds(part * ROWS, ROWS)]
            copies.append(pltpu.make_async_copy(src, dst, sems.at[part * 4 + i]))
    for copy in copies:
        copy.start()
    split = PEERS * LOW
    rows_ref[:split, :] = q_ref[:, :LOW, :].reshape(split, 128)
    listing.wait()
    peers = [pl.ds(full_ref[k, 0], 1) for k in range(FULL)]
    for k, peer in enumerate(peers):
        at = split + k * REST
        rows_ref[at : at + REST, :] = q_ref[peer, LOW:, :].reshape(REST, 128)
    sel_p = iota((16, ROWS), 1) // 128
    sel_h = (iota((16, ROWS), 1) % 128) // HD
    sel = (iota((16, ROWS), 0) == sel_h * 8 + sel_p).astype(F32).astype(BF)
    sum_p = iota((ROWS, 128), 0) // 128
    sum_h = (iota((ROWS, 128), 0) % 128) // HD
    sums = (iota((ROWS, 128), 1) == sum_h * 8 + sum_p).astype(F32).astype(BF)
    scores = []
    for i in range(4):
        q = rows_ref[i * n : (i + 1) * n, :].astype(F32)
        copies[i].wait()
        score = jnp.zeros((n, 128), F32)
        for p in range(0, 8, 2):
            highs, lows = [], []
            for t in (p, p + 1):
                prod = q * kv[i, :, t * 128 : (t + 1) * 128].astype(F32)
                high = prod.astype(BF)
                highs.append(high)
                lows.append((prod - high.astype(F32)).astype(BF))
            part = sums[p * 128 : (p + 2) * 128]
            highs, lows = jnp.concatenate(highs, axis=1), jnp.concatenate(lows, axis=1)
            score = score + jnp.dot(highs, part, preferred_element_type=F32)
            score = score + jnp.dot(lows, part, preferred_element_type=F32)
        scores.append(score.T[:16])
    score = jnp.concatenate(scores, axis=1) * (1.0 / HD**0.5)
    weights, parts = [], []
    for h in range(2):
        part = score[h * 8 : (h + 1) * 8]
        top = jnp.max(part, axis=0, keepdims=True)
        expo = jnp.exp(part - top)
        norm = jnp.sum(expo, axis=0, keepdims=True)
        weights.append(expo / norm)
        lse = top + jnp.log(norm)
        for _ in range(3):
            piece = lse.astype(BF).astype(F32)
            parts.append(piece)
            lse = lse - piece
    weight = jnp.concatenate(weights, axis=0).astype(BF)
    tail = jnp.concatenate(parts + [jnp.zeros((TAIL - 6, ROWS), F32)], axis=0)
    stage[:, LOW:CAP, :] = jnp.zeros((PEERS, REST, 128), BF)
    for k in range(PEERS):
        piece = tail[:, k * LOW : (k + 1) * LOW]
        piece = jnp.concatenate([piece, jnp.zeros((TAIL, 128 - LOW), F32)], axis=1)
        stage[k, CAP:, :] = piece.astype(BF)
    for i in range(4):
        wide = lax.dot_general(
            weight[:, i * n : (i + 1) * n], sel, TN, preferred_element_type=F32
        )
        copies[4 + i].wait()
        ctx = jnp.zeros((n, 128), F32)
        for p in range(8):
            value = kv[i, :, ROWS + p * 128 : ROWS + (p + 1) * 128].astype(F32)
            ctx = ctx + wide[:, p * 128 : (p + 1) * 128] * value
        ctx = ctx.astype(BF)
        if i < 2:
            stage[i * 16 : (i + 1) * 16, :LOW, :] = ctx.reshape(16, LOW, 128)
        else:
            for k in range(8):
                peer = peers[(i - 2) * 8 + k]
                stage[peer, LOW:CAP, :] = ctx[k * REST : (k + 1) * REST].reshape(1, REST, 128)
    for k, peer in enumerate(peers):
        at = split + k * REST
        before, after = jnp.zeros((TAIL, LOW), F32), jnp.zeros((TAIL, 128 - CAP), F32)
        piece = jnp.concatenate([before, tail[:, at : at + REST], after], axis=1).astype(BF)
        stage[peer, CAP:, :] = stage[peer, CAP:, :] + piece.reshape(1, TAIL, 128)
    end = pltpu.make_async_copy(stage, out_ref, sems.at[8])
    end.start()
    end.wait()


def merge_kernel(
    full_hbm, msg_hbm, place_hbm, v_hbm, mine_ref, theirs_ref, msg_ref, place_ref, v_ref, ctx_ref,
    full_ref, sems
):
    rows = 256
    outs = [r.at[pl.ds(n * rows, rows)] for r in (mine_ref, theirs_ref) for n in range(2)]
    pairs = [(full_hbm, full_ref), (msg_hbm, msg_ref), (place_hbm, place_ref), (v_hbm, v_ref)]
    fetch = [pltpu.make_async_copy(a, b, sems.at[i]) for i, (a, b) in enumerate(pairs)]
    for copy in fetch:
        copy.start()
    piece, lane = iota((128, 512), 0), iota((128, 512), 1)
    use = jnp.where(lane < 128, jnp.where(piece == 0, 32.0, jnp.where(piece == 1, 1.0, 0.0)), 0.0)
    use = use + jnp.where((lane // 128 == 1) & (piece == 2), 1.0, 0.0)
    use = use + jnp.where((lane // 128 == 2) & (piece == 3), 1.0, 0.0)
    scores = (lane >= 384) & (piece >= 4) & (piece < 10)
    head = (lane - 384) // HD
    use = use + jnp.where(scores & ((piece - 4) // 3 == head), 1.0, 0.0)
    use = use.astype(BF)
    lanes = iota((rows, 128), 1).astype(F32)
    entry = iota((rows, PEERS * TAIL), 1)
    of_source = (entry // TAIL).astype(F32)
    of_head = entry % TAIL // 3
    for copy in fetch:
        copy.wait()
    low = PEERS * LOW
    ctx_ref[:low, :] = msg_ref[:, :LOW, :].reshape(low, 128)
    for k in range(FULL):
        got = msg_ref[pl.ds(full_ref[k, 0], 1), LOW:CAP, :].reshape(REST, 128)
        ctx_ref[low + k * REST : low + (k + 1) * REST, :] = got
    parts = msg_ref[:, CAP:, :].reshape(PEERS * TAIL, 128)
    parity = lax.axis_index("x") % 2
    for i, out in enumerate(outs):
        block = (parity if i < 2 else 1 - parity) + 2 * (i % 2)
        at = pl.ds(pl.multiple_of(block * rows, rows), rows)
        known = jnp.dot(place_ref[at, :], use, preferred_element_type=F32)
        pos, own = known[:, :128], known[:, 384:]
        hot = [(lanes + float(t * 128) == pos).astype(F32).astype(BF) for t in range(8)]
        hot = jnp.concatenate(hot, axis=1)
        ctx = jnp.dot(hot, ctx_ref[...], preferred_element_type=F32)
        hit = of_source == jnp.concatenate([known[:, 256:384]] * (PEERS * TAIL // 128), axis=1)
        here = lanes == known[:, 128:256]
        cols = []
        for h in range(2):
            pick = jnp.where(hit & (of_head == h), 1.0, 0.0).astype(BF)
            lists = jnp.dot(pick, parts, preferred_element_type=F32)
            cols.append(jnp.sum(jnp.where(here, lists, 0.0), axis=1, keepdims=True))
        lse = jnp.where(lanes < HD, cols[0], cols[1])
        top = jnp.maximum(lse, own)
        a = jnp.exp(lse - top)
        b = jnp.exp(own - top)
        out[...] = ((a * ctx + b * v_ref[at, :].astype(F32)) / (a + b)).astype(BF)


def project_kernel(a0, a1, a2, a3, own_ref, two_ref, left_ref, right_ref, out_ref, near, sems):
    copies = [
        pltpu.make_async_copy(r.at[pl.ds(512, 128)], near.at[pl.ds(n * 128, 128)], sems.at[n])
        for n, r in enumerate((left_ref, right_ref))
    ]
    for copy in copies:
        copy.start()
    rows = jnp.concatenate([a0[...], a3[...]], axis=1)
    weight = jnp.concatenate([own_ref[...], two_ref[...]], axis=0)
    total = jnp.dot(rows, weight, preferred_element_type=F32)
    rows = jnp.concatenate([a1[...], a2[...]], axis=1)
    for copy in copies:
        copy.wait()
    total = total + jnp.dot(rows, near[...], preferred_element_type=F32)
    out_ref[...] = total.astype(BF)


def ffn_kernel(
    x_ref, p_ref, r_ref, up_ref, down_ref, right_ref, left_ref, same_ref, other_ref, ups, downs,
    hid, acc, sems
):
    pairs = []
    for n, src in enumerate((right_ref, left_ref)):
        for k in range(4):
            block = pl.ds(k * 256, 256)
            pairs.append((src.at[pl.ds(0, 256), block], ups.at[block, pl.ds(n * 256, 256)]))
    for n, src in enumerate((right_ref, left_ref)):
        pairs.append((src.at[pl.ds(256, 256)], downs.at[pl.ds(n * 256, 256)]))
    copies = [pltpu.make_async_copy(a, b, sems.at[i]) for i, (a, b) in enumerate(pairs)]
    for copy in copies:
        copy.start()
    x = lax.axis_index("x")
    core = lax.axis_index("core")
    normed = []
    for n in range(2):
        at = pl.ds(n * 256, 256)
        attn = p_ref[at].astype(F32) + r_ref[at].astype(F32)
        rows = pl.ds(pl.multiple_of((x % 2 + 2 * n) * 256, 256), 256)
        hidden = (x_ref[rows, :].astype(F32) + attn).astype(BF).astype(F32)
        scale = lax.rsqrt(jnp.mean(hidden * hidden, axis=-1, keepdims=True) + 1e-05)
        normed.append((hidden * scale).astype(BF))
        hid[at] = jnp.where(x // 2 == n, hidden, 0.0)
    normed = jnp.concatenate(normed, axis=0)
    act = jax.nn.gelu(jnp.dot(normed, up_ref[...], preferred_element_type=F32)).astype(BF)
    total = jnp.dot(act, down_ref[...], preferred_element_type=F32)
    for copy in copies[:8]:
        copy.wait()
    act = jax.nn.gelu(jnp.dot(normed, ups[...], preferred_element_type=F32)).astype(BF)
    for copy in copies[8:]:
        copy.wait()
    acc[...] = total + jnp.dot(act, downs[...], preferred_element_type=F32)
    for d in range(4):
        head = ((x + d) % 4) * 2
        at = pl.ds(pl.multiple_of((head + core) * 128, 128), 128)
        same_ref[d] = hid[:, at] + acc[:, at]
        at = pl.ds(pl.multiple_of((head + 1 - core) * 128, 128), 128)
        other_ref[d] = acc[:, at].astype(BF)


def final_kernel(same_ref, other_ref, o0, o1, o2, o3):
    for i, out in enumerate((o0, o1, o2, o3)):
        out[...] = (same_ref[i] + other_ref[i].astype(F32)).astype(BF)


def place_rows_kernel(p0, p1, p2, p3, out_ref):
    mine = lax.axis_index("x") % 2
    for n in range(2):
        at = pl.ds(n * 256, 256)
        for parity, a, b in ((mine, p0, p2), (1 - mine, p1, p3)):
            to = pl.multiple_of((parity + 2 * n) * 256, 256)
            out_ref[pl.ds(to, 256), :] = (a[at].astype(F32) + b[at].astype(F32)).astype(BF)


def shift(x, axis, by, size):
    return lax.ppermute(x, axis, [(i, (i + by) % size) for i in range(size)])


def body(stream_in, keys, values, counts, slots, w_qkv, w_out, w_up, w_down):
    vmem = pl.BlockSpec(memory_space=pltpu.VMEM)
    hbm = pl.BlockSpec(memory_space=pltpu.HBM)
    send, par, my_full = call(
        plan_kernel,
        (
            pltpu.HBM((PEERS, 128), jnp.int32),
            pltpu.HBM((PEERS + FULL, 128), jnp.int32),
            pltpu.HBM((FULL, 128), jnp.int32),
        ),
        (4 * 10**8, 10**6),
    )(keep(counts.reshape(1, ROWS), pltpu.HBM), keep(slots.T, pltpu.HBM))
    recv = lax.all_to_all(
        send.reshape(PEERS, 1, 128), SAMPLE, split_axis=0, concat_axis=0, tiled=True
    ).reshape(PEERS, 128)

    query = call(
        project_query_kernel,
        sds((ROWS, 128), BF),
        (3 * 10**8, 3 * 10**6),
        in_specs=[vmem, vmem],
        out_specs=vmem,
    )(stream_in, w_qkv)
    for_right, for_left = call(
        pack_kernel,
        (pltpu.HBM((640, ROWS), BF), pltpu.HBM((640, ROWS), BF)),
        (0, 5 * 10**6),
        in_specs=[hbm] * 3,
        out_specs=(hbm, hbm),
        scratch_shapes=[pltpu.VMEM((2, 640, ROWS), BF), pltpu.SemaphoreType.DMA((18,))],
    )(*(keep(w, pltpu.HBM) for w in (w_up, w_down, w_out)))
    q_send = call(
        query_kernel,
        pltpu.HBM((ITEMS, 128), BF),
        (2 * ITEMS * ROWS * 128, 10**6),
        in_specs=[vmem, vmem, hbm],
        out_specs=hbm,
        scratch_shapes=[pltpu.VMEM((ITEMS, 128), BF), pltpu.SemaphoreType.DMA((4,))],
    )(recv, query, keep(for_left, pltpu.HBM))
    kv = call(
        expand_kernel,
        pltpu.HBM((ROWS, 2 * ROWS), BF),
        (2 * ROWS * ROWS * ROWS * 2, 12 * 10**6),
        in_specs=[hbm, hbm, hbm],
        out_specs=hbm,
        scratch_shapes=[
            pltpu.VMEM((2, ROWS, 8, 128), BF),
            pltpu.VMEM((2, ROWS, 8, 128), BF),
            pltpu.VMEM((2, 4, 256, ROWS), BF),
            pltpu.SMEM((PEERS + FULL, 128), jnp.int32),
            pltpu.SemaphoreType.DMA((11,)),
        ],
    )(*(keep(a, pltpu.HBM) for a in (par, keys, values)))
    left = shift(for_right, "x", 1, 4)
    right = shift(for_left, "x", 3, 4)
    wo_two = shift(w_out, "x", 2, 4)

    q_recv = lax.all_to_all(q_send, SAMPLE, split_axis=0, concat_axis=0, tiled=True)

    places, your_full, own_key, own_value = call(
        place_kernel,
        (
            pltpu.HBM((ROWS, 128), BF),
            pltpu.HBM((FULL, 128), jnp.int32),
            sds((ROWS, 128), BF),
            pltpu.HBM((ROWS, 128), BF),
        ),
        (2 * 10**9, 4 * 10**6),
    )(recv, stream_in, w_qkv, keep(query, pltpu.HBM))
    new_kv = jnp.stack([own_key, own_value], axis=1)

    msg = call(
        attend_kernel,
        pltpu.HBM((PEERS, MSG, 128), BF),
        (2 * ROWS * ROWS * 128, 8 * 10**6),
        in_specs=[hbm, vmem, hbm],
        out_specs=hbm,
        scratch_shapes=[
            pltpu.VMEM((4, 256, 2 * ROWS), BF),
            pltpu.VMEM((ROWS, 128), BF),
            pltpu.VMEM((PEERS, MSG, 128), BF),
            pltpu.SMEM((FULL, 128), jnp.int32),
            pltpu.SemaphoreType.DMA((10,)),
        ],
    )(keep(my_full, pltpu.HBM), q_recv.reshape(PEERS, CAP, 128), keep(kv, pltpu.HBM))
    answer = lax.all_to_all(msg, SAMPLE, split_axis=0, concat_axis=0, tiled=True)
    pair = sds((512, 128), BF)
    mine, theirs = call(
        merge_kernel,
        (pair, pair),
        (2 * ITEMS * ROWS * 128, 5 * 10**6),
        in_specs=[hbm] * 4,
        out_specs=(vmem, vmem),
        scratch_shapes=[
            pltpu.VMEM((PEERS, MSG, 128), BF),
            pltpu.VMEM((ROWS, 128), BF),
            pltpu.VMEM((ROWS, 128), BF),
            pltpu.VMEM((ROWS, 128), BF),
            pltpu.SMEM((FULL, 128), jnp.int32),
            pltpu.SemaphoreType.DMA((4,)),
        ],
    )(*(keep(a, pltpu.HBM) for a in (your_full, answer, places, own_value)))

    from_left = shift(theirs, "x", 1, 4)
    from_right = shift(theirs, "x", 3, 4)
    from_two = shift(mine, "x", 2, 4)
    partial = call(
        project_kernel,
        sds((512, ROWS), BF),
        (6 * 10**8, 3 * 10**6),
        in_specs=[vmem] * 6 + [hbm] * 2,
        out_specs=vmem,
        scratch_shapes=[pltpu.VMEM((256, ROWS), BF), pltpu.SemaphoreType.DMA((2,))],
    )(
        mine,
        from_left,
        from_right,
        from_two,
        keep(w_out),
        keep(wo_two),
        keep(left, pltpu.HBM),
        keep(right, pltpu.HBM),
    )
    partner = shift(partial, "core", 1, 2)

    same, other = call(
        ffn_kernel,
        (sds((4, 512, 128), F32), sds((4, 512, 128), BF)),
        (2 * 10**9, 10 * 10**6),
        in_specs=[vmem] * 5 + [hbm] * 2,
        out_specs=(vmem, vmem),
        scratch_shapes=[
            pltpu.VMEM((ROWS, 512), BF),
            pltpu.VMEM((512, ROWS), BF),
            pltpu.VMEM((512, ROWS), F32),
            pltpu.VMEM((512, ROWS), F32),
            pltpu.SemaphoreType.DMA((10,)),
        ],
    )(
        stream_in,
        partial,
        partner,
        keep(w_up),
        keep(w_down),
        keep(right, pltpu.HBM),
        keep(left, pltpu.HBM),
    )

    swapped = shift(other, "core", 1, 2)
    done = call(final_kernel, (pair,) * 4, (10**6, 10**6))(same, swapped)
    parts = [done[0]] + [shift(done[d], "x", d, 4) for d in (1, 2, 3)]
    layer_out = call(
        place_rows_kernel,
        sds((ROWS, 128), BF),
        (10**6, 5 * 10**5),
        in_specs=[vmem] * 4,
        out_specs=vmem,
    )(*parts)
    return (layer_out, new_kv)


def solution(mesh):
    grid = Mesh(mesh.devices.reshape(8, 4, 4, 2), ("z", "y", "x", "core"))
    in_specs = (
        P(SAMPLE, None),
        P(SAMPLE, None, HEAD),
        P(SAMPLE, None, HEAD),
        P(SAMPLE),
        P(SAMPLE, None),
        P(None, None, HEAD),
        P(HEAD, None),
        P(None, HEAD),
        P(HEAD, None),
    )
    out_specs = (P(SAMPLE, HEAD), P(SAMPLE, None, HEAD))
    return jax.shard_map(body, mesh=grid, in_specs=in_specs, out_specs=out_specs, check_vma=False)
```

```python
import functools

import jax
import jax.numpy as jnp
from jax import lax
from jax.experimental import pallas as pl
from jax.experimental.pallas import tpu as pltpu
from jax.sharding import Mesh, PartitionSpec as P

HD = 64
PEERS = 32
CAP = 48
ROWS = 1024
ITEMS = PEERS * CAP
MSG = 56
TAIL = MSG - CAP
LOW = 16
FULL = PEERS // 2
REST = CAP - LOW
SAMPLE = ("z", "y")
HEAD = ("x", "core")
F32 = jnp.float32
BF = jnp.bfloat16
NT = (((1,), (1,)), ((), ()))
TN = (((0,), (0,)), ((), ()))


def iota(shape, dim):
    return lax.broadcasted_iota(jnp.int32, shape, dim)


def call(kernel, out, cost, vmem=24, **kw):
    return pl.pallas_call(
        kernel,
        out_shape=out,
        compiler_params=pltpu.CompilerParams(vmem_limit_bytes=vmem * 2**20),
        cost_estimate=pl.CostEstimate(flops=cost[0], bytes_accessed=cost[1], transcendentals=0),
        **kw,
    )


def keep(x, space=pltpu.VMEM):
    return pltpu.with_memory_space_constraint(x, space)


def sds(shape, dtype):
    return jax.ShapeDtypeStruct(shape, dtype)


def full_peers(last):
    rows, cols = iota((PEERS, PEERS), 0), iota((PEERS, PEERS), 1)
    order = jnp.sum(jnp.where(rows < cols, last, 0.0), axis=0, keepdims=True)
    flag = jnp.sum(jnp.where(rows == cols, last, 0.0), axis=0, keepdims=True)
    hit = iota((FULL, PEERS), 0).astype(F32) == order
    return jnp.where(hit, flag, 0.0).astype(BF)


def peer_numbers(chosen):
    numbers = iota((PEERS, 128), 0).astype(F32).astype(BF)
    return jnp.dot(chosen, numbers, preferred_element_type=F32).astype(jnp.int32)


def plan_kernel(cnt_ref, slot_ref, send_ref, par_ref, full_ref):
    width = 256
    blocks = ROWS // width
    cnt = cnt_ref[...]
    tri = (iota((width, width), 0) <= iota((width, width), 1)).astype(F32).astype(BF)
    ow = iota((PEERS, width), 0)
    groups = []
    for k in range(4):
        for b in range(blocks):
            sl = slot_ref[k : k + 1, b * width : (b + 1) * width]
            live = cnt[:, b * width : (b + 1) * width] > k
            owner = jnp.where(live, sl // ROWS, -1)
            member = (ow == owner).astype(F32)
            groups.append((sl, live, member, b))
    stacked = jnp.concatenate([g[2].astype(BF) for g in groups], axis=0)
    inc = jnp.dot(stacked, tri, preferred_element_type=F32)
    base = jnp.zeros((PEERS, 1), F32)
    total = jnp.zeros((5 * PEERS, CAP), F32)
    parent = iota((1, width), 1)
    for g, (sl, live, member, b) in enumerate(groups):
        run = inc[g * PEERS : (g + 1) * PEERS]
        rank = jnp.sum(member * (run + (base - 1.0)), axis=0, keepdims=True)
        base = base + run[:, width - 1 : width]
        rank = jnp.where(live, rank.astype(jnp.int32), -1)
        place = (iota((CAP, width), 0) == rank).astype(F32).astype(BF)
        local = sl % ROWS
        par = parent + b * width
        left = jnp.concatenate(
            [
                member * (local // 32).astype(F32),
                member * (local % 32).astype(F32),
                member,
                member * (par // 32).astype(F32),
                member * (par % 32).astype(F32),
            ],
            axis=0,
        ).astype(BF)
        total = total + lax.dot_general(left, place, NT, preferred_element_type=F32)
    whole = total.astype(jnp.int32)
    have = whole[2 * PEERS : 3 * PEERS] > 0
    send = jnp.where(have, whole[:PEERS] * 32 + whole[PEERS : 2 * PEERS], -1)
    fill = jnp.full((PEERS, 128 - CAP), -1, jnp.int32)
    send_ref[...] = jnp.concatenate([send, fill], axis=1)
    chosen = full_peers(jnp.where(have[:, CAP - 1 :], 1.0, 0.0))
    full_ref[...] = peer_numbers(chosen)
    high, low = total[3 * PEERS : 4 * PEERS], total[4 * PEERS :]
    rest = 32.0 * jnp.dot(chosen, high.astype(BF), preferred_element_type=F32)
    rest = rest + jnp.dot(chosen, low.astype(BF), preferred_element_type=F32)
    first = (high[:, :LOW] * 32.0 + low[:, :LOW]).astype(jnp.int32)
    par_ref[:PEERS, :LOW] = first
    par_ref[:PEERS, LOW:] = jnp.zeros((PEERS, 128 - LOW), jnp.int32)
    par_ref[PEERS:, :REST] = rest[:, LOW:].astype(jnp.int32)
    par_ref[PEERS:, REST:] = jnp.zeros((FULL, 128 - REST), jnp.int32)


def pack_kernel(up_ref, down_ref, wo_ref, right_ref, left_ref, stage, sems):
    loads, stores = [], []
    for n, out in enumerate((right_ref, left_ref)):
        half = pl.ds(n * 256, 256)
        pairs = [(up_ref.at[pl.ds(k * 256, 256), half], pl.ds(k * 256, 256)) for k in range(4)]
        pairs = [(a, stage.at[n, pl.ds(0, 256), b]) for a, b in pairs]
        pairs.append((down_ref.at[half], stage.at[n, pl.ds(256, 256)]))
        pairs.append((wo_ref, stage.at[n, pl.ds(512, 128)]))
        loads.append(
            [pltpu.make_async_copy(a, b, sems.at[n * 9 + i]) for i, (a, b) in enumerate(pairs)]
        )
        parts = [pl.ds(0, 256), pl.ds(256, 256), pl.ds(512, 128)]
        stores.append(
            [
                pltpu.make_async_copy(stage.at[n, p], out.at[p], sems.at[n * 9 + 6 + i])
                for i, p in enumerate(parts)
            ]
        )
    for copy in loads[0] + loads[1]:
        copy.start()
    for n in range(2):
        for i in range(3):
            for copy in (loads[n][:4], loads[n][4:5], loads[n][5:])[i]:
                copy.wait()
            stores[n][i].start()
    for copy in stores[0] + stores[1]:
        copy.wait()


def column(lists, count, depth):
    shape = (count, depth, 128)
    picked = jnp.where(
        iota(shape, 1) == iota(shape, 2), jnp.broadcast_to(lists[:, None, :], shape), 0.0
    )
    return jnp.sum(picked, axis=2, keepdims=True).reshape(count * depth, 1)


def expand_kernel(par_hbm, k_hbm, v_hbm, out_ref, raw, got, stage, par, sems):
    n = 256
    lists = pltpu.make_async_copy(par_hbm, par, sems.at[10])
    lists.start()
    loads = [
        pltpu.make_async_copy(a, raw.at[t], sems.at[t]) for t, a in enumerate((k_hbm, v_hbm))
    ]
    for copy in loads:
        copy.start()
    lists.wait()
    copies = []
    for t in range(2):
        loads[t].wait()

        def first(o, carry):
            for c in range(LOW):
                got[t, o * LOW + c] = raw[t, par[o, c]]
            return carry

        def rest(k, carry):
            for c in range(REST):
                got[t, PEERS * LOW + k * REST + c] = raw[t, par[PEERS + k, c]]
            return carry

        lax.fori_loop(0, PEERS, first, 0)
        lax.fori_loop(0, FULL, rest, 0)
        for i in range(4):
            stage[t, i] = got[t, i * n : (i + 1) * n].reshape(n, ROWS)
            to = out_ref.at[t, pl.ds(i * n, n)]
            copy = pltpu.make_async_copy(stage.at[t, i], to, sems.at[2 + t * 4 + i])
            copy.start()
            copies.append(copy)
    for copy in copies:
        copy.wait()


def row_scales(x):
    x = x.astype(F32)
    return lax.rsqrt(jnp.mean(x * x, axis=-1, keepdims=True) + 1e-05)


def project_query_kernel(x_ref, w_ref, out_ref):
    for n in range(4):
        at = pl.ds(n * 256, 256)
        got = jnp.dot(x_ref[at], w_ref[0], preferred_element_type=F32)
        out_ref[at] = (got * row_scales(x_ref[at])).astype(BF)


def query_kernel(recv_ref, q_ref, after_ref, out_ref, stage, sems):
    lists = recv_ref[...].astype(F32)
    slots = iota((8 * CAP, ROWS), 1).astype(F32)
    copies = []
    for n in range(4):
        at = pl.ds(n * 8 * CAP, 8 * CAP)
        col = column(lists[n * 8 : n * 8 + 8], 8, CAP)
        hot = (col == slots).astype(F32).astype(BF)
        stage[at] = jnp.dot(hot, q_ref[...], preferred_element_type=F32).astype(BF)
        copy = pltpu.make_async_copy(stage.at[at], out_ref.at[at], sems.at[n])
        copy.start()
        copies.append(copy)
    for copy in copies:
        copy.wait()


def place_kernel(recv_ref, x_ref, w_ref, q_ref, out_ref, full_ref, own_k_ref, own_v_ref):
    for n in range(4):
        at = pl.ds(n * 256, 256)
        scale = row_scales(x_ref[at])
        for t, own_ref in ((1, own_k_ref), (2, own_v_ref)):
            got = jnp.dot(x_ref[at], w_ref[t], preferred_element_type=F32)
            own_ref[at] = (got * scale).astype(BF)
    slot = recv_ref[...]
    last = jnp.where(slot[:, CAP - 1 : CAP] >= 0, 1.0, 0.0)
    full_ref[...] = peer_numbers(full_peers(last))
    below = iota((PEERS, PEERS), 1) < iota((PEERS, PEERS), 0)
    order = jnp.dot(
        below.astype(F32).astype(BF),
        jnp.broadcast_to(last, (PEERS, 128)).astype(BF),
        preferred_element_type=F32,
    )
    high = jnp.where(slot >= 0, slot // 32, -1)
    low = slot % 32
    acc = jnp.zeros((96, 32), F32)
    where_c = iota((32, 128), 1).astype(F32)
    for s in range(PEERS):
        a = (iota((32, 128), 0) == high[s : s + 1, :]).astype(F32)
        b = (iota((32, 128), 0) == low[s : s + 1, :]).astype(F32).astype(BF)
        left = jnp.concatenate([a * float(s), a * where_c, a * order[s : s + 1]], axis=0)
        acc = acc + lax.dot_general(left.astype(BF), b, NT, preferred_element_type=F32)
    wide = jnp.concatenate([acc, jnp.zeros((96, 96), F32)], axis=1)
    src, place, rank = (column(wide[n * 32 : n * 32 + 32], 32, 32) for n in range(3))
    rest = float(PEERS * LOW - LOW) + rank * float(REST) + place
    pos = jnp.where(place < float(LOW), src * float(LOW) + place, rest)
    prod = q_ref[...].astype(F32) * own_k_ref[...].astype(F32) * (1.0 / HD**0.5)
    s0 = jnp.sum(prod[:, :HD], axis=1, keepdims=True)
    s1 = jnp.sum(prod[:, HD:], axis=1, keepdims=True)
    high = jnp.floor(pos * (1.0 / 32.0))
    pieces = [high, pos - high * 32.0, place, src]
    for value in (s0, s1):
        for _ in range(3):
            piece = value.astype(BF).astype(F32)
            pieces.append(piece)
            value = value - piece
    lane = iota((ROWS, 128), 1)
    known = jnp.zeros((ROWS, 128), F32)
    for n, piece in enumerate(pieces):
        known = jnp.where(lane == n, piece, known)
    out_ref[...] = known.astype(BF)


def attend_kernel(full_hbm, q_ref, kv_ref, out_ref, kv, rows_ref, stage, full_ref, sems):
    n = 256
    listing = pltpu.make_async_copy(full_hbm, full_ref, sems.at[9])
    listing.start()
    copies = []
    for part in range(2):
        for i in range(4):
            src, dst = kv_ref.at[part, pl.ds(i * n, n)], kv.at[part, i]
            copies.append(pltpu.make_async_copy(src, dst, sems.at[part * 4 + i]))
    for copy in copies:
        copy.start()
    split = PEERS * LOW
    rows_ref[:split, :] = q_ref[:, :LOW, :].reshape(split, 128)
    listing.wait()
    peers = [pl.ds(full_ref[k, 0], 1) for k in range(FULL)]
    for k, peer in enumerate(peers):
        at = split + k * REST
        rows_ref[at : at + REST, :] = q_ref[peer, LOW:, :].reshape(REST, 128)
    sel_p = iota((16, ROWS), 1) // 128
    sel_h = (iota((16, ROWS), 1) % 128) // HD
    sel = (iota((16, ROWS), 0) == sel_h * 8 + sel_p).astype(F32).astype(BF)
    sum_p = iota((ROWS, 128), 0) // 128
    sum_h = (iota((ROWS, 128), 0) % 128) // HD
    sums = (iota((ROWS, 128), 1) == sum_h * 8 + sum_p).astype(F32).astype(BF)
    scores = []
    for i in range(4):
        q = rows_ref[i * n : (i + 1) * n, :].astype(F32)
        copies[i].wait()
        score = jnp.zeros((n, 128), F32)
        for p in range(0, 8, 2):
            highs, lows = [], []
            for t in (p, p + 1):
                prod = q * kv[0, i, :, t * 128 : (t + 1) * 128].astype(F32)
                high = prod.astype(BF)
                highs.append(high)
                lows.append((prod - high.astype(F32)).astype(BF))
            part = sums[p * 128 : (p + 2) * 128]
            highs, lows = jnp.concatenate(highs, axis=1), jnp.concatenate(lows, axis=1)
            score = score + jnp.dot(highs, part, preferred_element_type=F32)
            score = score + jnp.dot(lows, part, preferred_element_type=F32)
        scores.append(score.T[:16])
    score = jnp.concatenate(scores, axis=1) * (1.0 / HD**0.5)
    weights, parts = [], []
    for h in range(2):
        part = score[h * 8 : (h + 1) * 8]
        top = jnp.max(part, axis=0, keepdims=True)
        expo = jnp.exp(part - top)
        norm = jnp.sum(expo, axis=0, keepdims=True)
        weights.append(expo / norm)
        lse = top + jnp.log(norm)
        for _ in range(3):
            piece = lse.astype(BF).astype(F32)
            parts.append(piece)
            lse = lse - piece
    weight = jnp.concatenate(weights, axis=0).astype(BF)
    tail = jnp.concatenate(parts + [jnp.zeros((TAIL - 6, ROWS), F32)], axis=0)
    stage[:, LOW:CAP, :] = jnp.zeros((PEERS, REST, 128), BF)
    for k in range(PEERS):
        piece = tail[:, k * LOW : (k + 1) * LOW]
        piece = jnp.concatenate([piece, jnp.zeros((TAIL, 128 - LOW), F32)], axis=1)
        stage[k, CAP:, :] = piece.astype(BF)
    for i in range(4):
        wide = lax.dot_general(
            weight[:, i * n : (i + 1) * n], sel, TN, preferred_element_type=F32
        )
        copies[4 + i].wait()
        ctx = jnp.zeros((n, 128), F32)
        for p in range(8):
            value = kv[1, i, :, p * 128 : (p + 1) * 128].astype(F32)
            ctx = ctx + wide[:, p * 128 : (p + 1) * 128] * value
        ctx = ctx.astype(BF)
        if i < 2:
            stage[i * 16 : (i + 1) * 16, :LOW, :] = ctx.reshape(16, LOW, 128)
        else:
            for k in range(8):
                peer = peers[(i - 2) * 8 + k]
                stage[peer, LOW:CAP, :] = ctx[k * REST : (k + 1) * REST].reshape(1, REST, 128)
    for k, peer in enumerate(peers):
        at = split + k * REST
        before, after = jnp.zeros((TAIL, LOW), F32), jnp.zeros((TAIL, 128 - CAP), F32)
        piece = jnp.concatenate([before, tail[:, at : at + REST], after], axis=1).astype(BF)
        stage[peer, CAP:, :] = stage[peer, CAP:, :] + piece.reshape(1, TAIL, 128)
    end = pltpu.make_async_copy(stage, out_ref, sems.at[8])
    end.start()
    end.wait()


def merge_kernel(
    full_hbm, msg_hbm, place_hbm, v_hbm, mine_ref, theirs_ref, msg_ref, place_ref, v_ref, ctx_ref,
    full_ref, sems
):
    rows = 512
    pairs = [(full_hbm, full_ref), (msg_hbm, msg_ref), (place_hbm, place_ref), (v_hbm, v_ref)]
    fetch = [pltpu.make_async_copy(a, b, sems.at[i]) for i, (a, b) in enumerate(pairs)]
    for copy in fetch:
        copy.start()
    piece, lane = iota((128, 512), 0), iota((128, 512), 1)
    use = jnp.where(lane < 128, jnp.where(piece == 0, 32.0, jnp.where(piece == 1, 1.0, 0.0)), 0.0)
    use = use + jnp.where((lane // 128 == 1) & (piece == 2), 1.0, 0.0)
    use = use + jnp.where((lane // 128 == 2) & (piece == 3), 1.0, 0.0)
    scores = (lane >= 384) & (piece >= 4) & (piece < 10)
    head = (lane - 384) // HD
    use = use + jnp.where(scores & ((piece - 4) // 3 == head), 1.0, 0.0)
    use = use.astype(BF)
    lanes = iota((rows, 128), 1).astype(F32)
    entry = iota((rows, PEERS * TAIL), 1)
    of_source = (entry // TAIL).astype(F32)
    of_head = entry % TAIL // 3
    for copy in fetch:
        copy.wait()
    low = PEERS * LOW
    ctx_ref[:low, :] = msg_ref[:, :LOW, :].reshape(low, 128)
    for k in range(FULL):
        got = msg_ref[pl.ds(full_ref[k, 0], 1), LOW:CAP, :].reshape(REST, 128)
        ctx_ref[low + k * REST : low + (k + 1) * REST, :] = got
    parts = msg_ref[:, CAP:, :].reshape(PEERS * TAIL, 128)
    parity = lax.axis_index("x") % 2
    for i, out in enumerate((mine_ref, theirs_ref)):
        first = parity if i == 0 else 1 - parity
        at = [pl.ds(pl.multiple_of((first + 2 * n) * 256, 256), 256) for n in range(2)]
        known = jnp.concatenate([place_ref[a, :] for a in at], axis=0)
        value = jnp.concatenate([v_ref[a, :] for a in at], axis=0).astype(F32)
        known = jnp.dot(known, use, preferred_element_type=F32)
        pos, own = known[:, :128], known[:, 384:]
        hot = [(lanes + float(t * 128) == pos).astype(F32).astype(BF) for t in range(8)]
        hot = jnp.concatenate(hot, axis=1)
        ctx = jnp.dot(hot, ctx_ref[...], preferred_element_type=F32)
        hit = of_source == jnp.concatenate([known[:, 256:384]] * (PEERS * TAIL // 128), axis=1)
        here = lanes == known[:, 128:256]
        cols = []
        for h in range(2):
            pick = jnp.where(hit & (of_head == h), 1.0, 0.0).astype(BF)
            lists = jnp.dot(pick, parts, preferred_element_type=F32)
            cols.append(jnp.sum(jnp.where(here, lists, 0.0), axis=1, keepdims=True))
        lse = jnp.where(lanes < HD, cols[0], cols[1])
        top = jnp.maximum(lse, own)
        a = jnp.exp(lse - top)
        b = jnp.exp(own - top)
        out[...] = ((a * ctx + b * value) / (a + b)).astype(BF)


def project_kernel(a0, a1, a2, a3, own_ref, two_ref, left_ref, right_ref, out_ref, near, sems):
    copies = [
        pltpu.make_async_copy(r.at[pl.ds(512, 128)], near.at[pl.ds(n * 128, 128)], sems.at[n])
        for n, r in enumerate((left_ref, right_ref))
    ]
    for copy in copies:
        copy.start()
    rows = jnp.concatenate([a0[...], a3[...]], axis=1)
    weight = jnp.concatenate([own_ref[...], two_ref[...]], axis=0)
    total = jnp.dot(rows, weight, preferred_element_type=F32)
    rows = jnp.concatenate([a1[...], a2[...]], axis=1)
    for copy in copies:
        copy.wait()
    total = total + jnp.dot(rows, near[...], preferred_element_type=F32)
    out_ref[...] = total.astype(BF)


def ffn_kernel(
    x_ref, p_ref, r_ref, up_ref, down_ref, right_ref, left_ref, same_ref, other_ref, ups, downs,
    hid, acc, sems
):
    pairs = []
    for n, src in enumerate((right_ref, left_ref)):
        for k in range(4):
            block = pl.ds(k * 256, 256)
            pairs.append((src.at[pl.ds(0, 256), block], ups.at[block, pl.ds(n * 256, 256)]))
    for n, src in enumerate((right_ref, left_ref)):
        pairs.append((src.at[pl.ds(256, 256)], downs.at[pl.ds(n * 256, 256)]))
    copies = [pltpu.make_async_copy(a, b, sems.at[i]) for i, (a, b) in enumerate(pairs)]
    for copy in copies:
        copy.start()
    x = lax.axis_index("x")
    core = lax.axis_index("core")
    normed = []
    for n in range(2):
        at = pl.ds(n * 256, 256)
        attn = p_ref[at].astype(F32) + r_ref[at].astype(F32)
        rows = pl.ds(pl.multiple_of((x % 2 + 2 * n) * 256, 256), 256)
        hidden = (x_ref[rows, :].astype(F32) + attn).astype(BF).astype(F32)
        scale = lax.rsqrt(jnp.mean(hidden * hidden, axis=-1, keepdims=True) + 1e-05)
        normed.append((hidden * scale).astype(BF))
        hid[at] = jnp.where(x // 2 == n, hidden, 0.0)
    normed = jnp.concatenate(normed, axis=0)
    act = jax.nn.gelu(jnp.dot(normed, up_ref[...], preferred_element_type=F32)).astype(BF)
    total = jnp.dot(act, down_ref[...], preferred_element_type=F32)
    for copy in copies[:8]:
        copy.wait()
    act = jax.nn.gelu(jnp.dot(normed, ups[...], preferred_element_type=F32)).astype(BF)
    for copy in copies[8:]:
        copy.wait()
    acc[...] = total + jnp.dot(act, downs[...], preferred_element_type=F32)
    for d in range(4):
        head = ((x + d) % 4) * 2
        at = pl.ds(pl.multiple_of((head + core) * 128, 128), 128)
        same_ref[d] = hid[:, at] + acc[:, at]
        at = pl.ds(pl.multiple_of((head + 1 - core) * 128, 128), 128)
        other_ref[d] = acc[:, at].astype(BF)


def final_kernel(same_ref, other_ref, o0, o1, o2, o3):
    for i, out in enumerate((o0, o1, o2, o3)):
        out[...] = (same_ref[i] + other_ref[i].astype(F32)).astype(BF)


def place_rows_kernel(p0, p1, p2, p3, out_ref):
    mine = lax.axis_index("x") % 2
    for n in range(2):
        at = pl.ds(n * 256, 256)
        for parity, a, b in ((mine, p0, p2), (1 - mine, p1, p3)):
            to = pl.multiple_of((parity + 2 * n) * 256, 256)
            out_ref[pl.ds(to, 256), :] = (a[at].astype(F32) + b[at].astype(F32)).astype(BF)


def shift(x, axis, by, size):
    return lax.ppermute(x, axis, [(i, (i + by) % size) for i in range(size)])


def body(stream_in, keys, values, counts, slots, w_qkv, w_out, w_up, w_down):
    vmem = pl.BlockSpec(memory_space=pltpu.VMEM)
    hbm = pl.BlockSpec(memory_space=pltpu.HBM)
    send, par, my_full = call(
        plan_kernel,
        (
            pltpu.HBM((PEERS, 128), jnp.int32),
            pltpu.HBM((PEERS + FULL, 128), jnp.int32),
            pltpu.HBM((FULL, 128), jnp.int32),
        ),
        (4 * 10**8, 10**6),
    )(keep(counts.reshape(1, ROWS), pltpu.HBM), keep(slots.T, pltpu.HBM))
    recv = lax.all_to_all(
        send.reshape(PEERS, 1, 128), SAMPLE, split_axis=0, concat_axis=0, tiled=True
    ).reshape(PEERS, 128)

    query = call(
        project_query_kernel,
        sds((ROWS, 128), BF),
        (3 * 10**8, 3 * 10**6),
        in_specs=[vmem, vmem],
        out_specs=vmem,
    )(stream_in, w_qkv)
    for_right, for_left = call(
        pack_kernel,
        (pltpu.HBM((640, ROWS), BF), pltpu.HBM((640, ROWS), BF)),
        (0, 5 * 10**6),
        in_specs=[hbm] * 3,
        out_specs=(hbm, hbm),
        scratch_shapes=[pltpu.VMEM((2, 640, ROWS), BF), pltpu.SemaphoreType.DMA((18,))],
    )(*(keep(w, pltpu.HBM) for w in (w_up, w_down, w_out)))
    q_send = call(
        query_kernel,
        pltpu.HBM((ITEMS, 128), BF),
        (2 * ITEMS * ROWS * 128, 10**6),
        in_specs=[vmem, vmem, hbm],
        out_specs=hbm,
        scratch_shapes=[pltpu.VMEM((ITEMS, 128), BF), pltpu.SemaphoreType.DMA((4,))],
    )(recv, query, keep(for_left, pltpu.HBM))
    kv = call(
        expand_kernel,
        pltpu.HBM((2, ROWS, ROWS), BF),
        (2 * ROWS * ROWS * ROWS * 2, 12 * 10**6),
        in_specs=[hbm, hbm, hbm],
        out_specs=hbm,
        scratch_shapes=[
            pltpu.VMEM((2, ROWS, 8, 128), BF),
            pltpu.VMEM((2, ROWS, 8, 128), BF),
            pltpu.VMEM((2, 4, 256, ROWS), BF),
            pltpu.SMEM((PEERS + FULL, 128), jnp.int32),
            pltpu.SemaphoreType.DMA((11,)),
        ],
    )(*(keep(a, pltpu.HBM) for a in (par, keys, values)))
    left = shift(for_right, "x", 1, 4)
    right = shift(for_left, "x", 3, 4)
    wo_two = shift(w_out, "x", 2, 4)

    q_recv = lax.all_to_all(q_send, SAMPLE, split_axis=0, concat_axis=0, tiled=True)

    places, your_full, own_key, own_value = call(
        place_kernel,
        (
            pltpu.HBM((ROWS, 128), BF),
            pltpu.HBM((FULL, 128), jnp.int32),
            sds((ROWS, 128), BF),
            pltpu.HBM((ROWS, 128), BF),
        ),
        (2 * 10**9, 4 * 10**6),
    )(recv, stream_in, w_qkv, keep(query, pltpu.HBM))
    new_kv = jnp.stack([own_key, own_value], axis=1)

    msg = call(
        attend_kernel,
        pltpu.HBM((PEERS, MSG, 128), BF),
        (2 * ROWS * ROWS * 128, 8 * 10**6),
        in_specs=[hbm, vmem, hbm],
        out_specs=hbm,
        scratch_shapes=[
            pltpu.VMEM((2, 4, 256, ROWS), BF),
            pltpu.VMEM((ROWS, 128), BF),
            pltpu.VMEM((PEERS, MSG, 128), BF),
            pltpu.SMEM((FULL, 128), jnp.int32),
            pltpu.SemaphoreType.DMA((10,)),
        ],
    )(keep(my_full, pltpu.HBM), q_recv.reshape(PEERS, CAP, 128), keep(kv, pltpu.HBM))
    answer = lax.all_to_all(msg, SAMPLE, split_axis=0, concat_axis=0, tiled=True)
    pair = sds((512, 128), BF)
    mine, theirs = call(
        merge_kernel,
        (pair, pair),
        (2 * ITEMS * ROWS * 128, 5 * 10**6),
        in_specs=[hbm] * 4,
        out_specs=(vmem, vmem),
        scratch_shapes=[
            pltpu.VMEM((PEERS, MSG, 128), BF),
            pltpu.VMEM((ROWS, 128), BF),
            pltpu.VMEM((ROWS, 128), BF),
            pltpu.VMEM((ROWS, 128), BF),
            pltpu.SMEM((FULL, 128), jnp.int32),
            pltpu.SemaphoreType.DMA((4,)),
        ],
    )(*(keep(a, pltpu.HBM) for a in (your_full, answer, places, own_value)))

    from_left = shift(theirs, "x", 1, 4)
    from_right = shift(theirs, "x", 3, 4)
    from_two = shift(mine, "x", 2, 4)
    partial = call(
        project_kernel,
        sds((512, ROWS), BF),
        (6 * 10**8, 3 * 10**6),
        in_specs=[vmem] * 6 + [hbm] * 2,
        out_specs=vmem,
        scratch_shapes=[pltpu.VMEM((256, ROWS), BF), pltpu.SemaphoreType.DMA((2,))],
    )(
        mine,
        from_left,
        from_right,
        from_two,
        keep(w_out),
        keep(wo_two),
        keep(left, pltpu.HBM),
        keep(right, pltpu.HBM),
    )
    partner = shift(partial, "core", 1, 2)

    same, other = call(
        ffn_kernel,
        (sds((4, 512, 128), F32), sds((4, 512, 128), BF)),
        (2 * 10**9, 10 * 10**6),
        in_specs=[vmem] * 5 + [hbm] * 2,
        out_specs=(vmem, vmem),
        scratch_shapes=[
            pltpu.VMEM((ROWS, 512), BF),
            pltpu.VMEM((512, ROWS), BF),
            pltpu.VMEM((512, ROWS), F32),
            pltpu.VMEM((512, ROWS), F32),
            pltpu.SemaphoreType.DMA((10,)),
        ],
    )(
        stream_in,
        partial,
        partner,
        keep(w_up),
        keep(w_down),
        keep(right, pltpu.HBM),
        keep(left, pltpu.HBM),
    )

    swapped = shift(other, "core", 1, 2)
    done = call(final_kernel, (pair,) * 4, (10**6, 10**6))(same, swapped)
    parts = [done[0]] + [shift(done[d], "x", d, 4) for d in (1, 2, 3)]
    layer_out = call(
        place_rows_kernel,
        sds((ROWS, 128), BF),
        (10**6, 5 * 10**5),
        in_specs=[vmem] * 4,
        out_specs=vmem,
    )(*parts)
    return (layer_out, new_kv)


def solution(mesh):
    grid = Mesh(mesh.devices.reshape(8, 4, 4, 2), ("z", "y", "x", "core"))
    in_specs = (
        P(SAMPLE, None),
        P(SAMPLE, None, HEAD),
        P(SAMPLE, None, HEAD),
        P(SAMPLE),
        P(SAMPLE, None),
        P(None, None, HEAD),
        P(HEAD, None),
        P(None, HEAD),
        P(HEAD, None),
    )
    out_specs = (P(SAMPLE, HEAD), P(SAMPLE, None, HEAD))
    return jax.shard_map(body, mesh=grid, in_specs=in_specs, out_specs=out_specs, check_vma=False)
```
